128 devices in a mesh: dp: 4 (over x), ctx: 16 (over y, z), pair: 2 (over core).
Axes of the slice: x: 4, y: 4, z: 4, core: 2. Of those that a mesh axis runs over, the one named last changes fastest.
Arguments:
- queries: bfloat16 [8, 2048, 8192], P(('dp', 'pair'), 'ctx'), may hold values from -20 to 20
- keys: bfloat16 [8, 2048, 512], P(('dp', 'pair'), 'ctx'), may hold values from -20 to 20
- values: bfloat16 [8, 2048, 512], P(('dp', 'pair'), 'ctx'), may hold values from -6 to 6
- residual: bfloat16 [8, 2048, 2048], P(('dp', 'pair'), 'ctx'), may hold values from -6 to 6
- doc_lengths: int32 [8, 8], P(('dp', 'pair')), may hold values from 1 to 1024, 2048 in all within a row
- expert_ids: int32 [8, 2048, 8], P(('dp', 'pair'), 'ctx'), may hold values from 0 to 63, all different within a row; in each aligned block of 128 rows (0 to 127, 128 to 255, ..., all dimensions but the last counted through in order) at most 24 rows name the same one
- route_weights: float32 [8, 2048, 8], P(('dp', 'pair'), 'ctx'), may hold values from 0.05 to 1
- out_weight: bfloat16 [8192, 2048], P('ctx', 'dp'), may hold values from -0.25 to 0.25
- norm_gain: float32 [2048], replicated, may hold values from 0.5 to 1.5
- expert_gate: bfloat16 [64, 2048, 768], P(('ctx', 'pair')), may hold values from -0.125 to 0.125
- expert_up: bfloat16 [64, 2048, 768], P(('ctx', 'pair')), may hold values from -0.125 to 0.125
- expert_down: bfloat16 [64, 768, 2048], P(('ctx', 'pair')), may hold values from -0.21875 to 0.21875
Outputs:
- layer_out: bfloat16 [8, 2048, 2048], P(('dp', 'pair'), 'ctx')
The draws below stay inside these ranges and needn't reach their ends.
Inputs may be any that keep to these rules, and one draw needn't show every extreme that they name: `doc_lengths`: each row holds 8 document lengths that sum to 2048; the longest is exactly 1024. `expert_ids`: the 8 experts of a token differ. Among the tokens of one device no expert is named more than 24 times, a bound that some block reaches.
All inputs are finite; a program needn't handle non-finite values.
Results may differ from the reference program's by a relative error of at most 0.02.
Values may be sent and summed in bfloat16 or wider, within the bound.
No kernel may reach another device: no remote copies, remote signals or barrier semaphores. Data moves between devices by JAX's collectives and lax.ppermute only.
A program may use at most 128 MiB of HBM per device.

```python
import math
import jax
import jax.numpy as jnp
import numpy as np
from jax import lax

D = 2048
HEADS = 64
KV_HEADS = 4
HDIM = 128
FFE = 768
TOPK = 8
DOCS = 8
TOK_DEV = 128
SEQ = 2048
NSEQ = 8
EXP = 64
CAP = 24
N_CTX = 16


def draw_queries(key, part):
    key = jax.random.fold_in(key, 11)
    drawn = jnp.clip(jax.random.normal(key, (NSEQ, SEQ, HEADS * HDIM), jnp.float32), -4.0, 4.0)
    return drawn.astype(jnp.bfloat16)


def draw_keys(key, part):
    key = jax.random.fold_in(key, 12)
    drawn = jnp.clip(jax.random.normal(key, (NSEQ, SEQ, KV_HEADS * HDIM), jnp.float32), -4.0, 4.0)
    return drawn.astype(jnp.bfloat16)


def block_levels(stream_key, shape, cuts, least, top_value):
    def one(dim, blocks):
        draws = jax.random.uniform(jax.random.fold_in(jax.random.fold_in(stream_key, 6), dim), (blocks,), jnp.float32, least / len(cuts), top_value / len(cuts))
        return jnp.repeat(jnp.exp(draws), shape[dim] // blocks).reshape((-1,) + (1,) * (len(shape) - dim - 1))

    factor_of = one(*cuts[0])
    for cut in cuts[1:]:
        factor_of = factor_of * one(*cut)
    return factor_of


def length_profile(amount, total, reach, slope):
    portions = [(1 << 20) // math.isqrt(rank ** slope) + 1 for rank in range(2, amount + 1)]
    surplus, holding = total - reach - (amount - 1), [1] * (amount - 1)
    while surplus > 0:
        movable = [i for i in range(amount - 1) if holding[i] < reach]
        mass, remaining = sum([portions[i] for i in movable]), surplus
        for i in movable:
            addition = min(reach - holding[i], max(1, remaining * portions[i] // mass), surplus)
            holding[i] = holding[i] + addition
            surplus = surplus - addition
    return np.array([reach] + holding)


def uneven(own_key, count, total, reach, slope):
    if count == 2:
        one = jax.random.randint(own_key, (), max(1, total - reach), min(reach, total - 1) + 1)
        return jnp.stack([one, total - one])
    sizes = jnp.asarray(length_profile(count, total, reach, slope), jnp.int32)
    pairs = (count - 1) // 2
    giver, sink = sizes[1:1 + 2 * pairs:2], sizes[2:2 + 2 * pairs:2]
    margin = jnp.minimum(giver - 1, reach - sink)
    passed = jax.random.randint(jax.random.fold_in(own_key, 1), (pairs,), 0, 1 << 20) % (margin + 1)
    sizes = sizes.at[1:1 + 2 * pairs:2].set(giver - passed).at[2:2 + 2 * pairs:2].set(sink + passed)
    return sizes[jax.random.permutation(jax.random.fold_in(own_key, 2), count)]


def assign_block(key, own, number, rows, count, top, bound, lean):
    sequence = jax.random.permutation(key, count)
    heavy_load, common = load_shares(count, rows * top, bound, lean, True), load_shares(count, rows * top, bound, lean, False)
    places = jnp.arange(count)

    def named(sizes, rotation):
        used = int((sizes > 0).sum())
        fixed = max(1, used // 4)
        passed = fixed + (places - fixed + rotation * (used - fixed)) % max(1, count - fixed)
        return jnp.zeros((count,), jnp.int32).at[sequence[jnp.where(places < fixed, places, passed)]].set(jnp.asarray(sizes, jnp.int32))

    sizes = jnp.where(number % 4 == 0, named(heavy_load, number // 4), named(common, number - number // 4 - 1))
    mixed = jax.random.permutation(jax.random.fold_in(own, 3), count)
    giver, receiver = mixed[0:count // 2 * 2:2], mixed[1:count // 2 * 2:2]
    slack = jnp.minimum(sizes[giver] - 1, bound - sizes[receiver]) // 2
    slack = jnp.where((giver == sequence[0]) | (receiver == sequence[0]) | (sizes[receiver] == 0), 0, jnp.maximum(slack, 0))
    passed = jax.random.randint(jax.random.fold_in(own, 4), (count // 2,), 0, 1 << 20) % (slack + 1)
    sizes = sizes.at[giver].add(-passed).at[receiver].add(passed)
    items = jnp.searchsorted(jnp.cumsum(sizes), jnp.arange(rows * top), side="right").astype(jnp.int32)
    listing = items.reshape(top, rows).T
    listing = listing[jax.random.permutation(jax.random.fold_in(own, 1), rows)]
    rotation = jax.random.randint(jax.random.fold_in(own, 2), (rows, 1), 0, top)
    return jnp.take_along_axis(listing, (jnp.arange(top)[None, :] + rotation) % top, axis=1)


def load_shares(number_of, total, most, lean, full):
    loads = [(1 << 20) // math.isqrt(rank ** lean) + 1 for rank in range(1, number_of + 1)]
    largest = most if full else min(most, max(-(-total // number_of), total * loads[0] // sum(loads)))
    least = 1 if total - largest >= number_of - 1 else 0
    given, rest = [largest] + [least] * (number_of - 1), total - largest - least * (number_of - 1)
    while rest > 0:
        free = [i for i in range(1, number_of) if given[i] < largest] or [i for i in range(1, number_of) if given[i] < most]
        mass, budget = sum([loads[i] for i in free]), rest
        for i in free:
            addition = min(most - given[i], max(1, budget * loads[i] // mass), rest)
            given[i] = given[i] + addition
            rest = rest - addition
    return np.array(given)


def scatter_about(own_key, dims, scale, reach, cuts=(), kind=jnp.bfloat16):
    values = scale * jax.random.normal(own_key, dims, jnp.float32)
    if cuts:
        values = values * block_levels(own_key, dims, cuts, -0.22, 0.18)
    return jnp.clip(values, -reach, reach).astype(kind)


def setup_inputs(seed: int = 0) -> dict:
    seeds = jax.random.split(jax.random.key(seed), 13)
    queries = draw_queries(jax.random.fold_in(seeds[12], 71), 0)
    keys = draw_keys(jax.random.fold_in(seeds[12], 71), 0)
    values = scatter_about(seeds[2], (NSEQ, SEQ, KV_HEADS * HDIM), 1.0, 6.0, ((0, 8), (1, 16)))
    residual = scatter_about(seeds[3], (NSEQ, SEQ, D), 1.0, 6.0, ((0, 8), (1, 16)))
    doc_lengths = jax.vmap(lambda own: uneven(own, DOCS, SEQ, SEQ // 2, 2))(jax.random.split(seeds[4], NSEQ)).reshape((NSEQ, DOCS)).astype(jnp.int32)
    expert_ids_keys = jax.random.split(jax.random.fold_in(seeds[5], 1), NSEQ * SEQ // TOK_DEV)
    expert_ids_turns = jax.random.permutation(jax.random.fold_in(seeds[5], 3), NSEQ * SEQ // TOK_DEV)
    expert_ids = jax.vmap(lambda own, number: assign_block(jax.random.fold_in(seeds[5], 2), own, number, TOK_DEV, EXP, TOPK, CAP, 2))(expert_ids_keys, expert_ids_turns).reshape((NSEQ, SEQ, TOPK))
    route_weights = jnp.clip(jnp.exp(math.log(1.0) - 2.9957323 * jax.random.uniform(seeds[6], (NSEQ, SEQ, TOPK), jnp.float32) ** block_levels(seeds[6], (NSEQ, SEQ, TOPK), ((0, 8), (1, 16)), -0.2, 0.2)), 0.05, 1.0)
    out_weight = scatter_about(seeds[7], (HEADS * HDIM, D), (HEADS * HDIM // 16) ** -0.5, 0.25, ((0, 16), (1, 4)))
    norm_gain = jnp.clip(1.0 + 0.1 * jax.random.normal(seeds[8], (D,), jnp.float32), 0.5, 1.5)
    expert_gate = scatter_about(seeds[9], (EXP, D, FFE), D ** -0.5, 0.125, ((0, 32),))
    expert_up = scatter_about(seeds[10], (EXP, D, FFE), D ** -0.5, 0.125, ((0, 32),))
    expert_down = scatter_about(seeds[11], (EXP, FFE, D), FFE ** -0.5, 0.21875, ((0, 32),))
    return {"queries": queries, "keys": keys, "values": values, "residual": residual, "doc_lengths": doc_lengths, "expert_ids": expert_ids, "route_weights": route_weights, "out_weight": out_weight, "norm_gain": norm_gain, "expert_gate": expert_gate, "expert_up": expert_up, "expert_down": expert_down}


NEGATIVE = -1e+30
EPSILON = 1e-06

def segment_ids(lengths, positions_count):
    ends = jnp.cumsum(lengths, dtype=jnp.int32)
    positions = jnp.arange(positions_count, dtype=jnp.int32)
    return lax.optimization_barrier(jnp.sum((positions[:, None] >= ends[None, :]).astype(jnp.int32), axis=1, dtype=jnp.int32))

def attend(queries, own_keys, own_values, documents, block_rows):
    length, head_count, depth = queries.shape
    scaling = 1.0 / math.sqrt(depth)
    positions = jnp.arange(length, dtype=jnp.int32)

    def one_block(block_index):
        first = block_index * block_rows
        query_rows = lax.dynamic_slice_in_dim(queries, first, block_rows, 0)
        scores = jnp.einsum('qhd,kd->hqk', query_rows.astype(jnp.float32), own_keys.astype(jnp.float32)) * scaling
        query_places = lax.dynamic_slice_in_dim(positions, first, block_rows, 0)
        query_docs = lax.dynamic_slice_in_dim(documents, first, block_rows, 0)
        allowed = (query_docs[:, None] == documents[None, :]) & (positions[None, :] <= query_places[:, None])
        scores = jnp.where(allowed[None], scores, NEGATIVE)
        highest = lax.optimization_barrier(jnp.max(scores, axis=-1, keepdims=True))
        weights = jnp.exp(scores - highest)
        shares = (weights / lax.optimization_barrier(jnp.sum(weights, axis=-1, keepdims=True))).astype(jnp.bfloat16)
        mixed = jnp.einsum('hqk,kd->qhd', shares.astype(jnp.float32), own_values.astype(jnp.float32))
        return mixed.astype(jnp.bfloat16)
    blocks = lax.map(one_block, jnp.arange(length // block_rows, dtype=jnp.int32))
    return blocks.reshape(length, head_count, depth)

def reference(queries, keys, values, residual, doc_lengths, expert_ids, route_weights, out_weight, norm_gain, expert_gate, expert_up, expert_down):
    sequences = queries.shape[0]
    heads_here = HEADS // N_CTX
    group_size = HEADS // KV_HEADS
    block_rows = min(512, SEQ)
    width = out_weight.shape[1]

    def sequence_mix(inputs):
        query_seq, key_seq, value_seq, lengths = inputs
        documents = segment_ids(lengths, SEQ)

        def add_group(running, index):
            columns = heads_here * HDIM
            query_part = lax.dynamic_slice_in_dim(query_seq, index * columns, columns, 1).reshape(SEQ, heads_here, HDIM)
            kv_head = index * heads_here // group_size
            own_keys = lax.dynamic_slice_in_dim(key_seq, kv_head * HDIM, HDIM, 1)
            own_values = lax.dynamic_slice_in_dim(value_seq, kv_head * HDIM, HDIM, 1)
            attended = attend(query_part, own_keys, own_values, documents, block_rows).reshape(SEQ, columns)
            weight_rows = lax.dynamic_slice_in_dim(out_weight, index * columns, columns, 0)
            term = jnp.dot(attended, weight_rows, preferred_element_type=jnp.float32).astype(jnp.bfloat16)
            term = lax.optimization_barrier(term).astype(jnp.float32)
            return (running + term, None)
        projected, _ = lax.scan(add_group, jnp.zeros((SEQ, width), jnp.float32), jnp.arange(N_CTX, dtype=jnp.int32))
        return projected
    projected = lax.map(sequence_mix, (queries, keys, values, doc_lengths))
    hidden = residual.astype(jnp.float32) + projected
    mean_square = lax.optimization_barrier(jnp.mean(hidden * hidden, axis=-1, keepdims=True))
    normed = (hidden * lax.rsqrt(mean_square + EPSILON) * norm_gain).astype(jnp.bfloat16)
    tokens_all = sequences * SEQ
    flat_normed = normed.reshape(tokens_all, width)
    padded = jnp.concatenate([flat_normed, jnp.zeros((1, width), jnp.bfloat16)], axis=0)
    flat_ids = expert_ids.reshape(-1)
    flat_weights = route_weights.reshape(-1)
    owners = jnp.arange(tokens_all * TOPK, dtype=jnp.int32) // TOPK
    most_rows = CAP * sequences * N_CTX

    def add_expert(running, expert):
        chosen = flat_ids == expert
        places = jnp.cumsum(chosen.astype(jnp.int32), dtype=jnp.int32) - 1
        slots = jnp.where(chosen, places, most_rows)
        picked = jnp.full((most_rows,), tokens_all, jnp.int32).at[slots].set(owners, mode='drop')
        slot_weight = jnp.zeros((most_rows,), jnp.float32).at[slots].set(flat_weights, mode='drop')
        batch = padded[picked]
        gate = jnp.dot(batch, expert_gate[expert], preferred_element_type=jnp.float32)
        upward = jnp.dot(batch, expert_up[expert], preferred_element_type=jnp.float32)
        active = (jax.nn.silu(gate) * upward).astype(jnp.bfloat16)
        result = jnp.dot(active, expert_down[expert], preferred_element_type=jnp.float32).astype(jnp.bfloat16)
        added = result.astype(jnp.float32) * slot_weight[:, None]
        return (running.at[picked].add(added, mode='drop'), None)
    mixture, _ = lax.scan(add_expert, jnp.zeros((tokens_all, width), jnp.float32), jnp.arange(EXP, dtype=jnp.int32))
    return (hidden + mixture.reshape(sequences, SEQ, width)).astype(jnp.bfloat16)
```

```python
import functools
import math

import jax
import jax.numpy as jnp
from jax import lax
from jax.experimental import pallas as pl
from jax.experimental.pallas import tpu as pltpu
from jax.sharding import PartitionSpec as P

RING = 4
TOKENS = 128
WIDTH = 2048
HDIM = 128
HEADS_HERE = 16
FFE = 768
SLOTS = 48
EPSILON = 1e-06
NEGATIVE = -1e30
OFFSETS = (0, -1, 1, 2)
SLOT_OF = (0, 2, 3, 1)
AXES = ("dp", "ctx", "pair")


def shift(value, axes, distance):
    pairs = []
    for x in range(RING):
        for y in range(RING):
            for z in range(RING):
                for core in range(2):
                    to = {"x": x, "y": y, "z": z}
                    to[axes[core]] = (to[axes[core]] + distance) % RING
                    pairs.append(
                        (
                            (x * 16 + y * 4 + z) * 2 + core,
                            (to["x"] * 16 + to["y"] * 4 + to["z"]) * 2 + core,
                        )
                    )
    return lax.ppermute(value, AXES, pairs)


def swap(value):
    return lax.ppermute(value, "pair", [(0, 1), (1, 0)])


def attend_kernel(scalars, q_ref, kv_ref, out_ref, top_ref, sum_ref, acc_ref):
    block = scalars[0]
    scale = math.log2(math.e) / math.sqrt(HDIM)
    places = block * TOKENS + lax.broadcasted_iota(jnp.int32, (1, TOKENS), 1)
    starts = jnp.zeros((1, TOKENS), jnp.int32)
    first = jnp.int32(0)
    for d in range(8):
        end = scalars[1 + d]
        starts = jnp.maximum(starts, jnp.where(places >= end, end, 0))
        first = jnp.maximum(first, jnp.where(block * TOKENS >= end, end, 0))
    top_ref[...] = jnp.full_like(top_ref, NEGATIVE)
    sum_ref[...] = jnp.zeros_like(sum_ref)
    acc_ref[...] = jnp.zeros_like(acc_ref)
    rows = lax.broadcasted_iota(jnp.int32, (TOKENS, TOKENS), 0)

    def step(chunk, carry):
        slot = scalars[9 + chunk]
        keys = kv_ref[slot, :, :HDIM]
        values = kv_ref[slot, :, HDIM:].T
        key_places = chunk * TOKENS + rows
        allowed = (key_places <= places) & (key_places >= starts)
        bias = jnp.where(allowed, 0.0, NEGATIVE).astype(jnp.float32)
        bias = jnp.concatenate([bias, bias], axis=1)
        for pair in range(HEADS_HERE // 2):
            h = 2 * pair * HDIM
            q = jnp.concatenate([q_ref[:, h : h + HDIM], q_ref[:, h + HDIM : h + 2 * HDIM]], axis=0)
            s = lax.dot_general(
                keys, q, (((1,), (1,)), ((), ())), preferred_element_type=jnp.float32
            )
            s = s * scale + bias
            old = top_ref[pair]
            top = jnp.maximum(old, jnp.max(s, axis=0, keepdims=True))
            weights = jnp.exp2(s - top)
            fade = jnp.exp2(old - top)
            top_ref[pair] = top
            sum_ref[pair] = sum_ref[pair] * fade + jnp.sum(weights, axis=0, keepdims=True)
            acc_ref[pair] = acc_ref[pair] * fade + jnp.dot(
                values, weights.astype(jnp.bfloat16), preferred_element_type=jnp.float32
            )
        return carry

    lax.fori_loop(first // TOKENS, block + 1, step, 0)
    for pair in range(HEADS_HERE // 2):
        h = 2 * pair * HDIM
        mixed = (acc_ref[pair] / sum_ref[pair]).T.astype(jnp.bfloat16)
        out_ref[:, h : h + HDIM] = mixed[:TOKENS]
        out_ref[:, h + HDIM : h + 2 * HDIM] = mixed[TOKENS:]


def attend(scalars, queries, kv):
    vmem = pl.BlockSpec(memory_space=pltpu.VMEM)
    return pl.pallas_call(
        attend_kernel,
        out_shape=jax.ShapeDtypeStruct((TOKENS, WIDTH), jnp.bfloat16),
        in_specs=[pl.BlockSpec(memory_space=pltpu.SMEM), vmem, vmem],
        out_specs=vmem,
        scratch_shapes=[
            pltpu.VMEM((8, 1, 256), jnp.float32),
            pltpu.VMEM((8, 1, 256), jnp.float32),
            pltpu.VMEM((8, HDIM, 256), jnp.float32),
        ],
        compiler_params=pltpu.CompilerParams(vmem_limit_bytes=16 * 2**20),
        cost_estimate=pl.CostEstimate(
            flops=4 * 2048 * 640 * 128, bytes_accessed=3 * 2**20, transcendentals=2048 * 640
        ),
        name="attend",
    )(scalars, queries, kv)


def project_kernel(scalars, att_ref, *refs):
    own, other, out_ref = refs[0:4], refs[4:8], refs[8]
    x, z, core = scalars[0], scalars[1], scalars[2]

    def run(stacks):
        for i in range(4):
            column = lax.rem(x + OFFSETS[i] + 4, 4)
            total = None
            for half in range(2):
                for j in range(4):
                    place = lax.rem(z + OFFSETS[j] + 4, 4) * 512 + half * 256
                    left = att_ref[:, pl.ds(pl.multiple_of(place, 256), 256)]
                    right = stacks[0][j][i] if half == 0 else stacks[1][i][j]
                    term = jnp.dot(left, right, preferred_element_type=jnp.float32)
                    total = term if total is None else total + term
            out_ref[:, pl.ds(pl.multiple_of(column * 512, 512), 512)] = total.astype(jnp.bfloat16)

    @pl.when(core == 0)
    def _():
        run((own, other))

    @pl.when(core == 1)
    def _():
        run((other, own))


def project(scalars, attended, own, other):
    vmem = pl.BlockSpec(memory_space=pltpu.VMEM)
    rows = attended.shape[0]
    return pl.pallas_call(
        project_kernel,
        out_shape=jax.ShapeDtypeStruct((rows, WIDTH), jnp.bfloat16),
        in_specs=[pl.BlockSpec(memory_space=pltpu.SMEM)] + [vmem] * 9,
        out_specs=vmem,
        compiler_params=pltpu.CompilerParams(vmem_limit_bytes=32 * 2**20),
        cost_estimate=pl.CostEstimate(
            flops=2 * rows * 2048 * 2048, bytes_accessed=10 * 2**20, transcendentals=0
        ),
        name="project",
    )(scalars, attended, *own, *other)


def experts_kernel(*refs):
    pieces = refs[0:8]
    pick_ref, put_ref, weight_ref = refs[8:11]
    hbm = refs[11:17]
    outs = refs[17:25]
    rows_ref, act_ref, gate_buf, up_buf, down_buf, sems = refs[25:31]
    buffers = (gate_buf, up_buf, down_buf)

    def copies(e):
        side, index, slot = e // 2, e % 2, e % 2
        return [
            pltpu.make_async_copy(
                hbm[3 * side + w].at[index], buffers[w].at[slot], sems.at[w, slot]
            )
            for w in range(3)
        ]

    for e in range(2):
        for c in copies(e):
            c.start()
    for p in range(8):
        for n in range(4):
            cols = pl.ds(n * 512, 512)
            picked = jnp.dot(
                pick_ref[p],
                pieces[p][:, :, cols].reshape(256, 512),
                preferred_element_type=jnp.float32,
            )
            rows_ref[p, :, :, cols] = picked.astype(jnp.bfloat16).reshape(4, SLOTS, 512)
    for e in range(4):
        slot = e % 2
        waits = copies(e)
        waits[0].wait()
        waits[1].wait()
        rows = rows_ref[:, e].reshape(8 * SLOTS, WIDTH)

        for n in range(3):
            cols = pl.ds(n * 256, 256)
            gate = jnp.dot(rows, gate_buf[slot, :, cols], preferred_element_type=jnp.float32)
            upward = jnp.dot(rows, up_buf[slot, :, cols], preferred_element_type=jnp.float32)
            act_ref[:, cols] = (gate / (1.0 + jnp.exp(-gate)) * upward).astype(jnp.bfloat16)
        waits[2].wait()
        active = act_ref[...]
        scale = weight_ref[e]
        for n in range(4):
            cols = pl.ds(n * 512, 512)
            result = jnp.dot(active, down_buf[slot, :, cols], preferred_element_type=jnp.float32)
            rows_ref[:, e, :, cols] = (result * scale).astype(jnp.bfloat16).reshape(8, SLOTS, 512)
        if e + 2 < 4:
            for c in copies(e + 2):
                c.start()
    for p in range(8):
        for n in range(4):
            cols = pl.ds(n * 512, 512)
            mixed = jnp.dot(
                put_ref[p],
                rows_ref[p, :, :, cols].reshape(4 * SLOTS, 512),
                preferred_element_type=jnp.float32,
            )
            outs[p][:, :, cols] = mixed.astype(jnp.bfloat16).reshape(2, TOKENS, 512)


def experts(pieces, pick, put, weight, mine, others):
    vmem = pl.BlockSpec(memory_space=pltpu.VMEM)
    hbm = pl.BlockSpec(memory_space=pl.ANY)
    return pl.pallas_call(
        experts_kernel,
        out_shape=[jax.ShapeDtypeStruct((2, TOKENS, WIDTH), jnp.bfloat16)] * 8,
        in_specs=[vmem] * 11 + [hbm] * 6,
        out_specs=[vmem] * 8,
        scratch_shapes=[
            pltpu.VMEM((8, 4, SLOTS, WIDTH), jnp.bfloat16),
            pltpu.VMEM((8 * SLOTS, FFE), jnp.bfloat16),
            pltpu.VMEM((2, WIDTH, FFE), jnp.bfloat16),
            pltpu.VMEM((2, WIDTH, FFE), jnp.bfloat16),
            pltpu.VMEM((2, FFE, WIDTH), jnp.bfloat16),
            pltpu.SemaphoreType.DMA((3, 2)),
        ],
        compiler_params=pltpu.CompilerParams(vmem_limit_bytes=56 * 2**20),
        cost_estimate=pl.CostEstimate(
            flops=6 * 1536 * 2048 * 768, bytes_accessed=52 * 2**20, transcendentals=1536 * 768
        ),
        name="experts",
    )(*pieces, pick, put, weight, *mine, *others)


def routing(meta, y, z, core):
    sec = jnp.arange(16, dtype=jnp.int32) // 4
    prim = jnp.arange(16, dtype=jnp.int32) % 4
    offsets = jnp.array(OFFSETS, jnp.int32)
    on_y = jnp.where(core == 0, offsets[prim], offsets[sec])
    on_z = jnp.where(core == 0, offsets[sec], offsets[prim])
    order = (y + on_y + 4) % 4 * 4 + (z + on_z + 4) % 4
    meta = meta[order].reshape(8, 2, 16, TOKENS)
    meta = meta.transpose(0, 2, 1, 3).reshape(8, 16, 2 * TOKENS)
    ids, route = meta[:, :8].astype(jnp.int32), meta[:, 8:]
    chip = (y * 4 + z) * 4
    wanted = chip + jnp.stack([core * 2, core * 2 + 1, 2 - core * 2, 3 - core * 2])
    same = ids[:, None] == wanted[None, :, None, None]
    chosen = jnp.any(same, axis=2)
    share = jnp.sum(jnp.where(same, route[:, None], 0.0), axis=2)
    places = jnp.arange(2 * TOKENS, dtype=jnp.int32)
    before = (places[:, None] < places[None, :]).astype(jnp.bfloat16)
    rank = jnp.einsum(
        "pet,tu->peu", chosen.astype(jnp.bfloat16), before, preferred_element_type=jnp.float32
    )
    slots = jnp.arange(SLOTS, dtype=jnp.float32)
    pick = chosen[:, :, None] & (rank[:, :, None] == slots[None, None, :, None])
    weight = jnp.sum(jnp.where(pick, share[:, :, None], 0.0), axis=3)
    weight = weight.transpose(1, 0, 2).reshape(4, 8 * SLOTS, 1)
    pick = pick.astype(jnp.bfloat16).reshape(8, 4 * SLOTS, 2 * TOKENS)
    return pick, pick.transpose(0, 2, 1), weight


def body(
    queries,
    keys,
    values,
    residual,
    doc_lengths,
    expert_ids,
    route_weights,
    out_weight,
    norm_gain,
    expert_gate,
    expert_up,
    expert_down,
):
    x, core = lax.axis_index("dp"), lax.axis_index("pair")
    y, z = lax.axis_index("ctx") // 4, lax.axis_index("ctx") % 4
    yy, zz = ("y", "y"), ("z", "z")
    queries, keys, values = queries[0], keys[0], values[0]

    def kv_of(head):
        return jnp.concatenate(
            [
                lax.dynamic_slice_in_dim(keys, head * HDIM, HDIM, 1),
                lax.dynamic_slice_in_dim(values, head * HDIM, HDIM, 1),
            ],
            axis=1,
        )

    column = jnp.stack(
        [kv_of(y)] + [shift(kv_of((y - o + 4) % 4), yy, -o) for o in OFFSETS[1:]]
    )
    kv = jnp.concatenate([column] + [shift(column, zz, -o) for o in OFFSETS[1:]])

    def queries_of(group):
        return lax.dynamic_slice_in_dim(queries, group * WIDTH, WIDTH, 1)

    blocks = [queries_of(y)] + [shift(queries_of((y - o + 4) % 4), yy, -o) for o in OFFSETS[1:]]

    part = lax.dynamic_slice_in_dim(out_weight, core * 256, 256, 0)
    inner = jnp.stack([part] + [shift(part, ("x", "z"), -o) for o in OFFSETS[1:]])
    own = [inner] + [shift(inner, ("z", "x"), -o) for o in OFFSETS[1:]]
    other = [swap(w) for w in own]

    weights = [expert_gate, expert_up, expert_down]
    swapped = []
    for w in weights:
        if swapped:
            w, _ = lax.optimization_barrier((w, swapped[-1]))
        swapped.append(swap(w))

    meta = jnp.concatenate([expert_ids[0].T.astype(jnp.float32), route_weights[0].T])
    meta = lax.all_gather(meta, "ctx", axis=0)
    pick, put, weight = routing(meta, y, z, core)

    ends = jnp.cumsum(doc_lengths[0], dtype=jnp.int32)
    places = jnp.arange(16, dtype=jnp.int32)
    slot_of = jnp.array(SLOT_OF, jnp.int32)
    table = slot_of[(places % 4 - z + 4) % 4] * 4 + slot_of[(places // 4 - y + 4) % 4]

    def attended(k):
        block = (y + OFFSETS[k] + 4) % 4 * 4 + z
        return attend(jnp.concatenate([block[None], ends, table]), blocks[k], kv)

    where = jnp.stack([x, z, core]).astype(jnp.int32)
    mixed = [attended(k) for k in range(4)]
    far = project(where, mixed[3], own, other)
    near = project(where, jnp.concatenate([mixed[1], mixed[2], mixed[0]]), own, other)
    terms = [
        near[2 * TOKENS :],
        shift(near[:TOKENS], yy, -1),
        shift(near[TOKENS : 2 * TOKENS], yy, 1),
        shift(far, yy, 2),
    ]
    hidden = residual[0].astype(jnp.float32) + sum(t.astype(jnp.float32) for t in terms)
    mean_square = jnp.mean(hidden * hidden, axis=-1, keepdims=True)
    normed = (hidden * lax.rsqrt(mean_square + EPSILON) * norm_gain).astype(jnp.bfloat16)

    prim, sec = ("y", "z"), ("z", "y")
    got = [normed] + [shift(normed, prim, -o) for o in OFFSETS[1:]]
    low, high = jnp.stack(got[:2]), jnp.stack(got[2:])
    low_up, high_down = shift(low, sec, 1), shift(high, sec, -1)
    high_up, low_down = shift(high, sec, 1), shift(low, sec, -1)
    low_far, high_far = shift(low_up, sec, 1), shift(high_down, sec, -1)
    pieces = [low, high, low_up, high_up, low_down, high_down, low_far, high_far]
    parts = experts(pieces, pick, put, weight, weights, swapped)

    f32 = jnp.float32
    low, high, low_up, high_up, low_down, high_down, low_far, high_far = parts
    low_far, high_far = shift(low_far, sec, 1), shift(high_far, sec, -1)
    low_back = shift(low_up, sec, -1)
    high_back = shift(high_down, sec, 1)
    low_sum = (low_down.astype(f32) + low_far.astype(f32)).astype(jnp.bfloat16)
    high_sum = (high_up.astype(f32) + high_far.astype(f32)).astype(jnp.bfloat16)
    low_other, high_other = shift(low_sum, sec, 1), shift(high_sum, sec, -1)
    low = (low.astype(f32) + low_back.astype(f32) + low_other.astype(f32)).astype(jnp.bfloat16)
    high = (high.astype(f32) + high_back.astype(f32) + high_other.astype(f32)).astype(jnp.bfloat16)
    total = hidden + low[0].astype(f32)
    for block, o in ((low[1], -1), (high[0], 1), (high[1], 2)):
        total = total + shift(block, prim, o).astype(f32)
    return total.astype(jnp.bfloat16)[None]


def solution(mesh):
    return jax.shard_map(
        body,
        mesh=mesh,
        in_specs=(
            P(("dp", "pair"), "ctx", None),
            P(("dp", "pair"), "ctx", None),
            P(("dp", "pair"), "ctx", None),
            P(("dp", "pair"), "ctx", None),
            P(("dp", "pair"), None),
            P(("dp", "pair"), "ctx", None),
            P(("dp", "pair"), "ctx", None),
            P("ctx", "dp"),
            P(),
            P(("ctx", "pair"), None, None),
            P(("ctx", "pair"), None, None),
            P(("ctx", "pair"), None, None),
        ),
        out_specs=P(("dp", "pair"), "ctx", None),
        check_vma=False,
    )
```

```python
import functools
import math

import jax
import jax.numpy as jnp
from jax import lax
from jax.experimental import pallas as pl
from jax.experimental.pallas import tpu as pltpu
from jax.sharding import PartitionSpec as P

RING = 4
TOKENS = 128
WIDTH = 2048
HDIM = 128
HEADS_HERE = 16
FFE = 768
SLOTS = 48
EPSILON = 1e-06
NEGATIVE = -1e30
OFFSETS = (0, -1, 1, 2)
AXES = ("dp", "ctx", "pair")


def shift(value, axes, distance):
    pairs = []
    for x in range(RING):
        for y in range(RING):
            for z in range(RING):
                for core in range(2):
                    to = {"x": x, "y": y, "z": z}
                    to[axes[core]] = (to[axes[core]] + distance) % RING
                    pairs.append(
                        (
                            (x * 16 + y * 4 + z) * 2 + core,
                            (to["x"] * 16 + to["y"] * 4 + to["z"]) * 2 + core,
                        )
                    )
    return lax.ppermute(value, AXES, pairs)


def swap(value):
    return lax.ppermute(value, "pair", [(0, 1), (1, 0)])


def attend_kernel(scalars, q_ref, kv_ref, out_ref, top_ref, sum_ref, acc_ref):
    block = scalars[0]
    scale = math.log2(math.e) / math.sqrt(HDIM)
    places = block * TOKENS + lax.broadcasted_iota(jnp.int32, (1, TOKENS), 1)
    starts = jnp.zeros((1, TOKENS), jnp.int32)
    first = jnp.int32(0)
    for d in range(8):
        end = scalars[1 + d]
        starts = jnp.maximum(starts, jnp.where(places >= end, end, 0))
        first = jnp.maximum(first, jnp.where(block * TOKENS >= end, end, 0))
    top_ref[...] = jnp.full_like(top_ref, NEGATIVE)
    sum_ref[...] = jnp.zeros_like(sum_ref)
    acc_ref[...] = jnp.zeros_like(acc_ref)
    rows = lax.broadcasted_iota(jnp.int32, (TOKENS, TOKENS), 0)

    def step(chunk, carry):
        slot = scalars[9 + chunk]
        keys = kv_ref[slot, :TOKENS, :HDIM]
        values = kv_ref[slot, :TOKENS, HDIM:].T
        key_places = chunk * TOKENS + rows
        allowed = (key_places <= places) & (key_places >= starts)
        bias = jnp.where(allowed, 0.0, NEGATIVE).astype(jnp.float32)
        bias = jnp.concatenate([bias, bias], axis=1)
        for pair in range(HEADS_HERE // 2):
            h = 2 * pair * HDIM
            q = jnp.concatenate([q_ref[:, h : h + HDIM], q_ref[:, h + HDIM : h + 2 * HDIM]], axis=0)
            s = lax.dot_general(
                keys, q, (((1,), (1,)), ((), ())), preferred_element_type=jnp.float32
            )
            s = s * scale + bias
            old = top_ref[pair]
            top = jnp.maximum(old, jnp.max(s, axis=0, keepdims=True))
            weights = jnp.exp2(s - top)
            fade = jnp.exp2(old - top)
            top_ref[pair] = top
            sum_ref[pair] = sum_ref[pair] * fade + jnp.sum(weights, axis=0, keepdims=True)
            acc_ref[pair] = acc_ref[pair] * fade + jnp.dot(
                values, weights.astype(jnp.bfloat16), preferred_element_type=jnp.float32
            )
        return carry

    lax.fori_loop(first // TOKENS, block + 1, step, 0)
    for pair in range(HEADS_HERE // 2):
        h = 2 * pair * HDIM
        mixed = (acc_ref[pair] / sum_ref[pair]).T.astype(jnp.bfloat16)
        out_ref[:, h : h + HDIM] = mixed[:TOKENS]
        out_ref[:, h + HDIM : h + 2 * HDIM] = mixed[TOKENS:]


def attend(scalars, queries, kv):
    vmem = pl.BlockSpec(memory_space=pltpu.VMEM)
    return pl.pallas_call(
        attend_kernel,
        out_shape=jax.ShapeDtypeStruct((TOKENS, WIDTH), jnp.bfloat16),
        in_specs=[pl.BlockSpec(memory_space=pltpu.SMEM), vmem, vmem],
        out_specs=vmem,
        scratch_shapes=[
            pltpu.VMEM((8, 1, 256), jnp.float32),
            pltpu.VMEM((8, 1, 256), jnp.float32),
            pltpu.VMEM((8, HDIM, 256), jnp.float32),
        ],
        compiler_params=pltpu.CompilerParams(vmem_limit_bytes=16 * 2**20),
        cost_estimate=pl.CostEstimate(
            flops=4 * 2**30, bytes_accessed=3 * 2**20, transcendentals=2048 * 640
        ),
        name="attend",
    )(scalars, queries, kv)


def project_kernel(count, scalars, *refs):
    att, own, other = refs[0:count], refs[count : count + 4], refs[count + 4 : count + 8]
    outs = refs[count + 8 :]
    x, z, core = scalars[0], scalars[1], scalars[2]

    def run(stacks):
        for i in range(4):
            column = lax.rem(x + OFFSETS[i] + 4, 4) * 512
            total = None
            for half in range(2):
                for j in range(4):
                    place = lax.rem(z + OFFSETS[j] + 4, 4) * 512 + half * 256
                    place = pl.ds(pl.multiple_of(place, 256), 256)
                    left = jnp.concatenate([a[:, place] for a in att], axis=0)
                    right = stacks[0][j][i] if half == 0 else stacks[1][i][j]
                    term = jnp.dot(left, right, preferred_element_type=jnp.float32)
                    total = term if total is None else total + term
            total = total.astype(jnp.bfloat16)
            for n in range(count):
                part = total[n * TOKENS : (n + 1) * TOKENS]
                outs[n][:, pl.ds(pl.multiple_of(column, 512), 512)] = part

    @pl.when(core == 0)
    def _():
        run((own, other))

    @pl.when(core == 1)
    def _():
        run((other, own))


def project(scalars, attended, own, other):
    vmem = pl.BlockSpec(memory_space=pltpu.VMEM)
    count = len(attended)
    return pl.pallas_call(
        functools.partial(project_kernel, count),
        out_shape=[jax.ShapeDtypeStruct((TOKENS, WIDTH), jnp.bfloat16)] * count,
        in_specs=[pl.BlockSpec(memory_space=pltpu.SMEM)] + [vmem] * (count + 8),
        out_specs=[vmem] * count,
        compiler_params=pltpu.CompilerParams(vmem_limit_bytes=32 * 2**20),
        cost_estimate=pl.CostEstimate(
            flops=2 * count * TOKENS * 2048 * 2048,
            bytes_accessed=(8 + count) * 2**20,
            transcendentals=0,
        ),
        name="project",
    )(scalars, *attended, *own, *other)


def experts_kernel(count, *refs):
    pieces = refs[0:count]
    pick_ref, put_ref, weight_ref = refs[count : count + 3]
    hbm = refs[count + 3 : count + 9]
    outs = refs[count + 9 : 2 * count + 9]
    rows_ref, act_ref, gate_buf, up_buf, down_buf, sems = refs[2 * count + 9 :]
    buffers = (gate_buf, up_buf, down_buf)

    def copies(e):
        side, index, slot = e // 2, e % 2, e % 2
        return [
            pltpu.make_async_copy(
                hbm[3 * side + w].at[index], buffers[w].at[slot], sems.at[w, slot]
            )
            for w in range(3)
        ]

    for e in range(2):
        for c in copies(e):
            c.start()
    for p in range(count):
        for n in range(4):
            cols = pl.ds(n * 512, 512)
            picked = jnp.dot(
                pick_ref[p],
                pieces[p][:, :, cols].reshape(256, 512),
                preferred_element_type=jnp.float32,
            )
            rows_ref[p, :, :, cols] = picked.astype(jnp.bfloat16).reshape(4, SLOTS, 512)
    for e in range(4):
        slot = e % 2
        waits = copies(e)
        waits[0].wait()
        waits[1].wait()
        rows = rows_ref[:, e].reshape(count * SLOTS, WIDTH)
        for n in range(3):
            cols = pl.ds(n * 256, 256)
            gate = jnp.dot(rows, gate_buf[slot, :, cols], preferred_element_type=jnp.float32)
            upward = jnp.dot(rows, up_buf[slot, :, cols], preferred_element_type=jnp.float32)
            act_ref[:, cols] = (gate / (1.0 + jnp.exp(-gate)) * upward).astype(jnp.bfloat16)
        waits[2].wait()
        active = act_ref[...]
        scale = weight_ref[e]
        for n in range(4):
            cols = pl.ds(n * 512, 512)
            result = jnp.dot(active, down_buf[slot, :, cols], preferred_element_type=jnp.float32)
            result = (result * scale).astype(jnp.bfloat16)
            rows_ref[:, e, :, cols] = result.reshape(count, SLOTS, 512)
        if e + 2 < 4:
            for c in copies(e + 2):
                c.start()
    for p in range(count):
        for n in range(4):
            cols = pl.ds(n * 512, 512)
            mixed = jnp.dot(
                put_ref[p],
                rows_ref[p, :, :, cols].reshape(4 * SLOTS, 512),
                preferred_element_type=jnp.float32,
            )
            outs[p][:, :, cols] = mixed.astype(jnp.bfloat16).reshape(2, TOKENS, 512)


def experts(pieces, first, pick, put, weight, mine, others):
    count = len(pieces)
    vmem = pl.BlockSpec(memory_space=pltpu.VMEM)
    hbm = pl.BlockSpec(memory_space=pl.ANY)
    rows = count * 4 * SLOTS
    return pl.pallas_call(
        functools.partial(experts_kernel, count),
        out_shape=[jax.ShapeDtypeStruct((2, TOKENS, WIDTH), jnp.bfloat16)] * count,
        in_specs=[vmem] * (count + 3) + [hbm] * 6,
        out_specs=[vmem] * count,
        scratch_shapes=[
            pltpu.VMEM((count, 4, SLOTS, WIDTH), jnp.bfloat16),
            pltpu.VMEM((count * SLOTS, FFE), jnp.bfloat16),
            pltpu.VMEM((2, WIDTH, FFE), jnp.bfloat16),
            pltpu.VMEM((2, WIDTH, FFE), jnp.bfloat16),
            pltpu.VMEM((2, FFE, WIDTH), jnp.bfloat16),
            pltpu.SemaphoreType.DMA((3, 2)),
        ],
        compiler_params=pltpu.CompilerParams(vmem_limit_bytes=(24 + 4 * count) * 2**20),
        cost_estimate=pl.CostEstimate(
            flops=6 * rows * 2048 * 768,
            bytes_accessed=(36 + 2 * count) * 2**20,
            transcendentals=rows * 768,
        ),
        name="experts",
    )(
        *pieces,
        pick[first : first + count],
        put[first : first + count],
        weight[:, first * SLOTS : (first + count) * SLOTS],
        *mine,
        *others,
    )


def routing(meta, y, z, core):
    meta = jnp.where(core == 0, meta, meta.transpose(1, 0, 2, 3)).astype(jnp.float32)
    meta = meta.reshape(8, 2, 32, TOKENS).transpose(0, 2, 1, 3).reshape(8, 32, 2 * TOKENS)
    ids = meta[:, :8]
    route = meta[:, 8:16] + meta[:, 16:24] + meta[:, 24:32]
    chip = (y * 4 + z) * 4
    wanted = chip + jnp.stack([core * 2, core * 2 + 1, 2 - core * 2, 3 - core * 2])
    same = ids[:, None] == wanted.astype(jnp.float32)[None, :, None, None]
    chosen = jnp.any(same, axis=2)
    share = jnp.sum(jnp.where(same, route[:, None], 0.0), axis=2)
    places = jnp.arange(2 * TOKENS, dtype=jnp.int32)
    before = (places[:, None] < places[None, :]).astype(jnp.bfloat16)
    rank = jnp.einsum(
        "pet,tu->peu", chosen.astype(jnp.bfloat16), before, preferred_element_type=jnp.float32
    )
    slots = jnp.arange(SLOTS, dtype=jnp.float32)
    pick = chosen[:, :, None] & (rank[:, :, None] == slots[None, None, :, None])
    weight = jnp.sum(jnp.where(pick, share[:, :, None], 0.0), axis=3)
    weight = weight.transpose(1, 0, 2).reshape(4, 8 * SLOTS, 1)
    pick = pick.astype(jnp.bfloat16).reshape(8, 4 * SLOTS, 2 * TOKENS)
    return pick, pick.transpose(0, 2, 1), weight


def after(value, *others):
    return lax.optimization_barrier((value, *others))[0]


def body(
    queries,
    keys,
    values,
    residual,
    doc_lengths,
    expert_ids,
    route_weights,
    out_weight,
    norm_gain,
    expert_gate,
    expert_up,
    expert_down,
):
    f32 = jnp.float32
    x, core = lax.axis_index("dp"), lax.axis_index("pair")
    y, z = lax.axis_index("ctx") // 4, lax.axis_index("ctx") % 4
    yy, zz = ("y", "y"), ("z", "z")
    queries, keys, values = queries[0], keys[0], values[0]

    route = route_weights[0].T
    high = lax.reduce_precision(route, 8, 7)
    middle = lax.reduce_precision(route - high, 8, 7)
    low = route - high - middle
    meta = jnp.concatenate([expert_ids[0].T.astype(f32), high, middle, low])
    meta = meta.astype(jnp.bfloat16)
    meta = jnp.concatenate([meta[:16], meta[16:]], axis=1)

    def kv_of(head):
        pair = jnp.concatenate(
            [
                lax.dynamic_slice_in_dim(keys, head * HDIM, HDIM, 1),
                lax.dynamic_slice_in_dim(values, head * HDIM, HDIM, 1),
            ],
            axis=1,
        )
        return jnp.concatenate([pair, meta])

    kv_y = [kv_of(y)] + [shift(kv_of((y - o + 4) % 4), yy, -o) for o in OFFSETS[1:]]
    column = jnp.stack(kv_y)
    kv = jnp.concatenate([column] + [shift(column, zz, -o) for o in OFFSETS[1:]])

    def queries_of(group):
        return lax.dynamic_slice_in_dim(queries, group * WIDTH, WIDTH, 1)

    part = lax.dynamic_slice_in_dim(out_weight, core * 256, 256, 0)
    inner = jnp.stack([part] + [shift(part, ("x", "z"), -o) for o in OFFSETS[1:]])
    blocks = [queries_of(y), None, None, shift(queries_of((y + 2) % 4), yy, -2)]
    for k in (1, 2):
        o = OFFSETS[k]
        near = after(queries_of((y - o + 4) % 4), blocks[3], inner, column)
        blocks[k] = shift(near, yy, -o)

    inner = after(inner, kv)
    own = [inner] + [shift(inner, ("z", "x"), -o) for o in OFFSETS[1:]]
    meta = kv[:, TOKENS:]
    meta = jnp.concatenate([meta[:, :, :TOKENS], meta[:, :, TOKENS:]], axis=1)
    pick, put, weight = routing(meta.reshape(4, 4, 32, TOKENS), y, z, core)

    lengths = doc_lengths[0]
    ends = jnp.stack([jnp.sum(lengths[: d + 1]) for d in range(8)])
    places = jnp.arange(16, dtype=jnp.int32)

    def slot_of(distance):
        return jnp.where(distance == 3, 1, jnp.where(distance == 0, 0, distance + 1))

    table = slot_of((places % 4 - z + 4) % 4) * 4 + slot_of((places // 4 - y + 4) % 4)

    def attended(k):
        block = (y + OFFSETS[k] + 4) % 4 * 4 + z
        return attend(jnp.concatenate([block[None], ends, table]), blocks[k], kv)

    where = jnp.stack([x, z, core]).astype(jnp.int32)
    last = blocks[2]
    blocks[2] = after(last, *own)
    mixed = [attended(k) for k in range(4)]
    other = [swap(after(w, mixed[0], mixed[3], mixed[1], last)) for w in own]

    (far,) = project(where, [after(mixed[3], mixed[2])], own, other)
    near = [after(mixed[1], far), mixed[2], mixed[0]]
    below, above, here = project(where, near, own, other)

    weights = [expert_gate, expert_up, expert_down]
    swapped = [swap(after(expert_gate, far)), swap(after(expert_up, far))]

    terms = [here, shift(below, yy, -1), shift(above, yy, 1), shift(far, yy, 2)]
    hidden = residual[0].astype(f32) + sum(t.astype(f32) for t in terms)
    mean_square = jnp.mean(hidden * hidden, axis=-1, keepdims=True)
    normed = (hidden * lax.rsqrt(mean_square + EPSILON) * norm_gain).astype(jnp.bfloat16)
    normed = after(normed, *swapped)
    swapped.append(swap(after(expert_down, normed)))

    prim, sec = ("y", "z"), ("z", "y")
    got = [normed] + [shift(normed, prim, -o) for o in OFFSETS[1:]]
    low, high = jnp.stack(got[:2]), jnp.stack(got[2:])
    low_up, high_down = shift(low, sec, 1), shift(high, sec, -1)
    high_up, low_down = shift(high, sec, 1), shift(low, sec, -1)
    low_far, high_far = shift(low_up, sec, 1), shift(high_down, sec, -1)
    rest = (pick, put, weight, weights, swapped)
    low, high = experts([low, high], 0, *rest)
    low_up, high_up, low_down, high_down = experts(
        [low_up, high_up, low_down, high_down], 2, *rest
    )
    low_far, high_far = after((low_far, high_far), low_up, high_up)
    low_far, high_far = experts([low_far, high_far], 6, *rest)

    low_back, high_back = shift(low_up, sec, -1), shift(high_down, sec, 1)
    low_far, high_far = after((low_far, high_far), low_back, high_back)
    low_far, high_far = shift(low_far, sec, 1), shift(high_far, sec, -1)
    low_sum = (low_down.astype(f32) + low_far.astype(f32)).astype(jnp.bfloat16)
    high_sum = (high_up.astype(f32) + high_far.astype(f32)).astype(jnp.bfloat16)
    low_other, high_other = shift(low_sum, sec, 1), shift(high_sum, sec, -1)
    low = (low.astype(f32) + low_back.astype(f32) + low_other.astype(f32)).astype(jnp.bfloat16)
    high = (high.astype(f32) + high_back.astype(f32) + high_other.astype(f32)).astype(jnp.bfloat16)
    total = hidden + low[0].astype(f32)
    for block, o in ((low[1], -1), (high[0], 1), (high[1], 2)):
        total = total + shift(block, prim, o).astype(f32)
    return total.astype(jnp.bfloat16)[None]


def solution(mesh):
    return jax.shard_map(
        body,
        mesh=mesh,
        in_specs=(
            P(("dp", "pair"), "ctx", None),
            P(("dp", "pair"), "ctx", None),
            P(("dp", "pair"), "ctx", None),
            P(("dp", "pair"), "ctx", None),
            P(("dp", "pair"), None),
            P(("dp", "pair"), "ctx", None),
            P(("dp", "pair"), "ctx", None),
            P("ctx", "dp"),
            P(),
            P(("ctx", "pair"), None, None),
            P(("ctx", "pair"), None, None),
            P(("ctx", "pair"), None, None),
        ),
        out_specs=P(("dp", "pair"), "ctx", None),
        check_vma=False,
    )
```

```python
import functools
import math

import jax
import jax.numpy as jnp
from jax import lax
from jax.experimental import pallas as pl
from jax.experimental.pallas import tpu as pltpu
from jax.sharding import PartitionSpec as P

RING = 4
TOKENS = 128
WIDTH = 2048
HDIM = 128
HEADS_HERE = 16
FFE = 768
SLOTS = 48
EPSILON = 1e-06
NEGATIVE = -1e30
OFFSETS = (0, -1, 1, 2)
AXES = ("dp", "ctx", "pair")


def shift(value, axes, distance):
    pairs = []
    for x in range(RING):
        for y in range(RING):
            for z in range(RING):
                for core in range(2):
                    to = {"x": x, "y": y, "z": z}
                    to[axes[core]] = (to[axes[core]] + distance) % RING
                    pairs.append(
                        (
                            (x * 16 + y * 4 + z) * 2 + core,
                            (to["x"] * 16 + to["y"] * 4 + to["z"]) * 2 + core,
                        )
                    )
    return lax.ppermute(value, AXES, pairs)


def swap(value):
    return lax.ppermute(value, "pair", [(0, 1), (1, 0)])


def ring_slot(distance):
    distance = lax.rem(distance + 4, 4)
    return jnp.where(distance == 3, 1, jnp.where(distance == 0, 0, distance + 1))


def attend_kernel(offset, lengths, q_ref, kv_ref, out_ref, top_ref, sum_ref, acc_ref):
    place = lax.axis_index("ctx")
    y, z = place // 4, lax.rem(place, 4)
    block = lax.rem(y + offset + 4, 4) * 4 + z
    scale = math.log2(math.e) / math.sqrt(HDIM)
    places = block * TOKENS + lax.broadcasted_iota(jnp.int32, (1, TOKENS), 1)
    starts = jnp.zeros((1, TOKENS), jnp.int32)
    first = jnp.int32(0)
    end = jnp.int32(0)
    for d in range(8):
        end = end + lengths[0, d]
        starts = jnp.maximum(starts, jnp.where(places >= end, end, 0))
        first = jnp.maximum(first, jnp.where(block * TOKENS >= end, end, 0))
    top_ref[...] = jnp.full_like(top_ref, NEGATIVE)
    sum_ref[...] = jnp.zeros_like(sum_ref)
    acc_ref[...] = jnp.zeros_like(acc_ref)
    rows = lax.broadcasted_iota(jnp.int32, (TOKENS, TOKENS), 0)

    def step(chunk, carry):
        slot = ring_slot(lax.rem(chunk, 4) - z) * 4 + ring_slot(chunk // 4 - y)
        keys = kv_ref[slot, :TOKENS, :HDIM]
        values = kv_ref[slot, :TOKENS, HDIM:].T
        key_places = chunk * TOKENS + rows
        allowed = (key_places <= places) & (key_places >= starts)
        bias = jnp.where(allowed, 0.0, NEGATIVE).astype(jnp.float32)
        bias = jnp.concatenate([bias, bias], axis=1)
        for pair in range(HEADS_HERE // 2):
            h = 2 * pair * HDIM
            q = jnp.concatenate([q_ref[:, h : h + HDIM], q_ref[:, h + HDIM : h + 2 * HDIM]], axis=0)
            s = lax.dot_general(
                keys, q, (((1,), (1,)), ((), ())), preferred_element_type=jnp.float32
            )
            s = s * scale + bias
            old = top_ref[pair]
            top = jnp.maximum(old, jnp.max(s, axis=0, keepdims=True))
            weights = jnp.exp2(s - top)
            fade = jnp.exp2(old - top)
            top_ref[pair] = top
            sum_ref[pair] = sum_ref[pair] * fade + jnp.sum(weights, axis=0, keepdims=True)
            acc_ref[pair] = acc_ref[pair] * fade + jnp.dot(
                values, weights.astype(jnp.bfloat16), preferred_element_type=jnp.float32
            )
        return carry

    lax.fori_loop(first // TOKENS, block + 1, step, 0)
    for pair in range(HEADS_HERE // 2):
        h = 2 * pair * HDIM
        mixed = (acc_ref[pair] / sum_ref[pair]).T.astype(jnp.bfloat16)
        out_ref[:, h : h + HDIM] = mixed[:TOKENS]
        out_ref[:, h + HDIM : h + 2 * HDIM] = mixed[TOKENS:]


def attend(offset, lengths, queries, kv):
    vmem = pl.BlockSpec(memory_space=pltpu.VMEM)
    return pl.pallas_call(
        functools.partial(attend_kernel, offset),
        out_shape=jax.ShapeDtypeStruct((TOKENS, WIDTH), jnp.bfloat16),
        in_specs=[pl.BlockSpec(memory_space=pltpu.SMEM), vmem, vmem],
        out_specs=vmem,
        scratch_shapes=[
            pltpu.VMEM((8, 1, 256), jnp.float32),
            pltpu.VMEM((8, 1, 256), jnp.float32),
            pltpu.VMEM((8, HDIM, 256), jnp.float32),
        ],
        compiler_params=pltpu.CompilerParams(vmem_limit_bytes=8 * 2**20),
        cost_estimate=pl.CostEstimate(
            flops=4 * 2**30, bytes_accessed=3 * 2**20, transcendentals=2048 * 640
        ),
        name="attend",
    )(lengths, queries, kv)


def project_kernel(count, *refs):
    att, own, other = refs[0:count], refs[count : count + 4], refs[count + 4 : count + 8]
    outs = refs[count + 8 :]
    x, core = lax.axis_index("dp"), lax.axis_index("pair")
    z = lax.rem(lax.axis_index("ctx"), 4)

    def run(stacks):
        for i in range(4):
            column = lax.rem(x + OFFSETS[i] + 4, 4) * 512
            total = None
            for half in range(2):
                for j in range(4):
                    place = lax.rem(z + OFFSETS[j] + 4, 4) * 512 + half * 256
                    place = pl.ds(pl.multiple_of(place, 256), 256)
                    left = jnp.concatenate([a[:, place] for a in att], axis=0)
                    right = stacks[0][j][i] if half == 0 else stacks[1][i][j]
                    term = jnp.dot(left, right, preferred_element_type=jnp.float32)
                    total = term if total is None else total + term
            total = total.astype(jnp.bfloat16)
            for n in range(count):
                part = total[n * TOKENS : (n + 1) * TOKENS]
                outs[n][:, pl.ds(pl.multiple_of(column, 512), 512)] = part

    @pl.when(core == 0)
    def _():
        run((own, other))

    @pl.when(core == 1)
    def _():
        run((other, own))


def project(attended, own, other):
    vmem = pl.BlockSpec(memory_space=pltpu.VMEM)
    count = len(attended)
    return pl.pallas_call(
        functools.partial(project_kernel, count),
        out_shape=[jax.ShapeDtypeStruct((TOKENS, WIDTH), jnp.bfloat16)] * count,
        in_specs=[vmem] * (count + 8),
        out_specs=[vmem] * count,
        compiler_params=pltpu.CompilerParams(vmem_limit_bytes=14 * 2**20),
        cost_estimate=pl.CostEstimate(
            flops=2 * count * TOKENS * 2048 * 2048,
            bytes_accessed=(8 + count) * 2**20,
            transcendentals=0,
        ),
        name="project",
    )(*attended, *own, *other)


def experts_kernel(count, *refs):
    arrays = count // 2
    pieces, refs = refs[:arrays], refs[arrays:]
    pick_ref, put_ref, weight_ref = refs[:3]
    hbm = refs[3:9]
    outs, refs = refs[9 : 9 + arrays], refs[9 + arrays :]
    rows_ref, act_ref, gate_buf, up_buf, down_buf, sems = refs
    buffers = (gate_buf, up_buf, down_buf)

    def copies(e):
        side, index, slot = e // 2, e % 2, e % 2
        return [
            pltpu.make_async_copy(
                hbm[3 * side + w].at[index], buffers[w].at[slot], sems.at[w, slot]
            )
            for w in range(3)
        ]

    for e in range(2):
        for c in copies(e):
            c.start()
    for p in range(count):
        for n in range(4):
            cols = pl.ds(n * 512, 512)
            picked = jnp.dot(
                pick_ref[p],
                pieces[p // 2][p % 2 * 2 : p % 2 * 2 + 2, :, cols].reshape(256, 512),
                preferred_element_type=jnp.float32,
            )
            rows_ref[p, :, :, cols] = picked.astype(jnp.bfloat16).reshape(4, SLOTS, 512)
    for e in range(4):
        slot = e % 2
        waits = copies(e)
        waits[0].wait()
        waits[1].wait()
        rows = rows_ref[:, e].reshape(count * SLOTS, WIDTH)
        for n in range(3):
            cols = pl.ds(n * 256, 256)
            gate = jnp.dot(rows, gate_buf[slot, :, cols], preferred_element_type=jnp.float32)
            upward = jnp.dot(rows, up_buf[slot, :, cols], preferred_element_type=jnp.float32)
            act_ref[:, cols] = (gate / (1.0 + jnp.exp(-gate)) * upward).astype(jnp.bfloat16)
        waits[2].wait()
        active = act_ref[...]
        scale = weight_ref[e]
        for n in range(4):
            cols = pl.ds(n * 512, 512)
            result = jnp.dot(active, down_buf[slot, :, cols], preferred_element_type=jnp.float32)
            result = (result * scale).astype(jnp.bfloat16)
            rows_ref[:, e, :, cols] = result.reshape(count, SLOTS, 512)
        if e + 2 < 4:
            for c in copies(e + 2):
                c.start()
    for p in range(count):
        for n in range(4):
            cols = pl.ds(n * 512, 512)
            mixed = jnp.dot(
                put_ref[p],
                rows_ref[p, :, :, cols].reshape(4 * SLOTS, 512),
                preferred_element_type=jnp.float32,
            )
            mixed = mixed.astype(jnp.bfloat16).reshape(2, TOKENS, 512)
            outs[p // 2][p % 2 * 2 : p % 2 * 2 + 2, :, cols] = mixed


def experts(pieces, first, pick, put, weight, mine, others):
    count = 2 * len(pieces)
    vmem = pl.BlockSpec(memory_space=pltpu.VMEM)
    hbm = pl.BlockSpec(memory_space=pl.ANY)
    rows = count * 4 * SLOTS
    return pl.pallas_call(
        functools.partial(experts_kernel, count),
        out_shape=[jax.ShapeDtypeStruct((4, TOKENS, WIDTH), jnp.bfloat16)] * len(pieces),
        in_specs=[vmem] * (len(pieces) + 3) + [hbm] * 6,
        out_specs=[vmem] * len(pieces),
        scratch_shapes=[
            pltpu.VMEM((count, 4, SLOTS, WIDTH), jnp.bfloat16),
            pltpu.VMEM((count * SLOTS, FFE), jnp.bfloat16),
            pltpu.VMEM((2, WIDTH, FFE), jnp.bfloat16),
            pltpu.VMEM((2, WIDTH, FFE), jnp.bfloat16),
            pltpu.VMEM((2, FFE, WIDTH), jnp.bfloat16),
            pltpu.SemaphoreType.DMA((3, 2)),
        ],
        compiler_params=pltpu.CompilerParams(vmem_limit_bytes=(21 + 3 * count) * 2**20),
        cost_estimate=pl.CostEstimate(
            flops=6 * rows * 2048 * 768,
            bytes_accessed=(36 + 2 * count) * 2**20,
            transcendentals=rows * 768,
        ),
        name="experts",
    )(
        *pieces,
        pick[first : first + count],
        put[first : first + count],
        weight[:, first * SLOTS : (first + count) * SLOTS],
        *mine,
        *others,
    )


def routing(meta, y, z, core):
    meta = jnp.where(core == 0, meta, meta.transpose(1, 0, 2, 3)).astype(jnp.float32)
    meta = meta.reshape(8, 2, 32, TOKENS).transpose(0, 2, 1, 3).reshape(8, 32, 2 * TOKENS)
    ids = meta[:, :8]
    route = meta[:, 8:16] + meta[:, 16:24] + meta[:, 24:32]
    chip = (y * 4 + z) * 4
    wanted = chip + jnp.stack([core * 2, core * 2 + 1, 2 - core * 2, 3 - core * 2])
    same = ids[:, None] == wanted.astype(jnp.float32)[None, :, None, None]
    chosen = jnp.any(same, axis=2)
    share = jnp.sum(jnp.where(same, route[:, None], 0.0), axis=2)
    places = jnp.arange(2 * TOKENS, dtype=jnp.int32)
    before = (places[:, None] < places[None, :]).astype(jnp.bfloat16)
    rank = jnp.einsum(
        "pet,tu->peu", chosen.astype(jnp.bfloat16), before, preferred_element_type=jnp.float32
    )
    slots = jnp.arange(SLOTS, dtype=jnp.float32)
    pick = chosen[:, :, None] & (rank[:, :, None] == slots[None, None, :, None])
    weight = jnp.sum(jnp.where(pick, share[:, :, None], 0.0), axis=3)
    weight = weight.transpose(1, 0, 2).reshape(4, 8 * SLOTS, 1)
    pick = pick.astype(jnp.bfloat16).reshape(8, 4 * SLOTS, 2 * TOKENS)
    return pick, pick.transpose(0, 2, 1), weight


def after(value, *others):
    return lax.optimization_barrier((value, *others))[0]


def body(
    queries,
    keys,
    values,
    residual,
    doc_lengths,
    expert_ids,
    route_weights,
    out_weight,
    norm_gain,
    expert_gate,
    expert_up,
    expert_down,
):
    f32 = jnp.float32
    x, core = lax.axis_index("dp"), lax.axis_index("pair")
    y, z = lax.axis_index("ctx") // 4, lax.axis_index("ctx") % 4
    yy, zz = ("y", "y"), ("z", "z")
    queries, keys, values = queries[0], keys[0], values[0]

    route = route_weights[0].T
    high = lax.reduce_precision(route, 8, 7)
    middle = lax.reduce_precision(route - high, 8, 7)
    low = route - high - middle
    meta = jnp.concatenate([expert_ids[0].T.astype(f32), high, middle, low])
    meta = meta.astype(jnp.bfloat16)
    meta = jnp.concatenate([meta[:16], meta[16:]], axis=1)

    def kv_of(head):
        pair = jnp.concatenate(
            [
                lax.dynamic_slice_in_dim(keys, head * HDIM, HDIM, 1),
                lax.dynamic_slice_in_dim(values, head * HDIM, HDIM, 1),
            ],
            axis=1,
        )
        return jnp.concatenate([pair, meta])

    kv_y = [kv_of(y)] + [shift(kv_of((y - o + 4) % 4), yy, -o) for o in OFFSETS[1:]]
    column = jnp.stack(kv_y)
    kv = jnp.concatenate([column] + [shift(column, zz, -o) for o in OFFSETS[1:]])

    def queries_of(group):
        return lax.dynamic_slice_in_dim(queries, group * WIDTH, WIDTH, 1)

    part = lax.dynamic_slice_in_dim(out_weight, core * 256, 256, 0)
    inner = jnp.stack([part] + [shift(part, ("x", "z"), -o) for o in OFFSETS[1:]])
    blocks = [queries_of(y), None, None, shift(queries_of((y + 2) % 4), yy, -2)]
    for k in (1, 2):
        o = OFFSETS[k]
        near = after(queries_of((y - o + 4) % 4), blocks[3], inner, column)
        blocks[k] = shift(near, yy, -o)

    inner = after(inner, kv)
    own = [inner] + [shift(inner, ("z", "x"), -o) for o in OFFSETS[1:]]
    meta = kv[:, TOKENS:]
    meta = jnp.concatenate([meta[:, :, :TOKENS], meta[:, :, TOKENS:]], axis=1)
    pick, put, weight = routing(meta.reshape(4, 4, 32, TOKENS), y, z, core)

    def attended(k):
        return attend(OFFSETS[k], doc_lengths, blocks[k], kv)

    last = blocks[2]
    blocks[2] = after(last, *own)
    mixed = [attended(k) for k in range(4)]
    other = [swap(after(w, mixed[0], mixed[3], mixed[1], last)) for w in own]

    (far,) = project([after(mixed[3], mixed[2])], own, other)
    near = [after(mixed[1], far), mixed[2], mixed[0]]
    below, above, here = project(near, own, other)

    weights = [expert_gate, expert_up, expert_down]
    swapped = [swap(after(expert_gate, far)), swap(after(expert_up, far))]

    terms = [here, shift(below, yy, -1), shift(above, yy, 1), shift(far, yy, 2)]
    hidden = residual[0].astype(f32) + sum(t.astype(f32) for t in terms)
    mean_square = jnp.mean(hidden * hidden, axis=-1, keepdims=True)
    normed = (hidden * lax.rsqrt(mean_square + EPSILON) * norm_gain).astype(jnp.bfloat16)
    normed = after(normed, pick, put, weight, *swapped)
    swapped.append(swap(after(expert_down, normed)))

    prim, sec = ("y", "z"), ("z", "y")
    here = jnp.stack([normed] + [shift(normed, prim, -o) for o in OFFSETS[1:]])
    below, above, far = shift(here, sec, 1), shift(here, sec, -1), shift(here, sec, 2)
    rest = (pick, put, weight, weights, swapped)
    (here,) = experts([here], 0, *rest)
    below, above = experts(list(after((below, above), here)), 2, *rest)
    (far,) = experts([after(far, below)], 6, *rest)

    near = [here, shift(below, sec, -1), shift(above, sec, 1)]
    near = lax.optimization_barrier(sum(part.astype(f32) for part in near))
    total = near + shift(far, sec, 2).astype(f32)
    back = total[1:].astype(jnp.bfloat16)
    total = hidden + total[0]
    for k in range(3):
        total = total + shift(back[k], prim, OFFSETS[k + 1]).astype(f32)
    return total.astype(jnp.bfloat16)[None]


def solution(mesh):
    return jax.shard_map(
        body,
        mesh=mesh,
        in_specs=(
            P(("dp", "pair"), "ctx", None),
            P(("dp", "pair"), "ctx", None),
            P(("dp", "pair"), "ctx", None),
            P(("dp", "pair"), "ctx", None),
            P(("dp", "pair"), None),
            P(("dp", "pair"), "ctx", None),
            P(("dp", "pair"), "ctx", None),
            P("ctx", "dp"),
            P(),
            P(("ctx", "pair"), None, None),
            P(("ctx", "pair"), None, None),
            P(("ctx", "pair"), None, None),
        ),
        out_specs=P(("dp", "pair"), "ctx", None),
        check_vma=False,
    )
```

```python
import functools
import math

import jax
import jax.numpy as jnp
from jax import lax
from jax.experimental import pallas as pl
from jax.experimental.pallas import tpu as pltpu
from jax.sharding import PartitionSpec as P

RING = 4
TOKENS = 128
WIDTH = 2048
HDIM = 128
HEADS_HERE = 16
FFE = 768
SLOTS = 48
EPSILON = 1e-06
NEGATIVE = -1e30
OFFSETS = (0, -1, 1, 2)
AXES = ("dp", "ctx", "pair")


def shift(value, axes, distance):
    pairs = []
    for x in range(RING):
        for y in range(RING):
            for z in range(RING):
                for core in range(2):
                    to = {"x": x, "y": y, "z": z}
                    to[axes[core]] = (to[axes[core]] + distance) % RING
                    pairs.append(
                        (
                            (x * 16 + y * 4 + z) * 2 + core,
                            (to["x"] * 16 + to["y"] * 4 + to["z"]) * 2 + core,
                        )
                    )
    return lax.ppermute(value, AXES, pairs)


def swap(value):
    return lax.ppermute(value, "pair", [(0, 1), (1, 0)])


def ring_slot(distance):
    distance = lax.rem(distance + 4, 4)
    return jnp.where(distance == 3, 1, jnp.where(distance == 0, 0, distance + 1))


def attend_kernel(offset, lengths, q_ref, kv_ref, out_ref, top_ref, sum_ref, acc_ref):
    place = lax.axis_index("ctx")
    y, z = place // 4, lax.rem(place, 4)
    block = lax.rem(y + offset + 4, 4) * 4 + z
    scale = math.log2(math.e) / math.sqrt(HDIM)
    places = block * TOKENS + lax.broadcasted_iota(jnp.int32, (1, TOKENS), 1)
    starts = jnp.zeros((1, TOKENS), jnp.int32)
    first = jnp.int32(0)
    end = jnp.int32(0)
    for d in range(8):
        end = end + lengths[0, d]
        starts = jnp.maximum(starts, jnp.where(places >= end, end, 0))
        first = jnp.maximum(first, jnp.where(block * TOKENS >= end, end, 0))
    top_ref[...] = jnp.full_like(top_ref, NEGATIVE)
    sum_ref[...] = jnp.zeros_like(sum_ref)
    acc_ref[...] = jnp.zeros_like(acc_ref)
    rows = lax.broadcasted_iota(jnp.int32, (TOKENS, TOKENS), 0)

    def step(chunk, carry):
        slot = ring_slot(lax.rem(chunk, 4) - z) * 4 + ring_slot(chunk // 4 - y)
        keys = kv_ref[slot, :TOKENS, :HDIM]
        values = kv_ref[slot, :TOKENS, HDIM:].T
        key_places = chunk * TOKENS + rows
        allowed = (key_places <= places) & (key_places >= starts)
        bias = jnp.where(allowed, 0.0, NEGATIVE).astype(jnp.float32)
        bias = jnp.concatenate([bias, bias], axis=1)
        for pair in range(HEADS_HERE // 2):
            h = 2 * pair * HDIM
            q = jnp.concatenate([q_ref[:, h : h + HDIM], q_ref[:, h + HDIM : h + 2 * HDIM]], axis=0)
            s = lax.dot_general(
                keys, q, (((1,), (1,)), ((), ())), preferred_element_type=jnp.float32
            )
            s = s * scale + bias
            old = top_ref[pair]
            top = jnp.maximum(old, jnp.max(s, axis=0, keepdims=True))
            weights = jnp.exp2(s - top)
            fade = jnp.exp2(old - top)
            top_ref[pair] = top
            sum_ref[pair] = sum_ref[pair] * fade + jnp.sum(weights, axis=0, keepdims=True)
            acc_ref[pair] = acc_ref[pair] * fade + jnp.dot(
                values, weights.astype(jnp.bfloat16), preferred_element_type=jnp.float32
            )
        return carry

    lax.fori_loop(first // TOKENS, block + 1, step, 0)
    for pair in range(HEADS_HERE // 2):
        h = 2 * pair * HDIM
        mixed = (acc_ref[pair] / sum_ref[pair]).T.astype(jnp.bfloat16)
        out_ref[:, h : h + HDIM] = mixed[:TOKENS]
        out_ref[:, h + HDIM : h + 2 * HDIM] = mixed[TOKENS:]


def attend(offset, lengths, queries, kv):
    vmem = pl.BlockSpec(memory_space=pltpu.VMEM)
    return pl.pallas_call(
        functools.partial(attend_kernel, offset),
        out_shape=jax.ShapeDtypeStruct((TOKENS, WIDTH), jnp.bfloat16),
        in_specs=[pl.BlockSpec(memory_space=pltpu.SMEM), vmem, vmem],
        out_specs=vmem,
        scratch_shapes=[
            pltpu.VMEM((8, 1, 256), jnp.float32),
            pltpu.VMEM((8, 1, 256), jnp.float32),
            pltpu.VMEM((8, HDIM, 256), jnp.float32),
        ],
        compiler_params=pltpu.CompilerParams(vmem_limit_bytes=8 * 2**20),
        cost_estimate=pl.CostEstimate(
            flops=4 * 2**30, bytes_accessed=3 * 2**20, transcendentals=2048 * 640
        ),
        name="attend",
    )(lengths, queries, kv)


def project_kernel(count, *refs):
    att, own, other = refs[0:count], refs[count : count + 4], refs[count + 4 : count + 8]
    outs = refs[count + 8 :]
    x, core = lax.axis_index("dp"), lax.axis_index("pair")
    z = lax.rem(lax.axis_index("ctx"), 4)

    def run(stacks):
        for i in range(4):
            column = lax.rem(x + OFFSETS[i] + 4, 4) * 512
            total = None
            for half in range(2):
                for j in range(4):
                    place = lax.rem(z + OFFSETS[j] + 4, 4) * 512 + half * 256
                    place = pl.ds(pl.multiple_of(place, 256), 256)
                    left = jnp.concatenate([a[:, place] for a in att], axis=0)
                    right = stacks[0][j][i] if half == 0 else stacks[1][i][j]
                    term = jnp.dot(left, right, preferred_element_type=jnp.float32)
                    total = term if total is None else total + term
            total = total.astype(jnp.bfloat16)
            for n in range(count):
                part = total[n * TOKENS : (n + 1) * TOKENS]
                outs[n][:, pl.ds(pl.multiple_of(column, 512), 512)] = part

    @pl.when(core == 0)
    def _():
        run((own, other))

    @pl.when(core == 1)
    def _():
        run((other, own))


def project(attended, own, other):
    vmem = pl.BlockSpec(memory_space=pltpu.VMEM)
    count = len(attended)
    return pl.pallas_call(
        functools.partial(project_kernel, count),
        out_shape=[jax.ShapeDtypeStruct((TOKENS, WIDTH), jnp.bfloat16)] * count,
        in_specs=[vmem] * (count + 8),
        out_specs=[vmem] * count,
        compiler_params=pltpu.CompilerParams(vmem_limit_bytes=14 * 2**20),
        cost_estimate=pl.CostEstimate(
            flops=2 * count * TOKENS * 2048 * 2048,
            bytes_accessed=(8 + count) * 2**20,
            transcendentals=0,
        ),
        name="project",
    )(*attended, *own, *other)


def experts_kernel(count, *refs):
    arrays = count // 2
    pieces = []
    while len(pieces) < count:
        ref, refs = refs[0], refs[1:]
        pieces += [ref.at[b : b + 2] for b in range(0, ref.shape[0], 2)]
    pick_ref, put_ref, weight_ref = refs[:3]
    hbm = refs[3:6]
    outs, refs = refs[6 : 6 + arrays], refs[6 + arrays :]
    rows_ref, act_ref, gate_buf, up_buf, down_buf, sems = refs
    buffers = (gate_buf, up_buf, down_buf)

    def copies(e):
        slot = e % 2
        return [
            pltpu.make_async_copy(hbm[w].at[e], buffers[w].at[slot], sems.at[w, slot])
            for w in range(3)
        ]

    for e in range(2):
        for c in copies(e):
            c.start()
    for p in range(count):
        for n in range(4):
            cols = pl.ds(n * 512, 512)
            picked = jnp.dot(
                pick_ref[p],
                pieces[p][:, :, cols].reshape(256, 512),
                preferred_element_type=jnp.float32,
            )
            rows_ref[p, :, :, cols] = picked.astype(jnp.bfloat16).reshape(4, SLOTS, 512)
    for e in range(4):
        slot = e % 2
        waits = copies(e)
        waits[0].wait()
        waits[1].wait()
        rows = rows_ref[:, e].reshape(count * SLOTS, WIDTH)
        for n in range(3):
            cols = pl.ds(n * 256, 256)
            gate = jnp.dot(rows, gate_buf[slot, :, cols], preferred_element_type=jnp.float32)
            upward = jnp.dot(rows, up_buf[slot, :, cols], preferred_element_type=jnp.float32)
            act_ref[:, cols] = (gate / (1.0 + jnp.exp(-gate)) * upward).astype(jnp.bfloat16)
        waits[2].wait()
        active = act_ref[...]
        scale = weight_ref[e]
        for n in range(4):
            cols = pl.ds(n * 512, 512)
            result = jnp.dot(active, down_buf[slot, :, cols], preferred_element_type=jnp.float32)
            result = (result * scale).astype(jnp.bfloat16)
            rows_ref[:, e, :, cols] = result.reshape(count, SLOTS, 512)
        if e + 2 < 4:
            for c in copies(e + 2):
                c.start()
    for p in range(count):
        for n in range(4):
            cols = pl.ds(n * 512, 512)
            mixed = jnp.dot(
                put_ref[p],
                rows_ref[p, :, :, cols].reshape(4 * SLOTS, 512),
                preferred_element_type=jnp.float32,
            )
            mixed = mixed.astype(jnp.bfloat16).reshape(2, TOKENS, 512)
            outs[p // 2][p % 2 * 2 : p % 2 * 2 + 2, :, cols] = mixed


def experts(pieces, first, pick, put, weight, gate, up, down):
    count = sum(piece.shape[0] for piece in pieces) // 2
    vmem = pl.BlockSpec(memory_space=pltpu.VMEM)
    hbm = pl.BlockSpec(memory_space=pltpu.HBM)
    rows = count * 4 * SLOTS
    return pl.pallas_call(
        functools.partial(experts_kernel, count),
        out_shape=[jax.ShapeDtypeStruct((4, TOKENS, WIDTH), jnp.bfloat16)] * (count // 2),
        in_specs=[vmem] * (len(pieces) + 3) + [hbm] * 3,
        out_specs=[vmem] * (count // 2),
        scratch_shapes=[
            pltpu.VMEM((count, 4, SLOTS, WIDTH), jnp.bfloat16),
            pltpu.VMEM((count * SLOTS, FFE), jnp.bfloat16),
            pltpu.VMEM((2, WIDTH, FFE), jnp.bfloat16),
            pltpu.VMEM((2, WIDTH, FFE), jnp.bfloat16),
            pltpu.VMEM((2, FFE, WIDTH), jnp.bfloat16),
            pltpu.SemaphoreType.DMA((3, 2)),
        ],
        compiler_params=pltpu.CompilerParams(vmem_limit_bytes=(21 + 3 * count) * 2**20),
        cost_estimate=pl.CostEstimate(
            flops=6 * rows * 2048 * 768,
            bytes_accessed=(36 + 2 * count) * 2**20,
            transcendentals=rows * 768,
        ),
        name="experts",
    )(
        *pieces,
        pick[first : first + count],
        put[first : first + count],
        weight[:, first * SLOTS : (first + count) * SLOTS],
        gate,
        up,
        down,
    )


def routing(meta, y, z, core):
    meta = jnp.where(core == 0, meta, meta.transpose(1, 0, 2, 3)).astype(jnp.float32)
    meta = meta.reshape(8, 2, 32, TOKENS).transpose(0, 2, 1, 3).reshape(8, 32, 2 * TOKENS)
    ids = meta[:, :8]
    route = meta[:, 8:16] + meta[:, 16:24] + meta[:, 24:32]
    chip = (y * 4 + z) * 4
    wanted = chip + jnp.arange(4, dtype=jnp.int32)
    same = ids[:, None] == wanted.astype(jnp.float32)[None, :, None, None]
    chosen = jnp.any(same, axis=2)
    share = jnp.sum(jnp.where(same, route[:, None], 0.0), axis=2)
    places = jnp.arange(2 * TOKENS, dtype=jnp.int32)
    before = (places[:, None] < places[None, :]).astype(jnp.bfloat16)
    rank = jnp.einsum(
        "pet,tu->peu", chosen.astype(jnp.bfloat16), before, preferred_element_type=jnp.float32
    )
    slots = jnp.arange(SLOTS, dtype=jnp.float32)
    pick = chosen[:, :, None] & (rank[:, :, None] == slots[None, None, :, None])
    weight = jnp.sum(jnp.where(pick, share[:, :, None], 0.0), axis=3)
    weight = weight.transpose(1, 0, 2).reshape(4, 8 * SLOTS, 1)
    pick = pick.astype(jnp.bfloat16).reshape(8, 4 * SLOTS, 2 * TOKENS)
    return pick, pick.transpose(0, 2, 1), weight


def after(value, *others):
    return lax.optimization_barrier((value, *others))[0]


def body(
    queries,
    keys,
    values,
    residual,
    doc_lengths,
    expert_ids,
    route_weights,
    out_weight,
    norm_gain,
    expert_gate,
    expert_up,
    expert_down,
):
    f32 = jnp.float32
    x, core = lax.axis_index("dp"), lax.axis_index("pair")
    y, z = lax.axis_index("ctx") // 4, lax.axis_index("ctx") % 4
    yy, zz = ("y", "y"), ("z", "z")
    queries, keys, values = queries[0], keys[0], values[0]

    route = route_weights[0].T
    high = lax.reduce_precision(route, 8, 7)
    middle = lax.reduce_precision(route - high, 8, 7)
    low = route - high - middle
    meta = jnp.concatenate([expert_ids[0].T.astype(f32), high, middle, low])
    meta = meta.astype(jnp.bfloat16)
    meta = jnp.concatenate([meta[:16], meta[16:]], axis=1)

    weights = [
        lax.all_gather(w, "pair", axis=0, tiled=True)
        for w in (expert_gate, expert_up, expert_down)
    ]

    def kv_of(head):
        pair = jnp.concatenate(
            [
                lax.dynamic_slice_in_dim(keys, head * HDIM, HDIM, 1),
                lax.dynamic_slice_in_dim(values, head * HDIM, HDIM, 1),
            ],
            axis=1,
        )
        return jnp.concatenate([pair, meta])

    kv_y = [kv_of(y)] + [shift(kv_of((y - o + 4) % 4), yy, -o) for o in OFFSETS[1:]]
    column = jnp.stack(kv_y)
    kv = jnp.concatenate([column] + [shift(column, zz, -o) for o in OFFSETS[1:]])

    def queries_of(group):
        return lax.dynamic_slice_in_dim(queries, group * WIDTH, WIDTH, 1)

    part = lax.dynamic_slice_in_dim(out_weight, core * 256, 256, 0)
    inner = jnp.stack([part] + [shift(part, ("x", "z"), -o) for o in OFFSETS[1:]])
    blocks = [queries_of(y), None, None, shift(queries_of((y + 2) % 4), yy, -2)]
    for k in (1, 2):
        o = OFFSETS[k]
        near = after(queries_of((y - o + 4) % 4), blocks[3], inner, column)
        blocks[k] = shift(near, yy, -o)

    inner = after(inner, kv)
    own = [inner] + [shift(inner, ("z", "x"), -o) for o in OFFSETS[1:]]
    meta = kv[:, TOKENS:]
    meta = jnp.concatenate([meta[:, :, :TOKENS], meta[:, :, TOKENS:]], axis=1)
    pick, put, weight = routing(meta.reshape(4, 4, 32, TOKENS), y, z, core)

    def attended(k):
        return attend(OFFSETS[k], doc_lengths, blocks[k], kv)

    last = blocks[2]
    blocks[2] = after(last, *own)
    mixed = [attended(k) for k in range(4)]
    other = [swap(after(w, mixed[0], mixed[3], mixed[1], last)) for w in own]

    far, below, above, here = project([mixed[3], mixed[1], mixed[2], mixed[0]], own, other)
    terms = [here, shift(below, yy, -1), shift(above, yy, 1), shift(far, yy, 2)]
    hidden = residual[0].astype(f32) + sum(t.astype(f32) for t in terms)
    mean_square = jnp.mean(hidden * hidden, axis=-1, keepdims=True)
    normed = (hidden * lax.rsqrt(mean_square + EPSILON) * norm_gain).astype(jnp.bfloat16)
    normed = after(normed, pick, put, weight)

    prim, sec = ("y", "z"), ("z", "y")
    here = jnp.stack([normed] + [shift(normed, prim, -o) for o in OFFSETS[1:]])
    below, above = shift(here, sec, 1), shift(here, sec, -1)
    rest = (pick, put, weight, *weights)
    (here,) = experts([here], 0, *rest)
    below, above = after((below, above), here)
    far = [shift(below[:2], sec, 1), shift(above[2:], sec, -1)]
    below, above = experts([below, above], 2, *rest)
    (far,) = experts(list(after(tuple(far), below)), 6, *rest)

    near = [here, shift(below, sec, -1), shift(above, sec, 1)]
    near = lax.optimization_barrier(sum(part.astype(f32) for part in near))
    total = near + shift(far, sec, 2).astype(f32)
    back = total[1:].astype(jnp.bfloat16)
    total = hidden + total[0]
    for k in range(3):
        total = total + shift(back[k], prim, OFFSETS[k + 1]).astype(f32)
    return total.astype(jnp.bfloat16)[None]


def solution(mesh):
    return jax.shard_map(
        body,
        mesh=mesh,
        in_specs=(
            P(("dp", "pair"), "ctx", None),
            P(("dp", "pair"), "ctx", None),
            P(("dp", "pair"), "ctx", None),
            P(("dp", "pair"), "ctx", None),
            P(("dp", "pair"), None),
            P(("dp", "pair"), "ctx", None),
            P(("dp", "pair"), "ctx", None),
            P("ctx", "dp"),
            P(),
            P(("ctx", "pair"), None, None),
            P(("ctx", "pair"), None, None),
            P(("ctx", "pair"), None, None),
        ),
        out_specs=P(("dp", "pair"), "ctx", None),
        check_vma=False,
    )
```

```python
import functools
import math

import jax
import jax.numpy as jnp
from jax import lax
from jax.experimental import pallas as pl
from jax.experimental.pallas import tpu as pltpu
from jax.sharding import PartitionSpec as P

RING = 4
TOKENS = 128
WIDTH = 2048
HDIM = 128
HEADS_HERE = 16
FFE = 768
SLOTS = 48
EPSILON = 1e-06
NEGATIVE = -1e30
OFFSETS = (0, -1, 1, 2)
AXES = ("dp", "ctx", "pair")


def shift(value, axes, distance):
    pairs = []
    for x in range(RING):
        for y in range(RING):
            for z in range(RING):
                for core in range(2):
                    to = {"x": x, "y": y, "z": z}
                    to[axes[core]] = (to[axes[core]] + distance) % RING
                    pairs.append(
                        (
                            (x * 16 + y * 4 + z) * 2 + core,
                            (to["x"] * 16 + to["y"] * 4 + to["z"]) * 2 + core,
                        )
                    )
    return lax.ppermute(value, AXES, pairs)


def swap(value):
    return lax.ppermute(value, "pair", [(0, 1), (1, 0)])


def ring_slot(distance):
    distance = lax.rem(distance + 4, 4)
    return jnp.where(distance == 3, 1, jnp.where(distance == 0, 0, distance + 1))


def attend_kernel(offset, lengths, q_ref, kv_ref, out_ref, top_ref, sum_ref, acc_ref):
    place = lax.axis_index("ctx")
    y, z = place // 4, lax.rem(place, 4)
    block = lax.rem(y + offset + 4, 4) * 4 + z
    scale = math.log2(math.e) / math.sqrt(HDIM)
    places = block * TOKENS + lax.broadcasted_iota(jnp.int32, (1, TOKENS), 1)
    starts = jnp.zeros((1, TOKENS), jnp.int32)
    first = jnp.int32(0)
    end = jnp.int32(0)
    for d in range(8):
        end = end + lengths[0, d]
        starts = jnp.maximum(starts, jnp.where(places >= end, end, 0))
        first = jnp.maximum(first, jnp.where(block * TOKENS >= end, end, 0))
    top_ref[...] = jnp.full_like(top_ref, NEGATIVE)
    sum_ref[...] = jnp.zeros_like(sum_ref)
    acc_ref[...] = jnp.zeros_like(acc_ref)
    rows = lax.broadcasted_iota(jnp.int32, (TOKENS, TOKENS), 0)

    def step(chunk, carry):
        slot = ring_slot(lax.rem(chunk, 4) - z) * 4 + ring_slot(chunk // 4 - y)
        keys = kv_ref[slot, :TOKENS, :HDIM]
        values = kv_ref[slot, :TOKENS, HDIM:].T
        key_places = chunk * TOKENS + rows
        allowed = (key_places <= places) & (key_places >= starts)
        bias = jnp.where(allowed, 0.0, NEGATIVE).astype(jnp.float32)
        bias = jnp.concatenate([bias, bias], axis=1)
        for pair in range(HEADS_HERE // 2):
            h = 2 * pair * HDIM
            q = jnp.concatenate([q_ref[:, h : h + HDIM], q_ref[:, h + HDIM : h + 2 * HDIM]], axis=0)
            s = lax.dot_general(
                keys, q, (((1,), (1,)), ((), ())), preferred_element_type=jnp.float32
            )
            s = s * scale + bias
            old = top_ref[pair]
            top = jnp.maximum(old, jnp.max(s, axis=0, keepdims=True))
            weights = jnp.exp2(s - top)
            fade = jnp.exp2(old - top)
            top_ref[pair] = top
            sum_ref[pair] = sum_ref[pair] * fade + jnp.sum(weights, axis=0, keepdims=True)
            acc_ref[pair] = acc_ref[pair] * fade + jnp.dot(
                values, weights.astype(jnp.bfloat16), preferred_element_type=jnp.float32
            )
        return carry

    lax.fori_loop(first // TOKENS, block + 1, step, 0)
    for pair in range(HEADS_HERE // 2):
        h = 2 * pair * HDIM
        mixed = (acc_ref[pair] / sum_ref[pair]).T.astype(jnp.bfloat16)
        out_ref[:, h : h + HDIM] = mixed[:TOKENS]
        out_ref[:, h + HDIM : h + 2 * HDIM] = mixed[TOKENS:]


def attend(offset, lengths, queries, kv):
    vmem = pl.BlockSpec(memory_space=pltpu.VMEM)
    return pl.pallas_call(
        functools.partial(attend_kernel, offset),
        out_shape=jax.ShapeDtypeStruct((TOKENS, WIDTH), jnp.bfloat16),
        in_specs=[pl.BlockSpec(memory_space=pltpu.SMEM), vmem, vmem],
        out_specs=vmem,
        scratch_shapes=[
            pltpu.VMEM((8, 1, 256), jnp.float32),
            pltpu.VMEM((8, 1, 256), jnp.float32),
            pltpu.VMEM((8, HDIM, 256), jnp.float32),
        ],
        compiler_params=pltpu.CompilerParams(vmem_limit_bytes=8 * 2**20),
        cost_estimate=pl.CostEstimate(
            flops=4 * 2**30, bytes_accessed=3 * 2**20, transcendentals=2048 * 640
        ),
        name="attend",
    )(lengths, queries, kv)


def project_kernel(count, *refs):
    att, own, other = refs[0:count], refs[count : count + 4], refs[count + 4 : count + 8]
    outs = refs[count + 8 :]
    x, core = lax.axis_index("dp"), lax.axis_index("pair")
    z = lax.rem(lax.axis_index("ctx"), 4)

    def run(stacks):
        for i in range(4):
            column = lax.rem(x + OFFSETS[i] + 4, 4) * 512
            total = None
            for half in range(2):
                for j in range(4):
                    place = lax.rem(z + OFFSETS[j] + 4, 4) * 512 + half * 256
                    place = pl.ds(pl.multiple_of(place, 256), 256)
                    left = jnp.concatenate([a[:, place] for a in att], axis=0)
                    right = stacks[0][j][i] if half == 0 else stacks[1][i][j]
                    term = jnp.dot(left, right, preferred_element_type=jnp.float32)
                    total = term if total is None else total + term
            total = total.astype(jnp.bfloat16)
            for n in range(count):
                part = total[n * TOKENS : (n + 1) * TOKENS]
                outs[n][:, pl.ds(pl.multiple_of(column, 512), 512)] = part

    @pl.when(core == 0)
    def _():
        run((own, other))

    @pl.when(core == 1)
    def _():
        run((other, own))


def project(attended, own, other):
    vmem = pl.BlockSpec(memory_space=pltpu.VMEM)
    count = len(attended)
    return pl.pallas_call(
        functools.partial(project_kernel, count),
        out_shape=[jax.ShapeDtypeStruct((TOKENS, WIDTH), jnp.bfloat16)] * count,
        in_specs=[vmem] * (count + 8),
        out_specs=[vmem] * count,
        compiler_params=pltpu.CompilerParams(vmem_limit_bytes=14 * 2**20),
        cost_estimate=pl.CostEstimate(
            flops=2 * count * TOKENS * 2048 * 2048,
            bytes_accessed=(8 + count) * 2**20,
            transcendentals=0,
        ),
        name="project",
    )(*attended, *own, *other)


def experts_kernel(count, *refs):
    pieces, refs = refs[:count], refs[count:]
    pick_ref, put_ref, weight_ref = refs[:3]
    hbm = refs[3:9]
    outs, refs = refs[9:-6], refs[-6:]
    if len(outs) == 1:
        outs = [outs[0].at[2 * p : 2 * p + 2] for p in range(count)]
    rows_ref, act_ref, gate_buf, up_buf, down_buf, sems = refs
    buffers = (gate_buf, up_buf, down_buf)

    def copies(e):
        side, index, slot = e // 2, e % 2, e % 2
        return [
            pltpu.make_async_copy(
                hbm[3 * side + w].at[index], buffers[w].at[slot], sems.at[w, slot]
            )
            for w in range(3)
        ]

    for e in range(2):
        for c in copies(e):
            c.start()
    for p in range(count):
        for n in range(4):
            cols = pl.ds(n * 512, 512)
            picked = jnp.dot(
                pick_ref[p],
                pieces[p][:, :, cols].reshape(256, 512),
                preferred_element_type=jnp.float32,
            )
            rows_ref[p, :, :, cols] = picked.astype(jnp.bfloat16).reshape(4, SLOTS, 512)
    for e in range(4):
        slot = e % 2
        waits = copies(e)
        waits[0].wait()
        waits[1].wait()
        rows = rows_ref[:, e].reshape(count * SLOTS, WIDTH)
        for n in range(3):
            cols = pl.ds(n * 256, 256)
            gate = jnp.dot(rows, gate_buf[slot, :, cols], preferred_element_type=jnp.float32)
            upward = jnp.dot(rows, up_buf[slot, :, cols], preferred_element_type=jnp.float32)
            act_ref[:, cols] = (gate / (1.0 + jnp.exp(-gate)) * upward).astype(jnp.bfloat16)
        waits[2].wait()
        active = act_ref[...]
        scale = weight_ref[e]
        for n in range(4):
            cols = pl.ds(n * 512, 512)
            result = jnp.dot(active, down_buf[slot, :, cols], preferred_element_type=jnp.float32)
            result = (result * scale).astype(jnp.bfloat16)
            rows_ref[:, e, :, cols] = result.reshape(count, SLOTS, 512)
        if e + 2 < 4:
            for c in copies(e + 2):
                c.start()
    for p in range(count):
        for n in range(4):
            cols = pl.ds(n * 512, 512)
            mixed = jnp.dot(
                put_ref[p],
                rows_ref[p, :, :, cols].reshape(4 * SLOTS, 512),
                preferred_element_type=jnp.float32,
            )
            mixed = mixed.astype(jnp.bfloat16).reshape(2, TOKENS, 512)
            outs[p][:, :, cols] = mixed


def experts(pieces, places, pick, put, weight, mine, others, joined=False):
    count = len(pieces)
    arrays = 1 if joined else count
    vmem = pl.BlockSpec(memory_space=pltpu.VMEM)
    hbm = pl.BlockSpec(memory_space=pltpu.HBM)
    rows = count * 4 * SLOTS
    return pl.pallas_call(
        functools.partial(experts_kernel, count),
        out_shape=[jax.ShapeDtypeStruct((2 * count // arrays, TOKENS, WIDTH), jnp.bfloat16)] * arrays,
        in_specs=[vmem] * (len(pieces) + 3) + [hbm] * 6,
        out_specs=[vmem] * arrays,
        scratch_shapes=[
            pltpu.VMEM((count, 4, SLOTS, WIDTH), jnp.bfloat16),
            pltpu.VMEM((count * SLOTS, FFE), jnp.bfloat16),
            pltpu.VMEM((2, WIDTH, FFE), jnp.bfloat16),
            pltpu.VMEM((2, WIDTH, FFE), jnp.bfloat16),
            pltpu.VMEM((2, FFE, WIDTH), jnp.bfloat16),
            pltpu.SemaphoreType.DMA((3, 2)),
        ],
        compiler_params=pltpu.CompilerParams(vmem_limit_bytes=44 * 2**20),
        cost_estimate=pl.CostEstimate(
            flops=6 * rows * 2048 * 768,
            bytes_accessed=(36 + 2 * count) * 2**20,
            transcendentals=rows * 768,
        ),
        name="experts",
    )(
        *pieces,
        jnp.stack([pick[p] for p in places]),
        jnp.stack([put[p] for p in places]),
        jnp.concatenate([weight[:, p * SLOTS : (p + 1) * SLOTS] for p in places], axis=1),
        *mine,
        *others,
    )


def routing(meta, y, z, core):
    meta = jnp.where(core == 0, meta, meta.transpose(1, 0, 2, 3)).astype(jnp.float32)
    meta = meta.reshape(8, 2, 32, TOKENS).transpose(0, 2, 1, 3).reshape(8, 32, 2 * TOKENS)
    ids = meta[:, :8]
    route = meta[:, 8:16] + meta[:, 16:24] + meta[:, 24:32]
    chip = (y * 4 + z) * 4
    wanted = chip + jnp.stack([core * 2, core * 2 + 1, 2 - core * 2, 3 - core * 2])
    same = ids[:, None] == wanted.astype(jnp.float32)[None, :, None, None]
    chosen = jnp.any(same, axis=2)
    share = jnp.sum(jnp.where(same, route[:, None], 0.0), axis=2)
    places = jnp.arange(2 * TOKENS, dtype=jnp.int32)
    before = (places[:, None] < places[None, :]).astype(jnp.bfloat16)
    rank = jnp.einsum(
        "pet,tu->peu", chosen.astype(jnp.bfloat16), before, preferred_element_type=jnp.float32
    )
    slots = jnp.arange(SLOTS, dtype=jnp.float32)
    pick = chosen[:, :, None] & (rank[:, :, None] == slots[None, None, :, None])
    weight = jnp.sum(jnp.where(pick, share[:, :, None], 0.0), axis=3)
    weight = weight.transpose(1, 0, 2).reshape(4, 8 * SLOTS, 1)
    pick = pick.astype(jnp.bfloat16).reshape(8, 4 * SLOTS, 2 * TOKENS)
    return pick, pick.transpose(0, 2, 1), weight


def after(value, *others):
    return lax.optimization_barrier((value, *others))[0]


def body(
    queries,
    keys,
    values,
    residual,
    doc_lengths,
    expert_ids,
    route_weights,
    out_weight,
    norm_gain,
    expert_gate,
    expert_up,
    expert_down,
):
    f32 = jnp.float32
    x, core = lax.axis_index("dp"), lax.axis_index("pair")
    y, z = lax.axis_index("ctx") // 4, lax.axis_index("ctx") % 4
    yy, zz = ("y", "y"), ("z", "z")
    queries, keys, values = queries[0], keys[0], values[0]

    route = route_weights[0].T
    high = lax.reduce_precision(route, 8, 7)
    middle = lax.reduce_precision(route - high, 8, 7)
    low = route - high - middle
    meta = jnp.concatenate([expert_ids[0].T.astype(f32), high, middle, low])
    meta = meta.astype(jnp.bfloat16)
    meta = jnp.concatenate([meta[:16], meta[16:]], axis=1)

    def kv_of(head):
        pair = jnp.concatenate(
            [
                lax.dynamic_slice_in_dim(keys, head * HDIM, HDIM, 1),
                lax.dynamic_slice_in_dim(values, head * HDIM, HDIM, 1),
            ],
            axis=1,
        )
        return jnp.concatenate([pair, meta])

    kv_y = [kv_of(y)] + [shift(kv_of((y - o + 4) % 4), yy, -o) for o in OFFSETS[1:]]
    column = jnp.stack(kv_y)
    kv_z = [column] + [shift(column, zz, -o) for o in OFFSETS[1:]]
    kv = jnp.concatenate(kv_z)

    part = lax.dynamic_slice_in_dim(out_weight, core * 256, 256, 0)
    inner = jnp.stack([part] + [shift(part, ("x", "z"), -o) for o in OFFSETS[1:]])
    own = [inner] + [shift(inner, ("z", "x"), -o) for o in OFFSETS[1:3]]
    own.append(shift(after(inner, kv_z[1], kv_z[2]), ("z", "x"), -OFFSETS[3]))

    def queries_of(group):
        return lax.dynamic_slice_in_dim(queries, group * WIDTH, WIDTH, 1)

    blocks = [queries_of(y), None, None, shift(queries_of((y + 2) % 4), yy, -2)]
    for k in (1, 2):
        o = OFFSETS[k]
        near = after(queries_of((y - o + 4) % 4), blocks[3], kv)
        blocks[k] = shift(near, yy, -o)

    meta = kv[:, TOKENS:]
    meta = jnp.concatenate([meta[:, :, :TOKENS], meta[:, :, TOKENS:]], axis=1)
    pick, put, weight = routing(meta.reshape(4, 4, 32, TOKENS), y, z, core)

    def attended(k):
        return attend(OFFSETS[k], doc_lengths, blocks[k], kv)

    last = blocks[2]
    blocks[2] = after(last, *own)
    mixed = [attended(k) for k in range(4)]
    other = [swap(after(w, mixed[0], mixed[3], mixed[1], last)) for w in own]

    far, below, above, here = project([mixed[3], mixed[1], mixed[2], mixed[0]], own, other)

    weights = [expert_gate, expert_up, expert_down]
    swapped = [swap(after(expert_gate, far)), swap(after(expert_up, far))]

    terms = [here, shift(below, yy, -1), shift(above, yy, 1), shift(far, yy, 2)]
    hidden = residual[0].astype(f32) + sum(t.astype(f32) for t in terms)
    mean_square = jnp.mean(hidden * hidden, axis=-1, keepdims=True)
    normed = (hidden * lax.rsqrt(mean_square + EPSILON) * norm_gain).astype(jnp.bfloat16)
    normed = after(normed, pick, put, weight, *swapped)
    swapped.append(swap(after(expert_down, normed)))

    prim, sec = ("y", "z"), ("z", "y")
    got = [normed] + [shift(normed, prim, -o) for o in OFFSETS[1:]]
    low, high = jnp.stack(got[:2]), jnp.stack(got[2:])
    low_below, high_above = shift(low, sec, 1), shift(high, sec, -1)
    high_below, low_above = shift(high, sec, 1), shift(low, sec, -1)
    low_far, high_far = shift(low_below, sec, 1), shift(high_above, sec, -1)
    rest = (pick, put, weight, weights, swapped)
    low_below, high_above = experts([low_below, high_above], (2, 5), *rest)
    high_below, low_above = after((high_below, low_above), low_below)
    high_below, low_above = experts([high_below, low_above], (3, 4), *rest)
    low_far, high_far = after((low_far, high_far), high_below)
    (far,) = experts([low_far, high_far], (6, 7), *rest, joined=True)
    low, high = after((low, high), far)
    low, high = experts([low, high], (0, 1), *rest)

    def add(*values):
        return lax.optimization_barrier(sum(value.astype(f32) for value in values))

    low_below, high_above = shift(low_below, sec, -1), shift(high_above, sec, 1)
    high_below, low_above = shift(high_below, sec, -1), shift(low_above, sec, 1)
    low = add(low, low_below, low_above)
    high = add(high, high_below, high_above)
    far = shift(far, sec, 2)
    low, high = low + far[:2].astype(f32), high + far[2:].astype(f32)
    back = [low[1], high[0], high[1]]
    total = hidden + low[0]
    for k in range(3):
        total = total + shift(back[k].astype(jnp.bfloat16), prim, OFFSETS[k + 1]).astype(f32)
    return total.astype(jnp.bfloat16)[None]


def solution(mesh):
    return jax.shard_map(
        body,
        mesh=mesh,
        in_specs=(
            P(("dp", "pair"), "ctx", None),
            P(("dp", "pair"), "ctx", None),
            P(("dp", "pair"), "ctx", None),
            P(("dp", "pair"), "ctx", None),
            P(("dp", "pair"), None),
            P(("dp", "pair"), "ctx", None),
            P(("dp", "pair"), "ctx", None),
            P("ctx", "dp"),
            P(),
            P(("ctx", "pair"), None, None),
            P(("ctx", "pair"), None, None),
            P(("ctx", "pair"), None, None),
        ),
        out_specs=P(("dp", "pair"), "ctx", None),
        check_vma=False,
    )
```

```python
import functools
import math

import jax
import jax.numpy as jnp
from jax import lax
from jax.experimental import pallas as pl
from jax.experimental.pallas import tpu as pltpu
from jax.sharding import PartitionSpec as P

RING = 4
TOKENS = 128
WIDTH = 2048
HDIM = 128
HEADS_HERE = 16
FFE = 768
SLOTS = 48
EPSILON = 1e-06
NEGATIVE = -1e30
OFFSETS = (0, -1, 1, 2)
AXES = ("dp", "ctx", "pair")


def shift(value, axes, distance):
    pairs = []
    for x in range(RING):
        for y in range(RING):
            for z in range(RING):
                for core in range(2):
                    to = {"x": x, "y": y, "z": z}
                    to[axes[core]] = (to[axes[core]] + distance) % RING
                    pairs.append(
                        (
                            (x * 16 + y * 4 + z) * 2 + core,
                            (to["x"] * 16 + to["y"] * 4 + to["z"]) * 2 + core,
                        )
                    )
    return lax.ppermute(value, AXES, pairs)


def swap(value):
    return lax.ppermute(value, "pair", [(0, 1), (1, 0)])


def ring_slot(distance):
    distance = lax.rem(distance + 4, 4)
    return jnp.where(distance == 3, 1, jnp.where(distance == 0, 0, distance + 1))


def attend_kernel(offset, lengths, q_ref, kv_ref, out_ref, top_ref, sum_ref, acc_ref):
    place = lax.axis_index("ctx")
    y, z = place // 4, lax.rem(place, 4)
    block = lax.rem(y + offset + 4, 4) * 4 + z
    scale = math.log2(math.e) / math.sqrt(HDIM)
    places = block * TOKENS + lax.broadcasted_iota(jnp.int32, (1, TOKENS), 1)
    starts = jnp.zeros((1, TOKENS), jnp.int32)
    first = jnp.int32(0)
    end = jnp.int32(0)
    for d in range(8):
        end = end + lengths[0, d]
        starts = jnp.maximum(starts, jnp.where(places >= end, end, 0))
        first = jnp.maximum(first, jnp.where(block * TOKENS >= end, end, 0))
    top_ref[...] = jnp.full_like(top_ref, NEGATIVE)
    sum_ref[...] = jnp.zeros_like(sum_ref)
    acc_ref[...] = jnp.zeros_like(acc_ref)
    rows = lax.broadcasted_iota(jnp.int32, (TOKENS, TOKENS), 0)

    def step(chunk, carry):
        slot = ring_slot(lax.rem(chunk, 4) - z) * 4 + ring_slot(chunk // 4 - y)
        keys = kv_ref[slot, :TOKENS, :HDIM]
        values = kv_ref[slot, :TOKENS, HDIM:].T
        key_places = chunk * TOKENS + rows
        allowed = (key_places <= places) & (key_places >= starts)
        bias = jnp.where(allowed, 0.0, NEGATIVE).astype(jnp.float32)
        bias = jnp.concatenate([bias, bias], axis=1)
        for pair in range(HEADS_HERE // 2):
            h = 2 * pair * HDIM
            q = jnp.concatenate([q_ref[:, h : h + HDIM], q_ref[:, h + HDIM : h + 2 * HDIM]], axis=0)
            s = lax.dot_general(
                keys, q, (((1,), (1,)), ((), ())), preferred_element_type=jnp.float32
            )
            s = s * scale + bias
            old = top_ref[pair]
            top = jnp.maximum(old, jnp.max(s, axis=0, keepdims=True))
            weights = jnp.exp2(s - top)
            fade = jnp.exp2(old - top)
            top_ref[pair] = top
            sum_ref[pair] = sum_ref[pair] * fade + jnp.sum(weights, axis=0, keepdims=True)
            acc_ref[pair] = acc_ref[pair] * fade + jnp.dot(
                values, weights.astype(jnp.bfloat16), preferred_element_type=jnp.float32
            )
        return carry

    lax.fori_loop(first // TOKENS, block + 1, step, 0)
    for pair in range(HEADS_HERE // 2):
        h = 2 * pair * HDIM
        mixed = (acc_ref[pair] / sum_ref[pair]).T.astype(jnp.bfloat16)
        out_ref[:, h : h + HDIM] = mixed[:TOKENS]
        out_ref[:, h + HDIM : h + 2 * HDIM] = mixed[TOKENS:]


def attend(offset, lengths, queries, kv):
    vmem = pl.BlockSpec(memory_space=pltpu.VMEM)
    return pl.pallas_call(
        functools.partial(attend_kernel, offset),
        out_shape=jax.ShapeDtypeStruct((TOKENS, WIDTH), jnp.bfloat16),
        in_specs=[pl.BlockSpec(memory_space=pltpu.SMEM), vmem, vmem],
        out_specs=vmem,
        scratch_shapes=[
            pltpu.VMEM((8, 1, 256), jnp.float32),
            pltpu.VMEM((8, 1, 256), jnp.float32),
            pltpu.VMEM((8, HDIM, 256), jnp.float32),
        ],
        compiler_params=pltpu.CompilerParams(vmem_limit_bytes=8 * 2**20),
        cost_estimate=pl.CostEstimate(
            flops=4 * 2**30, bytes_accessed=3 * 2**20, transcendentals=2048 * 640
        ),
        name="attend",
    )(lengths, queries, kv)


def project_kernel(count, *refs):
    att, own, other = refs[0:count], refs[count : count + 4], refs[count + 4 : count + 8]
    outs = refs[count + 8 :]
    x, core = lax.axis_index("dp"), lax.axis_index("pair")
    z = lax.rem(lax.axis_index("ctx"), 4)

    def run(stacks):
        for i in range(4):
            column = lax.rem(x + OFFSETS[i] + 4, 4) * 512
            total = None
            for half in range(2):
                for j in range(4):
                    place = lax.rem(z + OFFSETS[j] + 4, 4) * 512 + half * 256
                    place = pl.ds(pl.multiple_of(place, 256), 256)
                    left = jnp.concatenate([a[:, place] for a in att], axis=0)
                    right = stacks[0][j][i] if half == 0 else stacks[1][i][j]
                    term = jnp.dot(left, right, preferred_element_type=jnp.float32)
                    total = term if total is None else total + term
            total = total.astype(jnp.bfloat16)
            for n in range(count):
                part = total[n * TOKENS : (n + 1) * TOKENS]
                outs[n][:, pl.ds(pl.multiple_of(column, 512), 512)] = part

    @pl.when(core == 0)
    def _():
        run((own, other))

    @pl.when(core == 1)
    def _():
        run((other, own))


def project(attended, own, other):
    vmem = pl.BlockSpec(memory_space=pltpu.VMEM)
    count = len(attended)
    return pl.pallas_call(
        functools.partial(project_kernel, count),
        out_shape=[jax.ShapeDtypeStruct((TOKENS, WIDTH), jnp.bfloat16)] * count,
        in_specs=[vmem] * (count + 8),
        out_specs=[vmem] * count,
        compiler_params=pltpu.CompilerParams(vmem_limit_bytes=14 * 2**20),
        cost_estimate=pl.CostEstimate(
            flops=2 * count * TOKENS * 2048 * 2048,
            bytes_accessed=(8 + count) * 2**20,
            transcendentals=0,
        ),
        name="project",
    )(*attended, *own, *other)


def experts_kernel(count, *refs):
    pieces, refs = refs[:count], refs[count:]
    pick_ref, put_ref, weight_ref = refs[:3]
    hbm = refs[3:9]
    outs, refs = refs[9:-6], refs[-6:]
    outs = [out.at[b : b + 2] for out in outs for b in (0, 2)]
    rows_ref, act_ref, gate_buf, up_buf, down_buf, sems = refs
    buffers = (gate_buf, up_buf, down_buf)

    def copies(e):
        side, index, slot = e // 2, e % 2, e % 2
        return [
            pltpu.make_async_copy(
                hbm[3 * side + w].at[index], buffers[w].at[slot], sems.at[w, slot]
            )
            for w in range(3)
        ]

    for e in range(2):
        for c in copies(e):
            c.start()
    for p in range(count):
        for n in range(4):
            cols = pl.ds(n * 512, 512)
            picked = jnp.dot(
                pick_ref[p],
                pieces[p][:, :, cols].reshape(256, 512),
                preferred_element_type=jnp.float32,
            )
            rows_ref[p, :, :, cols] = picked.astype(jnp.bfloat16).reshape(4, SLOTS, 512)
    for e in range(4):
        slot = e % 2
        waits = copies(e)
        waits[0].wait()
        waits[1].wait()
        rows = rows_ref[:, e].reshape(count * SLOTS, WIDTH)
        for n in range(3):
            cols = pl.ds(n * 256, 256)
            gate = jnp.dot(rows, gate_buf[slot, :, cols], preferred_element_type=jnp.float32)
            upward = jnp.dot(rows, up_buf[slot, :, cols], preferred_element_type=jnp.float32)
            act_ref[:, cols] = (gate / (1.0 + jnp.exp(-gate)) * upward).astype(jnp.bfloat16)
        waits[2].wait()
        active = act_ref[...]
        scale = weight_ref[e]
        for n in range(4):
            cols = pl.ds(n * 512, 512)
            result = jnp.dot(active, down_buf[slot, :, cols], preferred_element_type=jnp.float32)
            result = (result * scale).astype(jnp.bfloat16)
            rows_ref[:, e, :, cols] = result.reshape(count, SLOTS, 512)
        if e + 2 < 4:
            for c in copies(e + 2):
                c.start()
    for p in range(count):
        for n in range(4):
            cols = pl.ds(n * 512, 512)
            mixed = jnp.dot(
                put_ref[p],
                rows_ref[p, :, :, cols].reshape(4 * SLOTS, 512),
                preferred_element_type=jnp.float32,
            )
            mixed = mixed.astype(jnp.bfloat16).reshape(2, TOKENS, 512)
            outs[p][:, :, cols] = mixed


def experts(pieces, first, pick, put, weight, mine, others):
    count = len(pieces)
    vmem = pl.BlockSpec(memory_space=pltpu.VMEM)
    hbm = pl.BlockSpec(memory_space=pltpu.HBM)
    rows = count * 4 * SLOTS
    return pl.pallas_call(
        functools.partial(experts_kernel, count),
        out_shape=[jax.ShapeDtypeStruct((4, TOKENS, WIDTH), jnp.bfloat16)] * (count // 2),
        in_specs=[vmem] * (len(pieces) + 3) + [hbm] * 6,
        out_specs=[vmem] * (count // 2),
        scratch_shapes=[
            pltpu.VMEM((count, 4, SLOTS, WIDTH), jnp.bfloat16),
            pltpu.VMEM((count * SLOTS, FFE), jnp.bfloat16),
            pltpu.VMEM((2, WIDTH, FFE), jnp.bfloat16),
            pltpu.VMEM((2, WIDTH, FFE), jnp.bfloat16),
            pltpu.VMEM((2, FFE, WIDTH), jnp.bfloat16),
            pltpu.SemaphoreType.DMA((3, 2)),
        ],
        compiler_params=pltpu.CompilerParams(vmem_limit_bytes=40 * 2**20),
        cost_estimate=pl.CostEstimate(
            flops=6 * rows * 2048 * 768,
            bytes_accessed=(36 + 2 * count) * 2**20,
            transcendentals=rows * 768,
        ),
        name="experts",
    )(
        *pieces,
        pick[first : first + count],
        put[first : first + count],
        weight[:, first * SLOTS : (first + count) * SLOTS],
        *mine,
        *others,
    )


def routing(meta, y, z, core):
    meta = jnp.where(core == 0, meta, meta.transpose(1, 0, 2, 3)).astype(jnp.float32)
    meta = meta.reshape(8, 2, 32, TOKENS).transpose(0, 2, 1, 3).reshape(8, 32, 2 * TOKENS)
    ids = meta[:, :8]
    route = meta[:, 8:16] + meta[:, 16:24] + meta[:, 24:32]
    chip = (y * 4 + z) * 4
    wanted = chip + jnp.stack([core * 2, core * 2 + 1, 2 - core * 2, 3 - core * 2])
    same = ids[:, None] == wanted.astype(jnp.float32)[None, :, None, None]
    chosen = jnp.any(same, axis=2)
    share = jnp.sum(jnp.where(same, route[:, None], 0.0), axis=2)
    places = jnp.arange(2 * TOKENS, dtype=jnp.int32)
    before = (places[:, None] < places[None, :]).astype(jnp.bfloat16)
    rank = jnp.einsum(
        "pet,tu->peu", chosen.astype(jnp.bfloat16), before, preferred_element_type=jnp.float32
    )
    slots = jnp.arange(SLOTS, dtype=jnp.float32)
    pick = chosen[:, :, None] & (rank[:, :, None] == slots[None, None, :, None])
    weight = jnp.sum(jnp.where(pick, share[:, :, None], 0.0), axis=3)
    weight = weight.transpose(1, 0, 2).reshape(4, 8 * SLOTS, 1)
    pick = pick.astype(jnp.bfloat16).reshape(8, 4 * SLOTS, 2 * TOKENS)
    return pick, pick.transpose(0, 2, 1), weight


def after(value, *others):
    return lax.optimization_barrier((value, *others))[0]


def body(
    queries,
    keys,
    values,
    residual,
    doc_lengths,
    expert_ids,
    route_weights,
    out_weight,
    norm_gain,
    expert_gate,
    expert_up,
    expert_down,
):
    f32 = jnp.float32
    x, core = lax.axis_index("dp"), lax.axis_index("pair")
    y, z = lax.axis_index("ctx") // 4, lax.axis_index("ctx") % 4
    yy, zz = ("y", "y"), ("z", "z")
    queries, keys, values = queries[0], keys[0], values[0]

    route = route_weights[0].T
    high = lax.reduce_precision(route, 8, 7)
    middle = lax.reduce_precision(route - high, 8, 7)
    low = route - high - middle
    meta = jnp.concatenate([expert_ids[0].T.astype(f32), high, middle, low])
    meta = meta.astype(jnp.bfloat16)
    meta = jnp.concatenate([meta[:16], meta[16:]], axis=1)

    def kv_of(head):
        pair = jnp.concatenate(
            [
                lax.dynamic_slice_in_dim(keys, head * HDIM, HDIM, 1),
                lax.dynamic_slice_in_dim(values, head * HDIM, HDIM, 1),
            ],
            axis=1,
        )
        return jnp.concatenate([pair, meta])

    kv_y = [kv_of(y)] + [shift(kv_of((y - o + 4) % 4), yy, -o) for o in OFFSETS[1:]]
    column = jnp.stack(kv_y)
    kv_z = [column] + [shift(column, zz, -o) for o in OFFSETS[1:]]
    kv = jnp.concatenate(kv_z)

    part = lax.dynamic_slice_in_dim(out_weight, core * 256, 256, 0)
    inner = jnp.stack([part] + [shift(part, ("x", "z"), -o) for o in OFFSETS[1:]])
    own = [inner] + [shift(inner, ("z", "x"), -o) for o in OFFSETS[1:3]]
    own.append(shift(after(inner, kv_z[1], kv_z[2]), ("z", "x"), -OFFSETS[3]))

    def queries_of(group):
        return lax.dynamic_slice_in_dim(queries, group * WIDTH, WIDTH, 1)

    blocks = [queries_of(y), None, None, shift(queries_of((y + 2) % 4), yy, -2)]
    for k in (1, 2):
        o = OFFSETS[k]
        near = after(queries_of((y - o + 4) % 4), blocks[3], kv)
        blocks[k] = shift(near, yy, -o)

    meta = kv[:, TOKENS:]
    meta = jnp.concatenate([meta[:, :, :TOKENS], meta[:, :, TOKENS:]], axis=1)
    pick, put, weight = routing(meta.reshape(4, 4, 32, TOKENS), y, z, core)

    def attended(k):
        return attend(OFFSETS[k], doc_lengths, blocks[k], kv)

    last = blocks[2]
    blocks[2] = after(last, *own)
    mixed = [attended(k) for k in range(4)]
    other = [swap(after(w, mixed[0], mixed[3], mixed[1], last)) for w in own]

    far, below, above, here = project([mixed[3], mixed[1], mixed[2], mixed[0]], own, other)

    weights = [expert_gate, expert_up, expert_down]
    swapped = [swap(after(expert_gate, far)), swap(after(expert_up, far))]

    terms = [here, shift(below, yy, -1), shift(above, yy, 1), shift(far, yy, 2)]
    hidden = residual[0].astype(f32) + sum(t.astype(f32) for t in terms)
    mean_square = jnp.mean(hidden * hidden, axis=-1, keepdims=True)
    normed = (hidden * lax.rsqrt(mean_square + EPSILON) * norm_gain).astype(jnp.bfloat16)
    normed = after(normed, pick, put, weight, *swapped)
    swapped.append(swap(after(expert_down, normed)))

    prim, sec = ("y", "z"), ("z", "y")
    got = [normed] + [shift(normed, prim, -o) for o in OFFSETS[1:]]
    low, high = jnp.stack(got[:2]), jnp.stack(got[2:])
    low_below, high_above = shift(low, sec, 1), shift(high, sec, -1)
    high_below, low_above = shift(high, sec, 1), shift(low, sec, -1)
    rest = (pick, put, weight, weights, swapped)
    (here,) = experts([low, high], 0, *rest)
    low_far = shift(after(low_below, here), sec, 1)
    high_far = shift(after(high_above, here), sec, -1)
    below, above = experts([low_below, high_below, low_above, high_above], 2, *rest)
    (far,) = experts(list(after((low_far, high_far), below)), 6, *rest)

    near = [here, shift(below, sec, -1), shift(above, sec, 1)]
    near = lax.optimization_barrier(sum(part.astype(f32) for part in near))
    total = near + shift(far, sec, 2).astype(f32)
    back = total[1:].astype(jnp.bfloat16)
    total = hidden + total[0]
    for k in range(3):
        total = total + shift(back[k], prim, OFFSETS[k + 1]).astype(f32)
    return total.astype(jnp.bfloat16)[None]


def solution(mesh):
    return jax.shard_map(
        body,
        mesh=mesh,
        in_specs=(
            P(("dp", "pair"), "ctx", None),
            P(("dp", "pair"), "ctx", None),
            P(("dp", "pair"), "ctx", None),
            P(("dp", "pair"), "ctx", None),
            P(("dp", "pair"), None),
            P(("dp", "pair"), "ctx", None),
            P(("dp", "pair"), "ctx", None),
            P("ctx", "dp"),
            P(),
            P(("ctx", "pair"), None, None),
            P(("ctx", "pair"), None, None),
            P(("ctx", "pair"), None, None),
        ),
        out_specs=P(("dp", "pair"), "ctx", None),
        check_vma=False,
    )
```

```python
import functools
import math

import jax
import jax.numpy as jnp
from jax import lax
from jax.experimental import pallas as pl
from jax.experimental.pallas import tpu as pltpu
from jax.sharding import PartitionSpec as P

RING = 4
TOKENS = 128
WIDTH = 2048
HDIM = 128
HEADS_HERE = 16
FFE = 768
SLOTS = 48
EPSILON = 1e-06
NEGATIVE = -1e30
OFFSETS = (0, -1, 1, 2)
AXES = ("dp", "ctx", "pair")


def shift(value, axes, distance):
    pairs = []
    for x in range(RING):
        for y in range(RING):
            for z in range(RING):
                for core in range(2):
                    to = {"x": x, "y": y, "z": z}
                    to[axes[core]] = (to[axes[core]] + distance) % RING
                    pairs.append(
                        (
                            (x * 16 + y * 4 + z) * 2 + core,
                            (to["x"] * 16 + to["y"] * 4 + to["z"]) * 2 + core,
                        )
                    )
    return lax.ppermute(value, AXES, pairs)


def swap(value):
    return lax.ppermute(value, "pair", [(0, 1), (1, 0)])


def ring_slot(distance):
    distance = lax.rem(distance + 4, 4)
    return jnp.where(distance == 3, 1, jnp.where(distance == 0, 0, distance + 1))


def attend_kernel(offset, lengths, q_ref, kv_ref, out_ref, top_ref, sum_ref, acc_ref):
    place = lax.axis_index("ctx")
    y, z = place // 4, lax.rem(place, 4)
    block = lax.rem(y + offset + 4, 4) * 4 + z
    scale = math.log2(math.e) / math.sqrt(HDIM)
    places = block * TOKENS + lax.broadcasted_iota(jnp.int32, (1, TOKENS), 1)
    starts = jnp.zeros((1, TOKENS), jnp.int32)
    first = jnp.int32(0)
    end = jnp.int32(0)
    for d in range(8):
        end = end + lengths[0, d]
        starts = jnp.maximum(starts, jnp.where(places >= end, end, 0))
        first = jnp.maximum(first, jnp.where(block * TOKENS >= end, end, 0))
    top_ref[...] = jnp.full_like(top_ref, NEGATIVE)
    sum_ref[...] = jnp.zeros_like(sum_ref)
    acc_ref[...] = jnp.zeros_like(acc_ref)
    rows = lax.broadcasted_iota(jnp.int32, (TOKENS, TOKENS), 0)

    def step(chunk, carry):
        slot = ring_slot(lax.rem(chunk, 4) - z) * 4 + ring_slot(chunk // 4 - y)
        keys = kv_ref[slot, :TOKENS, :HDIM]
        values = kv_ref[slot, :TOKENS, HDIM:].T
        key_places = chunk * TOKENS + rows
        allowed = (key_places <= places) & (key_places >= starts)
        bias = jnp.where(allowed, 0.0, NEGATIVE).astype(jnp.float32)
        bias = jnp.concatenate([bias, bias], axis=1)
        for pair in range(HEADS_HERE // 2):
            h = 2 * pair * HDIM
            q = jnp.concatenate([q_ref[:, h : h + HDIM], q_ref[:, h + HDIM : h + 2 * HDIM]], axis=0)
            s = lax.dot_general(
                keys, q, (((1,), (1,)), ((), ())), preferred_element_type=jnp.float32
            )
            s = s * scale + bias
            old = top_ref[pair]
            top = jnp.maximum(old, jnp.max(s, axis=0, keepdims=True))
            weights = jnp.exp2(s - top)
            fade = jnp.exp2(old - top)
            top_ref[pair] = top
            sum_ref[pair] = sum_ref[pair] * fade + jnp.sum(weights, axis=0, keepdims=True)
            acc_ref[pair] = acc_ref[pair] * fade + jnp.dot(
                values, weights.astype(jnp.bfloat16), preferred_element_type=jnp.float32
            )
        return carry

    lax.fori_loop(first // TOKENS, block + 1, step, 0)
    for pair in range(HEADS_HERE // 2):
        h = 2 * pair * HDIM
        mixed = (acc_ref[pair] / sum_ref[pair]).T.astype(jnp.bfloat16)
        out_ref[:, h : h + HDIM] = mixed[:TOKENS]
        out_ref[:, h + HDIM : h + 2 * HDIM] = mixed[TOKENS:]


def attend(offset, lengths, queries, kv):
    vmem = pl.BlockSpec(memory_space=pltpu.VMEM)
    return pl.pallas_call(
        functools.partial(attend_kernel, offset),
        out_shape=jax.ShapeDtypeStruct((TOKENS, WIDTH), jnp.bfloat16),
        in_specs=[pl.BlockSpec(memory_space=pltpu.SMEM), vmem, vmem],
        out_specs=vmem,
        scratch_shapes=[
            pltpu.VMEM((8, 1, 256), jnp.float32),
            pltpu.VMEM((8, 1, 256), jnp.float32),
            pltpu.VMEM((8, HDIM, 256), jnp.float32),
        ],
        compiler_params=pltpu.CompilerParams(vmem_limit_bytes=8 * 2**20),
        cost_estimate=pl.CostEstimate(
            flops=4 * 2**30, bytes_accessed=3 * 2**20, transcendentals=2048 * 640
        ),
        name="attend",
    )(lengths, queries, kv)


def project_kernel(count, *refs):
    att, own, other = refs[0:count], refs[count : count + 4], refs[count + 4 : count + 8]
    outs = refs[count + 8 :]
    x, core = lax.axis_index("dp"), lax.axis_index("pair")
    z = lax.rem(lax.axis_index("ctx"), 4)

    def run(stacks):
        for i in range(4):
            column = lax.rem(x + OFFSETS[i] + 4, 4) * 512
            total = None
            for half in range(2):
                for j in range(4):
                    place = lax.rem(z + OFFSETS[j] + 4, 4) * 512 + half * 256
                    place = pl.ds(pl.multiple_of(place, 256), 256)
                    left = jnp.concatenate([a[:, place] for a in att], axis=0)
                    right = stacks[0][j][i] if half == 0 else stacks[1][i][j]
                    term = jnp.dot(left, right, preferred_element_type=jnp.float32)
                    total = term if total is None else total + term
            total = total.astype(jnp.bfloat16)
            for n in range(count):
                part = total[n * TOKENS : (n + 1) * TOKENS]
                outs[n][:, pl.ds(pl.multiple_of(column, 512), 512)] = part

    @pl.when(core == 0)
    def _():
        run((own, other))

    @pl.when(core == 1)
    def _():
        run((other, own))


def project(attended, own, other):
    vmem = pl.BlockSpec(memory_space=pltpu.VMEM)
    count = len(attended)
    return pl.pallas_call(
        functools.partial(project_kernel, count),
        out_shape=[jax.ShapeDtypeStruct((TOKENS, WIDTH), jnp.bfloat16)] * count,
        in_specs=[vmem] * (count + 8),
        out_specs=[vmem] * count,
        compiler_params=pltpu.CompilerParams(vmem_limit_bytes=14 * 2**20),
        cost_estimate=pl.CostEstimate(
            flops=2 * count * TOKENS * 2048 * 2048,
            bytes_accessed=(8 + count) * 2**20,
            transcendentals=0,
        ),
        name="project",
    )(*attended, *own, *other)


def pieces_of(blocks, cols):
    return [
        jnp.concatenate([blocks[2 * p][:, cols], blocks[2 * p + 1][:, cols]], axis=0)
        for p in range(2)
    ]


def dispatch_kernel(*refs):
    blocks, pick_ref, outs = refs[:4], refs[4], refs[5:]
    for n in range(4):
        cols = pl.ds(n * 512, 512)
        pieces = pieces_of(blocks, cols)
        for chip, out in enumerate(outs):
            for p in range(2):
                rows = jnp.dot(pick_ref[chip, p], pieces[p], preferred_element_type=jnp.float32)
                rows = rows.astype(jnp.bfloat16).reshape(4, SLOTS, 512)
                out[:, p * SLOTS : (p + 1) * SLOTS, cols] = rows


def dispatch(blocks, pick):
    vmem = pl.BlockSpec(memory_space=pltpu.VMEM)
    chips = pick.shape[0]
    return pl.pallas_call(
        dispatch_kernel,
        out_shape=[jax.ShapeDtypeStruct((4, 2 * SLOTS, WIDTH), jnp.bfloat16)] * chips,
        in_specs=[vmem] * 5,
        out_specs=[vmem] * chips,
        compiler_params=pltpu.CompilerParams(vmem_limit_bytes=12 * 2**20),
        cost_estimate=pl.CostEstimate(
            flops=2 * chips * 384 * 256 * 2048, bytes_accessed=6 * 2**20, transcendentals=0
        ),
        name="dispatch",
    )(*blocks, pick)


def combine_kernel(chips, last, *refs):
    sources, put_ref, refs = refs[:chips], refs[chips], refs[chips + 1 :]
    for n in range(4):
        cols = pl.ds(n * 512, 512)
        for p in range(2):
            rows = [
                source[e, p * SLOTS : (p + 1) * SLOTS, cols] for source in sources for e in range(4)
            ]
            mixed = jnp.dot(
                put_ref[p], jnp.concatenate(rows, axis=0), preferred_element_type=jnp.float32
            )
            for half in range(2):
                part = mixed[half * TOKENS : (half + 1) * TOKENS]
                if not last:
                    refs[0][2 * p + half, :, cols] = part
                    continue
                part = part + refs[0][2 * p + half, :, cols]
                out = refs[1 + 2 * p + half]
                out[:, cols] = part.astype(out.dtype)


def combine(sources, put, earlier=None):
    vmem = pl.BlockSpec(memory_space=pltpu.VMEM)
    last = earlier is not None
    if last:
        shapes = [jax.ShapeDtypeStruct((TOKENS, WIDTH), jnp.float32)]
        shapes += [jax.ShapeDtypeStruct((TOKENS, WIDTH), jnp.bfloat16)] * 3
    else:
        shapes = [jax.ShapeDtypeStruct((4, TOKENS, WIDTH), jnp.float32)]
    operands = [*sources, put] + ([earlier] if last else [])
    return pl.pallas_call(
        functools.partial(combine_kernel, len(sources), last),
        out_shape=shapes,
        in_specs=[vmem] * len(operands),
        out_specs=[vmem] * len(shapes),
        compiler_params=pltpu.CompilerParams(vmem_limit_bytes=16 * 2**20),
        cost_estimate=pl.CostEstimate(
            flops=2 * len(sources) * 384 * 256 * 2048, bytes_accessed=8 * 2**20, transcendentals=0
        ),
        name="combine",
    )(*operands)


def experts_kernel(count, *refs):
    sources, refs = refs[:count], refs[count:]
    hbm, refs = refs[:6], refs[6:]
    outs, refs = refs[:count], refs[count:]
    act_ref, gate_buf, up_buf, down_buf, sems = refs
    buffers = (gate_buf, up_buf, down_buf)

    def copies(e):
        side, index, slot = e // 2, e % 2, e % 2
        return [
            pltpu.make_async_copy(
                hbm[3 * side + w].at[index], buffers[w].at[slot], sems.at[w, slot]
            )
            for w in range(3)
        ]

    for e in range(2):
        for c in copies(e):
            c.start()
    for e in range(4):
        slot = e % 2
        waits = copies(e)
        waits[0].wait()
        waits[1].wait()
        rows = jnp.concatenate([source[e] for source in sources], axis=0)
        for n in range(3):
            cols = pl.ds(n * 256, 256)
            gate = jnp.dot(rows, gate_buf[slot, :, cols], preferred_element_type=jnp.float32)
            upward = jnp.dot(rows, up_buf[slot, :, cols], preferred_element_type=jnp.float32)
            act_ref[:, cols] = (gate / (1.0 + jnp.exp(-gate)) * upward).astype(jnp.bfloat16)
        waits[2].wait()
        active = act_ref[...]
        for n in range(4):
            cols = pl.ds(n * 512, 512)
            result = jnp.dot(active, down_buf[slot, :, cols], preferred_element_type=jnp.float32)
            result = result.astype(jnp.bfloat16)
            for i, out in enumerate(outs):
                out[e, :, cols] = result[i * 2 * SLOTS : (i + 1) * 2 * SLOTS]
        if e + 2 < 4:
            for c in copies(e + 2):
                c.start()


def experts(sources, mine, others):
    count = len(sources)
    vmem = pl.BlockSpec(memory_space=pltpu.VMEM)
    hbm = pl.BlockSpec(memory_space=pltpu.HBM)
    rows = count * 4 * 2 * SLOTS
    return pl.pallas_call(
        functools.partial(experts_kernel, count),
        out_shape=[jax.ShapeDtypeStruct((4, 2 * SLOTS, WIDTH), jnp.bfloat16)] * count,
        in_specs=[vmem] * count + [hbm] * 6,
        out_specs=[vmem] * count,
        scratch_shapes=[
            pltpu.VMEM((count * 2 * SLOTS, FFE), jnp.bfloat16),
            pltpu.VMEM((2, WIDTH, FFE), jnp.bfloat16),
            pltpu.VMEM((2, WIDTH, FFE), jnp.bfloat16),
            pltpu.VMEM((2, FFE, WIDTH), jnp.bfloat16),
            pltpu.SemaphoreType.DMA((3, 2)),
        ],
        compiler_params=pltpu.CompilerParams(vmem_limit_bytes=40 * 2**20),
        cost_estimate=pl.CostEstimate(
            flops=6 * rows * 2048 * 768,
            bytes_accessed=(36 + 3 * count) * 2**20,
            transcendentals=rows * 768,
        ),
        name="experts",
    )(*sources, *mine, *others)


def routing(meta, y, z, core):
    meta = jnp.where(core == 0, meta[0], meta[:, 0]).astype(jnp.float32)
    meta = meta.reshape(2, 2, 32, TOKENS).transpose(0, 2, 1, 3).reshape(2, 32, 2 * TOKENS)
    ids = meta[:, :8]
    route = meta[:, 8:16] + meta[:, 16:24] + meta[:, 24:32]
    index = jnp.arange(16, dtype=jnp.int32)
    chip, expert = index // 4, index % 4
    across = jnp.where(chip == 3, 2, jnp.where(chip == 2, 1, -chip))
    on_y, on_z = jnp.where(core == 0, 0, across), jnp.where(core == 0, across, 0)
    chip = (y + on_y + 4) % 4 * 4 + (z + on_z + 4) % 4
    wanted = chip * 4 + (expert + 2 * core) % 4
    same = ids[:, None] == wanted.astype(jnp.float32)[None, :, None, None]
    chosen = jnp.any(same, axis=2)
    share = jnp.sum(jnp.where(same, route[:, None], 0.0), axis=2)
    places = jnp.arange(2 * TOKENS, dtype=jnp.int32)
    before = (places[:, None] < places[None, :]).astype(jnp.bfloat16)
    rank = jnp.einsum(
        "pet,tu->peu", chosen.astype(jnp.bfloat16), before, preferred_element_type=jnp.float32
    )
    rank = jnp.where(chosen, rank, -1.0)
    slots = jnp.arange(SLOTS, dtype=jnp.float32)
    pick = (rank[:, :, None] == slots[None, None, :, None]).astype(jnp.bfloat16)
    pick = pick.reshape(2, 4, 4 * SLOTS, 2 * TOKENS).transpose(1, 0, 2, 3)
    by_slot = lambda v: jnp.repeat(v.transpose(0, 2, 1), SLOTS, axis=2)
    slots = jnp.tile(slots, 16)
    put = jnp.where(by_slot(rank) == slots, by_slot(share), 0.0).astype(jnp.bfloat16)
    return pick, put


def after(value, *others):
    return lax.optimization_barrier((value, *others))[0]


def body(
    queries,
    keys,
    values,
    residual,
    doc_lengths,
    expert_ids,
    route_weights,
    out_weight,
    norm_gain,
    expert_gate,
    expert_up,
    expert_down,
):
    f32 = jnp.float32
    x, core = lax.axis_index("dp"), lax.axis_index("pair")
    y, z = lax.axis_index("ctx") // 4, lax.axis_index("ctx") % 4
    yy, zz = ("y", "y"), ("z", "z")
    queries, keys, values = queries[0], keys[0], values[0]

    route = route_weights[0].T
    high = lax.reduce_precision(route, 8, 7)
    middle = lax.reduce_precision(route - high, 8, 7)
    low = route - high - middle
    meta = jnp.concatenate([expert_ids[0].T.astype(f32), high, middle, low])
    meta = meta.astype(jnp.bfloat16)
    meta = jnp.concatenate([meta[:16], meta[16:]], axis=1)

    def kv_of(head):
        pair = jnp.concatenate(
            [
                lax.dynamic_slice_in_dim(keys, head * HDIM, HDIM, 1),
                lax.dynamic_slice_in_dim(values, head * HDIM, HDIM, 1),
            ],
            axis=1,
        )
        return jnp.concatenate([pair, meta])

    kv_y = [kv_of(y)] + [shift(kv_of((y - o + 4) % 4), yy, -o) for o in OFFSETS[1:]]
    column = jnp.stack(kv_y)
    kv_z = [column] + [shift(column, zz, -o) for o in OFFSETS[1:]]
    kv = jnp.concatenate(kv_z)

    part = lax.dynamic_slice_in_dim(out_weight, core * 256, 256, 0)
    inner = jnp.stack([part] + [shift(part, ("x", "z"), -o) for o in OFFSETS[1:]])
    own = [inner] + [shift(inner, ("z", "x"), -o) for o in OFFSETS[1:3]]
    own.append(shift(after(inner, kv_z[1], kv_z[2]), ("z", "x"), -OFFSETS[3]))

    def queries_of(group):
        return lax.dynamic_slice_in_dim(queries, group * WIDTH, WIDTH, 1)

    blocks = [queries_of(y), None, None, shift(queries_of((y + 2) % 4), yy, -2)]
    for k in (1, 2):
        o = OFFSETS[k]
        near = after(queries_of((y - o + 4) % 4), blocks[3], kv)
        blocks[k] = shift(near, yy, -o)

    meta = kv[:, TOKENS:]
    meta = jnp.concatenate([meta[:, :, :TOKENS], meta[:, :, TOKENS:]], axis=1)
    pick, put = routing(meta.reshape(4, 4, 32, TOKENS), y, z, core)

    def attended(k):
        return attend(OFFSETS[k], doc_lengths, blocks[k], kv)

    last = blocks[2]
    blocks[2] = after(last, *own)
    mixed = [attended(k) for k in range(4)]
    other = [swap(after(w, mixed[0], mixed[3], mixed[1], last)) for w in own]

    far, below, above, here = project([mixed[3], mixed[1], mixed[2], mixed[0]], own, other)

    weights = [expert_gate, expert_up, expert_down]
    swapped = [swap(after(expert_gate, far)), swap(after(expert_up, far))]

    terms = [here, shift(below, yy, -1), shift(above, yy, 1), shift(far, yy, 2)]
    hidden = residual[0].astype(f32) + sum(t.astype(f32) for t in terms)
    mean_square = jnp.mean(hidden * hidden, axis=-1, keepdims=True)
    normed = (hidden * lax.rsqrt(mean_square + EPSILON) * norm_gain).astype(jnp.bfloat16)
    normed = after(normed, pick, put, *swapped)
    swapped.append(swap(after(expert_down, normed)))

    prim, sec = ("y", "z"), ("z", "y")
    line = [normed] + [shift(normed, prim, -o) for o in OFFSETS[1:]]
    below, above = dispatch(line, pick[1:3])
    here, far = dispatch(line, jnp.stack([pick[0], pick[3]]))
    below, above = shift(below, sec, -1), shift(above, sec, 1)
    rest = (weights, swapped)
    (here,) = experts([here], *rest)
    far = shift(after(far, here), sec, 2)
    below, above = experts([below, above], *rest)
    (far,) = experts([after(far, below)], *rest)

    below, above = shift(below, sec, 1), shift(above, sec, -1)
    (near,) = combine([here, below, above], put[:, :, : 12 * SLOTS])
    parts = combine([shift(far, sec, 2)], put[:, :, 12 * SLOTS :], near)
    total = hidden + parts[0]
    for k in range(1, 4):
        total = total + shift(parts[k], prim, OFFSETS[k]).astype(f32)
    return total.astype(jnp.bfloat16)[None]


def solution(mesh):
    return jax.shard_map(
        body,
        mesh=mesh,
        in_specs=(
            P(("dp", "pair"), "ctx", None),
            P(("dp", "pair"), "ctx", None),
            P(("dp", "pair"), "ctx", None),
            P(("dp", "pair"), "ctx", None),
            P(("dp", "pair"), None),
            P(("dp", "pair"), "ctx", None),
            P(("dp", "pair"), "ctx", None),
            P("ctx", "dp"),
            P(),
            P(("ctx", "pair"), None, None),
            P(("ctx", "pair"), None, None),
            P(("ctx", "pair"), None, None),
        ),
        out_specs=P(("dp", "pair"), "ctx", None),
        check_vma=False,
    )
```

```python
import functools
import math

import jax
import jax.numpy as jnp
from jax import lax
from jax.experimental import pallas as pl
from jax.experimental.pallas import tpu as pltpu
from jax.sharding import PartitionSpec as P

RING = 4
TOKENS = 128
WIDTH = 2048
HDIM = 128
HEADS_HERE = 16
FFE = 768
SLOTS = 48
EPSILON = 1e-06
NEGATIVE = -1e30
OFFSETS = (0, -1, 1, 2)
AXES = ("dp", "ctx", "pair")


def shift(value, axes, distance):
    pairs = []
    for x in range(RING):
        for y in range(RING):
            for z in range(RING):
                for core in range(2):
                    to = {"x": x, "y": y, "z": z}
                    to[axes[core]] = (to[axes[core]] + distance) % RING
                    pairs.append(
                        (
                            (x * 16 + y * 4 + z) * 2 + core,
                            (to["x"] * 16 + to["y"] * 4 + to["z"]) * 2 + core,
                        )
                    )
    return lax.ppermute(value, AXES, pairs)


def swap(value):
    return lax.ppermute(value, "pair", [(0, 1), (1, 0)])


def ring_slot(distance):
    distance = lax.rem(distance + 4, 4)
    return jnp.where(distance == 3, 1, jnp.where(distance == 0, 0, distance + 1))


def attend_kernel(offset, lengths, q_ref, kv_ref, out_ref, top_ref, sum_ref, acc_ref):
    place = lax.axis_index("ctx")
    y, z = place // 4, lax.rem(place, 4)
    block = lax.rem(y + offset + 4, 4) * 4 + z
    scale = math.log2(math.e) / math.sqrt(HDIM)
    places = block * TOKENS + lax.broadcasted_iota(jnp.int32, (1, TOKENS), 1)
    starts = jnp.zeros((1, TOKENS), jnp.int32)
    first = jnp.int32(0)
    end = jnp.int32(0)
    for d in range(8):
        end = end + lengths[0, d]
        starts = jnp.maximum(starts, jnp.where(places >= end, end, 0))
        first = jnp.maximum(first, jnp.where(block * TOKENS >= end, end, 0))
    top_ref[...] = jnp.full_like(top_ref, NEGATIVE)
    sum_ref[...] = jnp.zeros_like(sum_ref)
    acc_ref[...] = jnp.zeros_like(acc_ref)
    rows = lax.broadcasted_iota(jnp.int32, (TOKENS, TOKENS), 0)

    def step(chunk, carry):
        slot = ring_slot(lax.rem(chunk, 4) - z) * 4 + ring_slot(chunk // 4 - y)
        keys = kv_ref[slot, :TOKENS, :HDIM]
        values = kv_ref[slot, :TOKENS, HDIM:].T
        key_places = chunk * TOKENS + rows
        allowed = (key_places <= places) & (key_places >= starts)
        bias = jnp.where(allowed, 0.0, NEGATIVE).astype(jnp.float32)
        bias = jnp.concatenate([bias, bias], axis=1)
        for pair in range(HEADS_HERE // 2):
            h = 2 * pair * HDIM
            q = jnp.concatenate([q_ref[:, h : h + HDIM], q_ref[:, h + HDIM : h + 2 * HDIM]], axis=0)
            s = lax.dot_general(
                keys, q, (((1,), (1,)), ((), ())), preferred_element_type=jnp.float32
            )
            s = s * scale + bias
            old = top_ref[pair]
            top = jnp.maximum(old, jnp.max(s, axis=0, keepdims=True))
            weights = jnp.exp2(s - top)
            fade = jnp.exp2(old - top)
            top_ref[pair] = top
            sum_ref[pair] = sum_ref[pair] * fade + jnp.sum(weights, axis=0, keepdims=True)
            acc_ref[pair] = acc_ref[pair] * fade + jnp.dot(
                values, weights.astype(jnp.bfloat16), preferred_element_type=jnp.float32
            )
        return carry

    lax.fori_loop(first // TOKENS, block + 1, step, 0)
    for pair in range(HEADS_HERE // 2):
        h = 2 * pair * HDIM
        mixed = (acc_ref[pair] / sum_ref[pair]).T.astype(jnp.bfloat16)
        out_ref[:, h : h + HDIM] = mixed[:TOKENS]
        out_ref[:, h + HDIM : h + 2 * HDIM] = mixed[TOKENS:]


def attend(offset, lengths, queries, kv):
    vmem = pl.BlockSpec(memory_space=pltpu.VMEM)
    return pl.pallas_call(
        functools.partial(attend_kernel, offset),
        out_shape=jax.ShapeDtypeStruct((TOKENS, WIDTH), jnp.bfloat16),
        in_specs=[pl.BlockSpec(memory_space=pltpu.SMEM), vmem, vmem],
        out_specs=vmem,
        scratch_shapes=[
            pltpu.VMEM((8, 1, 256), jnp.float32),
            pltpu.VMEM((8, 1, 256), jnp.float32),
            pltpu.VMEM((8, HDIM, 256), jnp.float32),
        ],
        compiler_params=pltpu.CompilerParams(vmem_limit_bytes=8 * 2**20),
        cost_estimate=pl.CostEstimate(
            flops=4 * 2**30, bytes_accessed=3 * 2**20, transcendentals=2048 * 640
        ),
        name="attend",
    )(lengths, queries, kv)


def project_kernel(count, *refs):
    att, own, other = refs[0:count], refs[count : count + 4], refs[count + 4 : count + 8]
    outs = refs[count + 8 :]
    x, core = lax.axis_index("dp"), lax.axis_index("pair")
    z = lax.rem(lax.axis_index("ctx"), 4)

    def run(stacks):
        for i in range(4):
            column = lax.rem(x + OFFSETS[i] + 4, 4) * 512
            total = None
            for half in range(2):
                for j in range(4):
                    place = lax.rem(z + OFFSETS[j] + 4, 4) * 512 + half * 256
                    place = pl.ds(pl.multiple_of(place, 256), 256)
                    left = jnp.concatenate([a[:, place] for a in att], axis=0)
                    right = stacks[0][j][i] if half == 0 else stacks[1][i][j]
                    term = jnp.dot(left, right, preferred_element_type=jnp.float32)
                    total = term if total is None else total + term
            total = total.astype(jnp.bfloat16)
            for n in range(count):
                part = total[n * TOKENS : (n + 1) * TOKENS]
                outs[n][:, pl.ds(pl.multiple_of(column, 512), 512)] = part

    @pl.when(core == 0)
    def _():
        run((own, other))

    @pl.when(core == 1)
    def _():
        run((other, own))


def project(attended, own, other):
    vmem = pl.BlockSpec(memory_space=pltpu.VMEM)
    count = len(attended)
    return pl.pallas_call(
        functools.partial(project_kernel, count),
        out_shape=[jax.ShapeDtypeStruct((TOKENS, WIDTH), jnp.bfloat16)] * count,
        in_specs=[vmem] * (count + 8),
        out_specs=[vmem] * count,
        compiler_params=pltpu.CompilerParams(vmem_limit_bytes=14 * 2**20),
        cost_estimate=pl.CostEstimate(
            flops=2 * count * TOKENS * 2048 * 2048,
            bytes_accessed=(8 + count) * 2**20,
            transcendentals=0,
        ),
        name="project",
    )(*attended, *own, *other)


def pieces_of(blocks, cols):
    return [
        jnp.concatenate([blocks[2 * p][:, cols], blocks[2 * p + 1][:, cols]], axis=0)
        for p in range(2)
    ]


def dispatch_kernel(*refs):
    blocks, pick_ref, outs = refs[:4], refs[4], refs[5:]
    for n in range(4):
        cols = pl.ds(n * 512, 512)
        pieces = pieces_of(blocks, cols)
        for chip, out in enumerate(outs):
            for p in range(2):
                rows = jnp.dot(pick_ref[chip, p], pieces[p], preferred_element_type=jnp.float32)
                rows = rows.astype(jnp.bfloat16).reshape(4, SLOTS, 512)
                out[:, p * SLOTS : (p + 1) * SLOTS, cols] = rows


def dispatch(blocks, pick):
    vmem = pl.BlockSpec(memory_space=pltpu.VMEM)
    chips = pick.shape[0]
    return pl.pallas_call(
        dispatch_kernel,
        out_shape=[jax.ShapeDtypeStruct((4, 2 * SLOTS, WIDTH), jnp.bfloat16)] * chips,
        in_specs=[vmem] * 5,
        out_specs=[vmem] * chips,
        compiler_params=pltpu.CompilerParams(vmem_limit_bytes=12 * 2**20),
        cost_estimate=pl.CostEstimate(
            flops=2 * chips * 384 * 256 * 2048, bytes_accessed=6 * 2**20, transcendentals=0
        ),
        name="dispatch",
    )(*blocks, pick)


def combine_kernel(chips, last, *refs):
    sources, put_ref, refs = refs[:chips], refs[chips], refs[chips + 1 :]
    for n in range(4):
        cols = pl.ds(n * 512, 512)
        for p in range(2):
            rows = [
                source[e, p * SLOTS : (p + 1) * SLOTS, cols] for source in sources for e in range(4)
            ]
            mixed = jnp.dot(
                put_ref[p], jnp.concatenate(rows, axis=0), preferred_element_type=jnp.float32
            )
            for half in range(2):
                part = mixed[half * TOKENS : (half + 1) * TOKENS]
                if not last:
                    refs[0][2 * p + half, :, cols] = part
                    continue
                part = part + refs[0][2 * p + half, :, cols]
                out = refs[1 + 2 * p + half]
                out[:, cols] = part.astype(out.dtype)


def combine(sources, put, earlier=None):
    vmem = pl.BlockSpec(memory_space=pltpu.VMEM)
    last = earlier is not None
    if last:
        shapes = [jax.ShapeDtypeStruct((TOKENS, WIDTH), jnp.float32)]
        shapes += [jax.ShapeDtypeStruct((TOKENS, WIDTH), jnp.bfloat16)] * 3
    else:
        shapes = [jax.ShapeDtypeStruct((4, TOKENS, WIDTH), jnp.float32)]
    operands = [*sources, put] + ([earlier] if last else [])
    return pl.pallas_call(
        functools.partial(combine_kernel, len(sources), last),
        out_shape=shapes,
        in_specs=[vmem] * len(operands),
        out_specs=[vmem] * len(shapes),
        compiler_params=pltpu.CompilerParams(vmem_limit_bytes=16 * 2**20),
        cost_estimate=pl.CostEstimate(
            flops=2 * len(sources) * 384 * 256 * 2048, bytes_accessed=8 * 2**20, transcendentals=0
        ),
        name="combine",
    )(*operands)


def experts_kernel(count, *refs):
    sources, refs = refs[:count], refs[count:]
    hbm, refs = refs[:6], refs[6:]
    outs, refs = refs[:count], refs[count:]
    act_ref, gate_buf, up_buf, down_buf, sems = refs
    buffers = (gate_buf, up_buf, down_buf)

    def copies(e):
        side, index, slot = e // 2, e % 2, e % 2
        return [
            pltpu.make_async_copy(
                hbm[3 * side + w].at[index], buffers[w].at[slot], sems.at[w, slot]
            )
            for w in range(3)
        ]

    for e in range(2):
        for c in copies(e):
            c.start()
    for e in range(4):
        slot = e % 2
        waits = copies(e)
        waits[0].wait()
        waits[1].wait()
        rows = jnp.concatenate([source[e] for source in sources], axis=0)
        for n in range(3):
            cols = pl.ds(n * 256, 256)
            gate = jnp.dot(rows, gate_buf[slot, :, cols], preferred_element_type=jnp.float32)
            upward = jnp.dot(rows, up_buf[slot, :, cols], preferred_element_type=jnp.float32)
            act_ref[:, cols] = (gate / (1.0 + jnp.exp(-gate)) * upward).astype(jnp.bfloat16)
        waits[2].wait()
        active = act_ref[...]
        for n in range(4):
            cols = pl.ds(n * 512, 512)
            result = jnp.dot(active, down_buf[slot, :, cols], preferred_element_type=jnp.float32)
            result = result.astype(jnp.bfloat16)
            for i, out in enumerate(outs):
                out[e, :, cols] = result[i * 2 * SLOTS : (i + 1) * 2 * SLOTS]
        if e + 2 < 4:
            for c in copies(e + 2):
                c.start()


def experts(sources, mine, others):
    count = len(sources)
    vmem = pl.BlockSpec(memory_space=pltpu.VMEM)
    hbm = pl.BlockSpec(memory_space=pltpu.HBM)
    rows = count * 4 * 2 * SLOTS
    return pl.pallas_call(
        functools.partial(experts_kernel, count),
        out_shape=[jax.ShapeDtypeStruct((4, 2 * SLOTS, WIDTH), jnp.bfloat16)] * count,
        in_specs=[vmem] * count + [hbm] * 6,
        out_specs=[vmem] * count,
        scratch_shapes=[
            pltpu.VMEM((count * 2 * SLOTS, FFE), jnp.bfloat16),
            pltpu.VMEM((2, WIDTH, FFE), jnp.bfloat16),
            pltpu.VMEM((2, WIDTH, FFE), jnp.bfloat16),
            pltpu.VMEM((2, FFE, WIDTH), jnp.bfloat16),
            pltpu.SemaphoreType.DMA((3, 2)),
        ],
        compiler_params=pltpu.CompilerParams(vmem_limit_bytes=40 * 2**20),
        cost_estimate=pl.CostEstimate(
            flops=6 * rows * 2048 * 768,
            bytes_accessed=(36 + 3 * count) * 2**20,
            transcendentals=rows * 768,
        ),
        name="experts",
    )(*sources, *mine, *others)


def routing(meta, y, z, core):
    meta = jnp.where(core == 0, meta[0], meta[:, 0]).astype(jnp.float32)
    meta = meta.reshape(2, 2, 32, TOKENS).transpose(0, 2, 1, 3).reshape(2, 32, 2 * TOKENS)
    ids = meta[:, :8]
    route = meta[:, 8:16] + meta[:, 16:24] + meta[:, 24:32]
    index = jnp.arange(16, dtype=jnp.int32)
    chip, expert = index // 4, index % 4
    across = jnp.where(chip == 3, 2, jnp.where(chip == 2, 1, -chip))
    on_y, on_z = jnp.where(core == 0, 0, across), jnp.where(core == 0, across, 0)
    chip = (y + on_y + 4) % 4 * 4 + (z + on_z + 4) % 4
    wanted = chip * 4 + (expert + 2 * core) % 4
    same = ids[:, None] == wanted.astype(jnp.float32)[None, :, None, None]
    chosen = jnp.any(same, axis=2)
    share = jnp.sum(jnp.where(same, route[:, None], 0.0), axis=2)
    places = jnp.arange(2 * TOKENS, dtype=jnp.int32)
    before = (places[:, None] < places[None, :]).astype(jnp.bfloat16)
    rank = jnp.einsum(
        "pet,tu->peu", chosen.astype(jnp.bfloat16), before, preferred_element_type=jnp.float32
    )
    rank = jnp.where(chosen, rank, -1.0)
    slots = jnp.arange(SLOTS, dtype=jnp.float32)
    pick = (rank[:, :, None] == slots[None, None, :, None]).astype(jnp.bfloat16)
    pick = pick.reshape(2, 4, 4 * SLOTS, 2 * TOKENS).transpose(1, 0, 2, 3)
    by_slot = lambda v: jnp.repeat(v.transpose(0, 2, 1), SLOTS, axis=2)
    slots = jnp.tile(slots, 16)
    put = jnp.where(by_slot(rank) == slots, by_slot(share), 0.0).astype(jnp.bfloat16)
    return pick, put


def after(value, *others):
    return lax.optimization_barrier((value, *others))[0]


def body(
    queries,
    keys,
    values,
    residual,
    doc_lengths,
    expert_ids,
    route_weights,
    out_weight,
    norm_gain,
    expert_gate,
    expert_up,
    expert_down,
):
    f32 = jnp.float32
    x, core = lax.axis_index("dp"), lax.axis_index("pair")
    y, z = lax.axis_index("ctx") // 4, lax.axis_index("ctx") % 4
    yy, zz = ("y", "y"), ("z", "z")
    queries, keys, values = queries[0], keys[0], values[0]

    route = route_weights[0].T
    high = lax.reduce_precision(route, 8, 7)
    middle = lax.reduce_precision(route - high, 8, 7)
    low = route - high - middle
    meta = jnp.concatenate([expert_ids[0].T.astype(f32), high, middle, low])
    meta = meta.astype(jnp.bfloat16)
    meta = jnp.concatenate([meta[:16], meta[16:]], axis=1)

    def kv_of(head):
        pair = jnp.concatenate(
            [
                lax.dynamic_slice_in_dim(keys, head * HDIM, HDIM, 1),
                lax.dynamic_slice_in_dim(values, head * HDIM, HDIM, 1),
            ],
            axis=1,
        )
        return jnp.concatenate([pair, meta])

    kv_to = [kv_of((y - o + 4) % 4) for o in OFFSETS]
    kv_y = kv_to[:1] + [shift(kv_to[k], yy, -OFFSETS[k]) for k in (1, 2, 3)]
    column = jnp.stack(kv_y)
    kv_z = [column] + [shift(column, zz, -o) for o in OFFSETS[1:]]
    kv = jnp.concatenate(kv_z)

    part = lax.dynamic_slice_in_dim(out_weight, core * 256, 256, 0)
    part = after(part, *kv_to)
    inner = jnp.stack([part] + [shift(part, ("x", "z"), -o) for o in OFFSETS[1:]])
    own = [inner] + [shift(inner, ("z", "x"), -o) for o in OFFSETS[1:3]]
    own.append(shift(after(inner, kv_z[1], kv_z[2]), ("z", "x"), -OFFSETS[3]))

    def queries_of(group):
        return lax.dynamic_slice_in_dim(queries, group * WIDTH, WIDTH, 1)

    blocks = [queries_of(y), None, None, shift(queries_of((y + 2) % 4), yy, -2)]
    for k in (1, 2):
        o = OFFSETS[k]
        near = after(queries_of((y - o + 4) % 4), blocks[3], kv)
        blocks[k] = shift(near, yy, -o)

    meta = kv[:, TOKENS:]
    meta = jnp.concatenate([meta[:, :, :TOKENS], meta[:, :, TOKENS:]], axis=1)
    pick, put = routing(meta.reshape(4, 4, 32, TOKENS), y, z, core)

    def attended(k):
        return attend(OFFSETS[k], doc_lengths, blocks[k], kv)

    last = blocks[2]
    blocks[2] = after(last, own[1], own[2], pick, put)
    mixed = [attended(k) for k in range(4)]
    other = [swap(after(w, mixed[0], mixed[3], mixed[1], last)) for w in own[:3]]
    other.append(swap(after(own[3], mixed[2])))

    far, below, above, here = project([mixed[3], mixed[1], mixed[2], mixed[0]], own, other)

    weights = [expert_gate, expert_up, expert_down]
    swapped = [swap(after(expert_gate, far)), swap(after(expert_up, far))]

    terms = [here, shift(below, yy, -1), shift(above, yy, 1), shift(far, yy, 2)]
    hidden = residual[0].astype(f32) + sum(t.astype(f32) for t in terms)
    mean_square = jnp.mean(hidden * hidden, axis=-1, keepdims=True)
    normed = (hidden * lax.rsqrt(mean_square + EPSILON) * norm_gain).astype(jnp.bfloat16)
    normed = after(normed, *swapped)
    swapped.append(swap(after(expert_down, normed)))

    prim, sec = ("y", "z"), ("z", "y")
    line = [normed] + [shift(normed, prim, -o) for o in OFFSETS[1:]]
    below, above = dispatch(line, pick[1:3])
    here, far = dispatch(line, jnp.stack([pick[0], pick[3]]))
    below, above = shift(below, sec, -1), shift(above, sec, 1)
    rest = (weights, swapped)
    (here,) = experts([here], *rest)
    far = shift(after(far, here), sec, 2)
    below, above = experts([below, above], *rest)
    (far,) = experts([after(far, below)], *rest)

    below, above = shift(below, sec, 1), shift(above, sec, -1)
    (near,) = combine([here, below, above], put[:, :, : 12 * SLOTS])
    parts = combine([shift(far, sec, 2)], put[:, :, 12 * SLOTS :], near)
    total = hidden + parts[0]
    for k in range(1, 4):
        total = total + shift(parts[k], prim, OFFSETS[k]).astype(f32)
    return total.astype(jnp.bfloat16)[None]


def solution(mesh):
    return jax.shard_map(
        body,
        mesh=mesh,
        in_specs=(
            P(("dp", "pair"), "ctx", None),
            P(("dp", "pair"), "ctx", None),
            P(("dp", "pair"), "ctx", None),
            P(("dp", "pair"), "ctx", None),
            P(("dp", "pair"), None),
            P(("dp", "pair"), "ctx", None),
            P(("dp", "pair"), "ctx", None),
            P("ctx", "dp"),
            P(),
            P(("ctx", "pair"), None, None),
            P(("ctx", "pair"), None, None),
            P(("ctx", "pair"), None, None),
        ),
        out_specs=P(("dp", "pair"), "ctx", None),
        check_vma=False,
    )
```

```python
import functools
import math

import jax
import jax.numpy as jnp
from jax import lax
from jax.experimental import pallas as pl
from jax.experimental.pallas import tpu as pltpu
from jax.sharding import PartitionSpec as P

RING = 4
TOKENS = 128
WIDTH = 2048
HDIM = 128
HEADS_HERE = 16
FFE = 768
SLOTS = 48
EPSILON = 1e-06
NEGATIVE = -1e30
OFFSETS = (0, -1, 1, 2)
AXES = ("dp", "ctx", "pair")


def shift(value, axes, distance):
    pairs = []
    for x in range(RING):
        for y in range(RING):
            for z in range(RING):
                for core in range(2):
                    to = {"x": x, "y": y, "z": z}
                    to[axes[core]] = (to[axes[core]] + distance) % RING
                    pairs.append(
                        (
                            (x * 16 + y * 4 + z) * 2 + core,
                            (to["x"] * 16 + to["y"] * 4 + to["z"]) * 2 + core,
                        )
                    )
    return lax.ppermute(value, AXES, pairs)


def swap(value):
    return lax.ppermute(value, "pair", [(0, 1), (1, 0)])


def ring_slot(distance):
    distance = lax.rem(distance + 4, 4)
    return jnp.where(distance == 3, 1, jnp.where(distance == 0, 0, distance + 1))


def attend_kernel(offset, lengths, q_ref, kv_ref, out_ref, top_ref, sum_ref, acc_ref):
    place = lax.axis_index("ctx")
    y, z = place // 4, lax.rem(place, 4)
    block = lax.rem(y + offset + 4, 4) * 4 + z
    scale = math.log2(math.e) / math.sqrt(HDIM)
    places = block * TOKENS + lax.broadcasted_iota(jnp.int32, (1, TOKENS), 1)
    starts = jnp.zeros((1, TOKENS), jnp.int32)
    first = jnp.int32(0)
    end = jnp.int32(0)
    for d in range(8):
        end = end + lengths[0, d]
        starts = jnp.maximum(starts, jnp.where(places >= end, end, 0))
        first = jnp.maximum(first, jnp.where(block * TOKENS >= end, end, 0))
    top_ref[...] = jnp.full_like(top_ref, NEGATIVE)
    sum_ref[...] = jnp.zeros_like(sum_ref)
    acc_ref[...] = jnp.zeros_like(acc_ref)
    rows = lax.broadcasted_iota(jnp.int32, (TOKENS, TOKENS), 0)

    def step(chunk, carry):
        slot = ring_slot(lax.rem(chunk, 4) - z) * 4 + ring_slot(chunk // 4 - y)
        keys = kv_ref[slot, :TOKENS, :HDIM]
        values = kv_ref[slot, :TOKENS, HDIM:].T
        key_places = chunk * TOKENS + rows
        allowed = (key_places <= places) & (key_places >= starts)
        bias = jnp.where(allowed, 0.0, NEGATIVE).astype(jnp.float32)
        bias = jnp.concatenate([bias, bias], axis=1)
        for pair in range(HEADS_HERE // 2):
            h = 2 * pair * HDIM
            q = jnp.concatenate([q_ref[:, h : h + HDIM], q_ref[:, h + HDIM : h + 2 * HDIM]], axis=0)
            s = lax.dot_general(
                keys, q, (((1,), (1,)), ((), ())), preferred_element_type=jnp.float32
            )
            s = s * scale + bias
            old = top_ref[pair]
            top = jnp.maximum(old, jnp.max(s, axis=0, keepdims=True))
            weights = jnp.exp2(s - top)
            fade = jnp.exp2(old - top)
            top_ref[pair] = top
            sum_ref[pair] = sum_ref[pair] * fade + jnp.sum(weights, axis=0, keepdims=True)
            acc_ref[pair] = acc_ref[pair] * fade + jnp.dot(
                values, weights.astype(jnp.bfloat16), preferred_element_type=jnp.float32
            )
        return carry

    lax.fori_loop(first // TOKENS, block + 1, step, 0)
    for pair in range(HEADS_HERE // 2):
        h = 2 * pair * HDIM
        mixed = (acc_ref[pair] / sum_ref[pair]).T.astype(jnp.bfloat16)
        out_ref[:, h : h + HDIM] = mixed[:TOKENS]
        out_ref[:, h + HDIM : h + 2 * HDIM] = mixed[TOKENS:]


def attend(offset, lengths, queries, kv):
    vmem = pl.BlockSpec(memory_space=pltpu.VMEM)
    return pl.pallas_call(
        functools.partial(attend_kernel, offset),
        out_shape=jax.ShapeDtypeStruct((TOKENS, WIDTH), jnp.bfloat16),
        in_specs=[pl.BlockSpec(memory_space=pltpu.SMEM), vmem, vmem],
        out_specs=vmem,
        scratch_shapes=[
            pltpu.VMEM((8, 1, 256), jnp.float32),
            pltpu.VMEM((8, 1, 256), jnp.float32),
            pltpu.VMEM((8, HDIM, 256), jnp.float32),
        ],
        compiler_params=pltpu.CompilerParams(vmem_limit_bytes=8 * 2**20),
        cost_estimate=pl.CostEstimate(
            flops=4 * 2**30, bytes_accessed=3 * 2**20, transcendentals=2048 * 640
        ),
        name="attend",
    )(lengths, queries, kv)


def project_kernel(count, *refs):
    att, own, other = refs[0:count], refs[count : count + 4], refs[count + 4 : count + 8]
    outs = refs[count + 8 :]
    x, core = lax.axis_index("dp"), lax.axis_index("pair")
    z = lax.rem(lax.axis_index("ctx"), 4)

    def run(stacks):
        for i in range(4):
            column = lax.rem(x + OFFSETS[i] + 4, 4) * 512
            total = None
            for half in range(2):
                for j in range(4):
                    place = lax.rem(z + OFFSETS[j] + 4, 4) * 512 + half * 256
                    place = pl.ds(pl.multiple_of(place, 256), 256)
                    left = jnp.concatenate([a[:, place] for a in att], axis=0)
                    right = stacks[0][j][i] if half == 0 else stacks[1][i][j]
                    term = jnp.dot(left, right, preferred_element_type=jnp.float32)
                    total = term if total is None else total + term
            total = total.astype(jnp.bfloat16)
            for n in range(count):
                part = total[n * TOKENS : (n + 1) * TOKENS]
                outs[n][:, pl.ds(pl.multiple_of(column, 512), 512)] = part

    @pl.when(core == 0)
    def _():
        run((own, other))

    @pl.when(core == 1)
    def _():
        run((other, own))


def project(attended, own, other):
    vmem = pl.BlockSpec(memory_space=pltpu.VMEM)
    count = len(attended)
    return pl.pallas_call(
        functools.partial(project_kernel, count),
        out_shape=[jax.ShapeDtypeStruct((TOKENS, WIDTH), jnp.bfloat16)] * count,
        in_specs=[vmem] * (count + 8),
        out_specs=[vmem] * count,
        compiler_params=pltpu.CompilerParams(vmem_limit_bytes=14 * 2**20),
        cost_estimate=pl.CostEstimate(
            flops=2 * count * TOKENS * 2048 * 2048,
            bytes_accessed=(8 + count) * 2**20,
            transcendentals=0,
        ),
        name="project",
    )(*attended, *own, *other)


def pieces_of(blocks, cols):
    return [
        jnp.concatenate([blocks[2 * p][:, cols], blocks[2 * p + 1][:, cols]], axis=0)
        for p in range(2)
    ]


def dispatch_kernel(*refs):
    blocks, pick_ref, outs = refs[:4], refs[4], refs[5:]
    for n in range(4):
        cols = pl.ds(n * 512, 512)
        pieces = pieces_of(blocks, cols)
        for chip, out in enumerate(outs):
            for p in range(2):
                rows = jnp.dot(pick_ref[chip, p], pieces[p], preferred_element_type=jnp.float32)
                rows = rows.astype(jnp.bfloat16).reshape(4, SLOTS, 512)
                out[:, p * SLOTS : (p + 1) * SLOTS, cols] = rows


def dispatch(blocks, pick):
    vmem = pl.BlockSpec(memory_space=pltpu.VMEM)
    chips = pick.shape[0]
    return pl.pallas_call(
        dispatch_kernel,
        out_shape=[jax.ShapeDtypeStruct((4, 2 * SLOTS, WIDTH), jnp.bfloat16)] * chips,
        in_specs=[vmem] * 5,
        out_specs=[vmem] * chips,
        compiler_params=pltpu.CompilerParams(vmem_limit_bytes=12 * 2**20),
        cost_estimate=pl.CostEstimate(
            flops=2 * chips * 384 * 256 * 2048, bytes_accessed=6 * 2**20, transcendentals=0
        ),
        name="dispatch",
    )(*blocks, pick)


def combine_kernel(chips, last, *refs):
    sources, put_ref, refs = refs[:chips], refs[chips], refs[chips + 1 :]
    for n in range(4):
        cols = pl.ds(n * 512, 512)
        for p in range(2):
            rows = [
                source[e, p * SLOTS : (p + 1) * SLOTS, cols] for source in sources for e in range(4)
            ]
            mixed = jnp.dot(
                put_ref[p], jnp.concatenate(rows, axis=0), preferred_element_type=jnp.float32
            )
            for half in range(2):
                part = mixed[half * TOKENS : (half + 1) * TOKENS]
                if not last:
                    refs[0][2 * p + half, :, cols] = part
                    continue
                part = part + refs[0][2 * p + half, :, cols]
                out = refs[1 + 2 * p + half]
                out[:, cols] = part.astype(out.dtype)


def combine(sources, put, earlier=None):
    vmem = pl.BlockSpec(memory_space=pltpu.VMEM)
    last = earlier is not None
    if last:
        shapes = [jax.ShapeDtypeStruct((TOKENS, WIDTH), jnp.float32)]
        shapes += [jax.ShapeDtypeStruct((TOKENS, WIDTH), jnp.bfloat16)] * 3
    else:
        shapes = [jax.ShapeDtypeStruct((4, TOKENS, WIDTH), jnp.float32)]
    operands = [*sources, put] + ([earlier] if last else [])
    return pl.pallas_call(
        functools.partial(combine_kernel, len(sources), last),
        out_shape=shapes,
        in_specs=[vmem] * len(operands),
        out_specs=[vmem] * len(shapes),
        compiler_params=pltpu.CompilerParams(vmem_limit_bytes=16 * 2**20),
        cost_estimate=pl.CostEstimate(
            flops=2 * len(sources) * 384 * 256 * 2048, bytes_accessed=8 * 2**20, transcendentals=0
        ),
        name="combine",
    )(*operands)


def experts_kernel(count, *refs):
    sources, refs = refs[:count], refs[count:]
    hbm, refs = refs[:6], refs[6:]
    outs, refs = refs[:count], refs[count:]
    act_ref, gate_buf, up_buf, down_buf, sems = refs
    buffers = (gate_buf, up_buf, down_buf)

    def copies(e):
        side, index, slot = e // 2, e % 2, e % 2
        return [
            pltpu.make_async_copy(
                hbm[3 * side + w].at[index], buffers[w].at[slot], sems.at[w, slot]
            )
            for w in range(3)
        ]

    for e in range(2):
        for c in copies(e):
            c.start()
    for e in range(4):
        slot = e % 2
        waits = copies(e)
        waits[0].wait()
        waits[1].wait()
        rows = jnp.concatenate([source[e] for source in sources], axis=0)
        for n in range(3):
            cols = pl.ds(n * 256, 256)
            gate = jnp.dot(rows, gate_buf[slot, :, cols], preferred_element_type=jnp.float32)
            upward = jnp.dot(rows, up_buf[slot, :, cols], preferred_element_type=jnp.float32)
            act_ref[:, cols] = (gate / (1.0 + jnp.exp(-gate)) * upward).astype(jnp.bfloat16)
        waits[2].wait()
        active = act_ref[...]
        for n in range(4):
            cols = pl.ds(n * 512, 512)
            result = jnp.dot(active, down_buf[slot, :, cols], preferred_element_type=jnp.float32)
            result = result.astype(jnp.bfloat16)
            for i, out in enumerate(outs):
                out[e, :, cols] = result[i * 2 * SLOTS : (i + 1) * 2 * SLOTS]
        if e + 2 < 4:
            for c in copies(e + 2):
                c.start()


def experts(sources, mine, others):
    count = len(sources)
    vmem = pl.BlockSpec(memory_space=pltpu.VMEM)
    hbm = pl.BlockSpec(memory_space=pltpu.HBM)
    rows = count * 4 * 2 * SLOTS
    return pl.pallas_call(
        functools.partial(experts_kernel, count),
        out_shape=[jax.ShapeDtypeStruct((4, 2 * SLOTS, WIDTH), jnp.bfloat16)] * count,
        in_specs=[vmem] * count + [hbm] * 6,
        out_specs=[vmem] * count,
        scratch_shapes=[
            pltpu.VMEM((count * 2 * SLOTS, FFE), jnp.bfloat16),
            pltpu.VMEM((2, WIDTH, FFE), jnp.bfloat16),
            pltpu.VMEM((2, WIDTH, FFE), jnp.bfloat16),
            pltpu.VMEM((2, FFE, WIDTH), jnp.bfloat16),
            pltpu.SemaphoreType.DMA((3, 2)),
        ],
        compiler_params=pltpu.CompilerParams(vmem_limit_bytes=40 * 2**20),
        cost_estimate=pl.CostEstimate(
            flops=6 * rows * 2048 * 768,
            bytes_accessed=(36 + 3 * count) * 2**20,
            transcendentals=rows * 768,
        ),
        name="experts",
    )(*sources, *mine, *others)


def routing(meta, y, z, core):
    meta = jnp.where(core == 0, meta[0], meta[:, 0]).astype(jnp.float32)
    meta = meta.reshape(2, 2, 32, TOKENS).transpose(0, 2, 1, 3).reshape(2, 32, 2 * TOKENS)
    ids = meta[:, :8]
    route = meta[:, 8:16] + meta[:, 16:24] + meta[:, 24:32]
    index = jnp.arange(16, dtype=jnp.int32)
    chip, expert = index // 4, index % 4
    across = jnp.where(chip == 3, 2, jnp.where(chip == 2, 1, -chip))
    on_y, on_z = jnp.where(core == 0, 0, across), jnp.where(core == 0, across, 0)
    chip = (y + on_y + 4) % 4 * 4 + (z + on_z + 4) % 4
    wanted = chip * 4 + (expert + 2 * core) % 4
    same = ids[:, None] == wanted.astype(jnp.float32)[None, :, None, None]
    chosen = jnp.any(same, axis=2)
    share = jnp.sum(jnp.where(same, route[:, None], 0.0), axis=2)
    places = jnp.arange(2 * TOKENS, dtype=jnp.int32)
    before = (places[:, None] < places[None, :]).astype(jnp.bfloat16)
    rank = jnp.einsum(
        "pet,tu->peu", chosen.astype(jnp.bfloat16), before, preferred_element_type=jnp.float32
    )
    rank = jnp.where(chosen, rank, -1.0)
    slots = jnp.arange(SLOTS, dtype=jnp.float32)
    pick = (rank[:, :, None] == slots[None, None, :, None]).astype(jnp.bfloat16)
    pick = pick.reshape(2, 4, 4 * SLOTS, 2 * TOKENS).transpose(1, 0, 2, 3)
    by_slot = lambda v: jnp.repeat(v.transpose(0, 2, 1), SLOTS, axis=2)
    slots = jnp.tile(slots, 16)
    put = jnp.where(by_slot(rank) == slots, by_slot(share), 0.0).astype(jnp.bfloat16)
    return pick, put


def after(value, *others):
    return lax.optimization_barrier((value, *others))[0]


def body(
    queries,
    keys,
    values,
    residual,
    doc_lengths,
    expert_ids,
    route_weights,
    out_weight,
    norm_gain,
    expert_gate,
    expert_up,
    expert_down,
):
    f32 = jnp.float32
    x, core = lax.axis_index("dp"), lax.axis_index("pair")
    y, z = lax.axis_index("ctx") // 4, lax.axis_index("ctx") % 4
    yy, zz = ("y", "y"), ("z", "z")
    queries, keys, values = queries[0], keys[0], values[0]

    route = route_weights[0].T
    high = lax.reduce_precision(route, 8, 7)
    middle = lax.reduce_precision(route - high, 8, 7)
    low = route - high - middle
    meta = jnp.concatenate([expert_ids[0].T.astype(f32), high, middle, low])
    meta = meta.astype(jnp.bfloat16)
    meta = jnp.concatenate([meta[:16], meta[16:]], axis=1)

    def kv_of(head):
        pair = jnp.concatenate(
            [
                lax.dynamic_slice_in_dim(keys, head * HDIM, HDIM, 1),
                lax.dynamic_slice_in_dim(values, head * HDIM, HDIM, 1),
            ],
            axis=1,
        )
        return jnp.concatenate([pair, meta])

    kv_to = [kv_of((y - o + 4) % 4) for o in OFFSETS]
    kv_y = kv_to[:1] + [shift(kv_to[k], yy, -OFFSETS[k]) for k in (1, 2, 3)]
    column = jnp.stack(kv_y)
    kv_z = [column] + [shift(column, zz, -o) for o in OFFSETS[1:]]
    kv = jnp.concatenate(kv_z)

    part = lax.dynamic_slice_in_dim(out_weight, core * 256, 256, 0)
    part = after(part, *kv_to)
    inner = jnp.stack([part] + [shift(part, ("x", "z"), -o) for o in OFFSETS[1:]])
    own = [inner] + [shift(inner, ("z", "x"), -o) for o in OFFSETS[1:3]]
    own.append(shift(after(inner, kv_z[1], kv_z[2]), ("z", "x"), -OFFSETS[3]))

    def queries_of(group):
        return lax.dynamic_slice_in_dim(queries, group * WIDTH, WIDTH, 1)

    blocks = [queries_of(y), None, None, shift(queries_of((y + 2) % 4), yy, -2)]
    for k in (1, 2):
        o = OFFSETS[k]
        near = after(queries_of((y - o + 4) % 4), blocks[3], kv)
        blocks[k] = shift(near, yy, -o)

    def attended(k):
        return attend(OFFSETS[k], doc_lengths, blocks[k], kv)

    last = blocks[2]
    blocks[2] = after(last, own[1], own[2])
    mixed = [attended(k) for k in range(4)]
    meta = after(kv[:, TOKENS:], mixed[1])
    meta = jnp.concatenate([meta[:, :, :TOKENS], meta[:, :, TOKENS:]], axis=1)
    pick, put = routing(meta.reshape(4, 4, 32, TOKENS), y, z, core)

    other = [swap(after(w, mixed[0], mixed[3], mixed[1], last)) for w in own[:3]]
    other.append(swap(after(own[3], mixed[2], pick, put)))

    far, below, above, here = project([mixed[3], mixed[1], mixed[2], mixed[0]], own, other)

    weights = [expert_gate, expert_up, expert_down]
    swapped = [swap(after(expert_gate, far)), swap(after(expert_up, far))]

    terms = [here, shift(below, yy, -1), shift(above, yy, 1), shift(far, yy, 2)]
    hidden = residual[0].astype(f32) + sum(t.astype(f32) for t in terms)
    mean_square = jnp.mean(hidden * hidden, axis=-1, keepdims=True)
    normed = (hidden * lax.rsqrt(mean_square + EPSILON) * norm_gain).astype(jnp.bfloat16)
    normed = after(normed, *swapped)
    swapped.append(swap(after(expert_down, normed)))

    prim, sec = ("y", "z"), ("z", "y")
    line = [normed] + [shift(normed, prim, -o) for o in OFFSETS[1:]]
    below, above = dispatch(line, pick[1:3])
    here, far = dispatch(line, jnp.stack([pick[0], pick[3]]))
    below, above = shift(below, sec, -1), shift(above, sec, 1)
    rest = (weights, swapped)
    (here,) = experts([here], *rest)
    far = shift(after(far, here, below, above), sec, 2)
    below, above = experts([below, above], *rest)
    (far,) = experts([after(far, below)], *rest)

    below, above = shift(below, sec, 1), shift(above, sec, -1)
    (near,) = combine([here, below, above], put[:, :, : 12 * SLOTS])
    parts = combine([shift(far, sec, 2)], put[:, :, 12 * SLOTS :], near)
    total = hidden + parts[0]
    for k in range(1, 4):
        total = total + shift(parts[k], prim, OFFSETS[k]).astype(f32)
    return total.astype(jnp.bfloat16)[None]


def solution(mesh):
    return jax.shard_map(
        body,
        mesh=mesh,
        in_specs=(
            P(("dp", "pair"), "ctx", None),
            P(("dp", "pair"), "ctx", None),
            P(("dp", "pair"), "ctx", None),
            P(("dp", "pair"), "ctx", None),
            P(("dp", "pair"), None),
            P(("dp", "pair"), "ctx", None),
            P(("dp", "pair"), "ctx", None),
            P("ctx", "dp"),
            P(),
            P(("ctx", "pair"), None, None),
            P(("ctx", "pair"), None, None),
            P(("ctx", "pair"), None, None),
        ),
        out_specs=P(("dp", "pair"), "ctx", None),
        check_vma=False,
    )
```

```python
import functools
import math

import jax
import jax.numpy as jnp
from jax import lax
from jax.experimental import pallas as pl
from jax.experimental.pallas import tpu as pltpu
from jax.sharding import PartitionSpec as P

RING = 4
TOKENS = 128
WIDTH = 2048
HDIM = 128
HEADS_HERE = 16
FFE = 768
SLOTS = 48
EPSILON = 1e-06
NEGATIVE = -1e30
OFFSETS = (0, -1, 1, 2)
AXES = ("dp", "ctx", "pair")


def shift(value, axes, distance):
    pairs = []
    for x in range(RING):
        for y in range(RING):
            for z in range(RING):
                for core in range(2):
                    to = {"x": x, "y": y, "z": z}
                    to[axes[core]] = (to[axes[core]] + distance) % RING
                    pairs.append(
                        (
                            (x * 16 + y * 4 + z) * 2 + core,
                            (to["x"] * 16 + to["y"] * 4 + to["z"]) * 2 + core,
                        )
                    )
    return lax.ppermute(value, AXES, pairs)


def swap(value):
    return lax.ppermute(value, "pair", [(0, 1), (1, 0)])


def ring_slot(distance):
    distance = lax.rem(distance + 4, 4)
    return jnp.where(distance == 3, 1, jnp.where(distance == 0, 0, distance + 1))


def attend_kernel(offset, lengths, q_ref, kv_ref, out_ref, top_ref, sum_ref, acc_ref):
    place = lax.axis_index("ctx")
    y, z = place // 4, lax.rem(place, 4)
    block = lax.rem(y + offset + 4, 4) * 4 + z
    scale = math.log2(math.e) / math.sqrt(HDIM)
    places = block * TOKENS + lax.broadcasted_iota(jnp.int32, (1, TOKENS), 1)
    starts = jnp.zeros((1, TOKENS), jnp.int32)
    first = jnp.int32(0)
    end = jnp.int32(0)
    for d in range(8):
        end = end + lengths[0, d]
        starts = jnp.maximum(starts, jnp.where(places >= end, end, 0))
        first = jnp.maximum(first, jnp.where(block * TOKENS >= end, end, 0))
    top_ref[...] = jnp.full_like(top_ref, NEGATIVE)
    sum_ref[...] = jnp.zeros_like(sum_ref)
    acc_ref[...] = jnp.zeros_like(acc_ref)
    rows = lax.broadcasted_iota(jnp.int32, (TOKENS, TOKENS), 0)

    def step(chunk, carry):
        slot = ring_slot(lax.rem(chunk, 4) - z) * 4 + ring_slot(chunk // 4 - y)
        keys = kv_ref[slot, :TOKENS, :HDIM]
        values = kv_ref[slot, :TOKENS, HDIM:].T
        key_places = chunk * TOKENS + rows
        allowed = (key_places <= places) & (key_places >= starts)
        bias = jnp.where(allowed, 0.0, NEGATIVE).astype(jnp.float32)
        bias = jnp.concatenate([bias, bias], axis=1)
        for pair in range(HEADS_HERE // 2):
            h = 2 * pair * HDIM
            q = jnp.concatenate([q_ref[:, h : h + HDIM], q_ref[:, h + HDIM : h + 2 * HDIM]], axis=0)
            s = lax.dot_general(
                keys, q, (((1,), (1,)), ((), ())), preferred_element_type=jnp.float32
            )
            s = s * scale + bias
            old = top_ref[pair]
            top = jnp.maximum(old, jnp.max(s, axis=0, keepdims=True))
            weights = jnp.exp2(s - top)
            fade = jnp.exp2(old - top)
            top_ref[pair] = top
            sum_ref[pair] = sum_ref[pair] * fade + jnp.sum(weights, axis=0, keepdims=True)
            acc_ref[pair] = acc_ref[pair] * fade + jnp.dot(
                values, weights.astype(jnp.bfloat16), preferred_element_type=jnp.float32
            )
        return carry

    lax.fori_loop(first // TOKENS, block + 1, step, 0)
    for pair in range(HEADS_HERE // 2):
        h = 2 * pair * HDIM
        mixed = (acc_ref[pair] / sum_ref[pair]).T.astype(jnp.bfloat16)
        out_ref[:, h : h + HDIM] = mixed[:TOKENS]
        out_ref[:, h + HDIM : h + 2 * HDIM] = mixed[TOKENS:]


def attend(offset, lengths, queries, kv):
    vmem = pl.BlockSpec(memory_space=pltpu.VMEM)
    return pl.pallas_call(
        functools.partial(attend_kernel, offset),
        out_shape=jax.ShapeDtypeStruct((TOKENS, WIDTH), jnp.bfloat16),
        in_specs=[pl.BlockSpec(memory_space=pltpu.SMEM), vmem, vmem],
        out_specs=vmem,
        scratch_shapes=[
            pltpu.VMEM((8, 1, 256), jnp.float32),
            pltpu.VMEM((8, 1, 256), jnp.float32),
            pltpu.VMEM((8, HDIM, 256), jnp.float32),
        ],
        compiler_params=pltpu.CompilerParams(vmem_limit_bytes=8 * 2**20),
        cost_estimate=pl.CostEstimate(
            flops=4 * 2**30, bytes_accessed=3 * 2**20, transcendentals=2048 * 640
        ),
        name="attend",
    )(lengths, queries, kv)


def project_kernel(count, *refs):
    att, own, other = refs[0:count], refs[count : count + 4], refs[count + 4 : count + 8]
    outs = refs[count + 8 :]
    x, core = lax.axis_index("dp"), lax.axis_index("pair")
    z = lax.rem(lax.axis_index("ctx"), 4)

    def run(stacks):
        for i in range(4):
            column = lax.rem(x + OFFSETS[i] + 4, 4) * 512
            total = None
            for half in range(2):
                for j in range(4):
                    place = lax.rem(z + OFFSETS[j] + 4, 4) * 512 + half * 256
                    place = pl.ds(pl.multiple_of(place, 256), 256)
                    left = jnp.concatenate([a[:, place] for a in att], axis=0)
                    right = stacks[0][j][i] if half == 0 else stacks[1][i][j]
                    term = jnp.dot(left, right, preferred_element_type=jnp.float32)
                    total = term if total is None else total + term
            total = total.astype(jnp.bfloat16)
            for n in range(count):
                part = total[n * TOKENS : (n + 1) * TOKENS]
                outs[n][:, pl.ds(pl.multiple_of(column, 512), 512)] = part

    @pl.when(core == 0)
    def _():
        run((own, other))

    @pl.when(core == 1)
    def _():
        run((other, own))


def project(attended, own, other):
    vmem = pl.BlockSpec(memory_space=pltpu.VMEM)
    count = len(attended)
    return pl.pallas_call(
        functools.partial(project_kernel, count),
        out_shape=[jax.ShapeDtypeStruct((TOKENS, WIDTH), jnp.bfloat16)] * count,
        in_specs=[vmem] * (count + 8),
        out_specs=[vmem] * count,
        compiler_params=pltpu.CompilerParams(vmem_limit_bytes=14 * 2**20),
        cost_estimate=pl.CostEstimate(
            flops=2 * count * TOKENS * 2048 * 2048,
            bytes_accessed=(8 + count) * 2**20,
            transcendentals=0,
        ),
        name="project",
    )(*attended, *own, *other)


def pieces_of(blocks, cols):
    return [
        jnp.concatenate([blocks[2 * p][:, cols], blocks[2 * p + 1][:, cols]], axis=0)
        for p in range(2)
    ]


def dispatch_kernel(*refs):
    blocks, pick_ref, outs = refs[:4], refs[4], refs[5:]
    for n in range(4):
        cols = pl.ds(n * 512, 512)
        pieces = pieces_of(blocks, cols)
        for chip, out in enumerate(outs):
            for p in range(2):
                rows = jnp.dot(pick_ref[chip, p], pieces[p], preferred_element_type=jnp.float32)
                rows = rows.astype(jnp.bfloat16).reshape(4, SLOTS, 512)
                out[:, p * SLOTS : (p + 1) * SLOTS, cols] = rows


def dispatch(blocks, pick):
    vmem = pl.BlockSpec(memory_space=pltpu.VMEM)
    chips = pick.shape[0]
    return pl.pallas_call(
        dispatch_kernel,
        out_shape=[jax.ShapeDtypeStruct((4, 2 * SLOTS, WIDTH), jnp.bfloat16)] * chips,
        in_specs=[vmem] * 5,
        out_specs=[vmem] * chips,
        compiler_params=pltpu.CompilerParams(vmem_limit_bytes=12 * 2**20),
        cost_estimate=pl.CostEstimate(
            flops=2 * chips * 384 * 256 * 2048, bytes_accessed=6 * 2**20, transcendentals=0
        ),
        name="dispatch",
    )(*blocks, pick)


def combine_kernel(chips, last, *refs):
    sources, put_ref, refs = refs[:chips], refs[chips], refs[chips + 1 :]
    for n in range(4):
        cols = pl.ds(n * 512, 512)
        for p in range(2):
            rows = [
                source[e, p * SLOTS : (p + 1) * SLOTS, cols] for source in sources for e in range(4)
            ]
            mixed = jnp.dot(
                put_ref[p], jnp.concatenate(rows, axis=0), preferred_element_type=jnp.float32
            )
            for half in range(2):
                part = mixed[half * TOKENS : (half + 1) * TOKENS]
                if not last:
                    refs[0][2 * p + half, :, cols] = part
                    continue
                part = part + refs[0][2 * p + half, :, cols]
                out = refs[1 + 2 * p + half]
                out[:, cols] = part.astype(out.dtype)


def combine(sources, put, earlier=None):
    vmem = pl.BlockSpec(memory_space=pltpu.VMEM)
    last = earlier is not None
    if last:
        shapes = [jax.ShapeDtypeStruct((TOKENS, WIDTH), jnp.float32)]
        shapes += [jax.ShapeDtypeStruct((TOKENS, WIDTH), jnp.bfloat16)] * 3
    else:
        shapes = [jax.ShapeDtypeStruct((4, TOKENS, WIDTH), jnp.float32)]
    operands = [*sources, put] + ([earlier] if last else [])
    return pl.pallas_call(
        functools.partial(combine_kernel, len(sources), last),
        out_shape=shapes,
        in_specs=[vmem] * len(operands),
        out_specs=[vmem] * len(shapes),
        compiler_params=pltpu.CompilerParams(vmem_limit_bytes=16 * 2**20),
        cost_estimate=pl.CostEstimate(
            flops=2 * len(sources) * 384 * 256 * 2048, bytes_accessed=8 * 2**20, transcendentals=0
        ),
        name="combine",
    )(*operands)


def experts_kernel(count, *refs):
    sources, refs = refs[:count], refs[count:]
    hbm, refs = refs[:6], refs[6:]
    outs, refs = refs[:count], refs[count:]
    act_ref, gate_buf, up_buf, down_buf, sems = refs
    buffers = (gate_buf, up_buf, down_buf)

    def copies(e):
        side, index, slot = e // 2, e % 2, e % 2
        return [
            pltpu.make_async_copy(
                hbm[3 * side + w].at[index], buffers[w].at[slot], sems.at[w, slot]
            )
            for w in range(3)
        ]

    for e in range(2):
        for c in copies(e):
            c.start()
    for e in range(4):
        slot = e % 2
        waits = copies(e)
        waits[0].wait()
        waits[1].wait()
        rows = jnp.concatenate([source[e] for source in sources], axis=0)
        for n in range(3):
            cols = pl.ds(n * 256, 256)
            gate = jnp.dot(rows, gate_buf[slot, :, cols], preferred_element_type=jnp.float32)
            upward = jnp.dot(rows, up_buf[slot, :, cols], preferred_element_type=jnp.float32)
            act_ref[:, cols] = (gate / (1.0 + jnp.exp(-gate)) * upward).astype(jnp.bfloat16)
        waits[2].wait()
        active = act_ref[...]
        for n in range(4):
            cols = pl.ds(n * 512, 512)
            result = jnp.dot(active, down_buf[slot, :, cols], preferred_element_type=jnp.float32)
            result = result.astype(jnp.bfloat16)
            for i, out in enumerate(outs):
                out[e, :, cols] = result[i * 2 * SLOTS : (i + 1) * 2 * SLOTS]
        if e + 2 < 4:
            for c in copies(e + 2):
                c.start()


def experts(sources, mine, others):
    count = len(sources)
    vmem = pl.BlockSpec(memory_space=pltpu.VMEM)
    hbm = pl.BlockSpec(memory_space=pltpu.HBM)
    rows = count * 4 * 2 * SLOTS
    return pl.pallas_call(
        functools.partial(experts_kernel, count),
        out_shape=[jax.ShapeDtypeStruct((4, 2 * SLOTS, WIDTH), jnp.bfloat16)] * count,
        in_specs=[vmem] * count + [hbm] * 6,
        out_specs=[vmem] * count,
        scratch_shapes=[
            pltpu.VMEM((count * 2 * SLOTS, FFE), jnp.bfloat16),
            pltpu.VMEM((2, WIDTH, FFE), jnp.bfloat16),
            pltpu.VMEM((2, WIDTH, FFE), jnp.bfloat16),
            pltpu.VMEM((2, FFE, WIDTH), jnp.bfloat16),
            pltpu.SemaphoreType.DMA((3, 2)),
        ],
        compiler_params=pltpu.CompilerParams(vmem_limit_bytes=40 * 2**20),
        cost_estimate=pl.CostEstimate(
            flops=6 * rows * 2048 * 768,
            bytes_accessed=(36 + 3 * count) * 2**20,
            transcendentals=rows * 768,
        ),
        name="experts",
    )(*sources, *mine, *others)


def routing(meta, y, z, core):
    meta = jnp.where(core == 0, meta[0], meta[:, 0]).astype(jnp.float32)
    meta = meta.reshape(2, 2, 32, TOKENS).transpose(0, 2, 1, 3).reshape(2, 32, 2 * TOKENS)
    ids = meta[:, :8]
    route = meta[:, 8:16] + meta[:, 16:24] + meta[:, 24:32]
    index = jnp.arange(16, dtype=jnp.int32)
    chip, expert = index // 4, index % 4
    across = jnp.where(chip == 3, 2, jnp.where(chip == 2, 1, -chip))
    on_y, on_z = jnp.where(core == 0, 0, across), jnp.where(core == 0, across, 0)
    chip = (y + on_y + 4) % 4 * 4 + (z + on_z + 4) % 4
    wanted = chip * 4 + (expert + 2 * core) % 4
    same = ids[:, None] == wanted.astype(jnp.float32)[None, :, None, None]
    chosen = jnp.any(same, axis=2)
    share = jnp.sum(jnp.where(same, route[:, None], 0.0), axis=2)
    places = jnp.arange(2 * TOKENS, dtype=jnp.int32)
    before = (places[:, None] < places[None, :]).astype(jnp.bfloat16)
    rank = jnp.einsum(
        "pet,tu->peu", chosen.astype(jnp.bfloat16), before, preferred_element_type=jnp.float32
    )
    rank = jnp.where(chosen, rank, -1.0).astype(jnp.bfloat16)
    share = share.astype(jnp.bfloat16)
    slots = jnp.arange(SLOTS, dtype=jnp.bfloat16)
    pick = (rank[:, :, None] == slots[None, None, :, None]).astype(jnp.bfloat16)
    pick = pick.reshape(2, 4, 4 * SLOTS, 2 * TOKENS).transpose(1, 0, 2, 3)
    by_slot = lambda v: jnp.repeat(v.transpose(0, 2, 1), SLOTS, axis=2)
    slots = jnp.tile(slots, 16)
    put = jnp.where(by_slot(rank) == slots, by_slot(share), jnp.bfloat16(0))
    return pick, put


def after(value, *others):
    return lax.optimization_barrier((value, *others))[0]


def body(
    queries,
    keys,
    values,
    residual,
    doc_lengths,
    expert_ids,
    route_weights,
    out_weight,
    norm_gain,
    expert_gate,
    expert_up,
    expert_down,
):
    f32 = jnp.float32
    x, core = lax.axis_index("dp"), lax.axis_index("pair")
    y, z = lax.axis_index("ctx") // 4, lax.axis_index("ctx") % 4
    yy, zz = ("y", "y"), ("z", "z")
    queries, keys, values = queries[0], keys[0], values[0]

    route = route_weights[0].T
    high = lax.reduce_precision(route, 8, 7)
    middle = lax.reduce_precision(route - high, 8, 7)
    low = route - high - middle
    meta = jnp.concatenate([expert_ids[0].T.astype(f32), high, middle, low])
    meta = meta.astype(jnp.bfloat16)
    meta = jnp.concatenate([meta[:16], meta[16:]], axis=1)

    def kv_of(head):
        pair = jnp.concatenate(
            [
                lax.dynamic_slice_in_dim(keys, head * HDIM, HDIM, 1),
                lax.dynamic_slice_in_dim(values, head * HDIM, HDIM, 1),
            ],
            axis=1,
        )
        return jnp.concatenate([pair, meta])

    kv_to = [kv_of((y - o + 4) % 4) for o in OFFSETS]
    kv_y = kv_to[:1] + [shift(kv_to[k], yy, -OFFSETS[k]) for k in (1, 2, 3)]
    column = jnp.stack(kv_y)
    kv_z = [column] + [shift(column, zz, -o) for o in OFFSETS[1:]]
    kv = jnp.concatenate(kv_z)

    part = lax.dynamic_slice_in_dim(out_weight, core * 256, 256, 0)
    part = after(part, *kv_to)
    inner = jnp.stack([part] + [shift(part, ("x", "z"), -o) for o in OFFSETS[1:]])
    own = [inner] + [shift(inner, ("z", "x"), -o) for o in OFFSETS[1:3]]
    own.append(shift(after(inner, kv_z[1], kv_z[2]), ("z", "x"), -OFFSETS[3]))

    def queries_of(group):
        return lax.dynamic_slice_in_dim(queries, group * WIDTH, WIDTH, 1)

    blocks = [queries_of(y), None, None, shift(queries_of((y + 2) % 4), yy, -2)]
    for k in (1, 2):
        o = OFFSETS[k]
        near = after(queries_of((y - o + 4) % 4), blocks[3], kv)
        blocks[k] = shift(near, yy, -o)

    def attended(k):
        return attend(OFFSETS[k], doc_lengths, blocks[k], kv)

    last = blocks[2]
    blocks[2] = after(last, own[1], own[2])
    mixed = [attended(k) for k in range(4)]
    meta = after(kv[:, TOKENS:], mixed[1])
    meta = jnp.concatenate([meta[:, :, :TOKENS], meta[:, :, TOKENS:]], axis=1)
    pick, put = routing(meta.reshape(4, 4, 32, TOKENS), y, z, core)

    other = [swap(after(w, mixed[0], mixed[3], mixed[1], last, pick, put)) for w in own[:3]]
    other.append(swap(after(own[3], mixed[2])))

    far, below, above, here = project([mixed[3], mixed[1], mixed[2], mixed[0]], own, other)

    weights = [expert_gate, expert_up, expert_down]
    swapped = [swap(after(expert_gate, far)), swap(after(expert_up, far))]

    terms = [here, shift(below, yy, -1), shift(above, yy, 1), shift(far, yy, 2)]
    hidden = residual[0].astype(f32) + sum(t.astype(f32) for t in terms)
    mean_square = jnp.mean(hidden * hidden, axis=-1, keepdims=True)
    normed = (hidden * lax.rsqrt(mean_square + EPSILON) * norm_gain).astype(jnp.bfloat16)
    normed = after(normed, *swapped)
    swapped.append(swap(after(expert_down, normed)))

    prim, sec = ("y", "z"), ("z", "y")
    line = [normed] + [shift(normed, prim, -o) for o in OFFSETS[1:]]
    below, above = dispatch(line, pick[1:3])
    here, far = dispatch(line, jnp.stack([pick[0], pick[3]]))
    below, above = shift(below, sec, -1), shift(above, sec, 1)
    rest = (weights, swapped)
    (here,) = experts([here], *rest)
    far = shift(after(far, here, below, above), sec, 2)
    below, above = experts([below, above], *rest)
    (far,) = experts([after(far, below)], *rest)

    below, above = shift(below, sec, 1), shift(above, sec, -1)
    (near,) = combine([here, below, above], put[:, :, : 12 * SLOTS])
    parts = combine([shift(far, sec, 2)], put[:, :, 12 * SLOTS :], near)
    total = hidden + parts[0]
    for k in range(1, 4):
        total = total + shift(parts[k], prim, OFFSETS[k]).astype(f32)
    return total.astype(jnp.bfloat16)[None]


def solution(mesh):
    return jax.shard_map(
        body,
        mesh=mesh,
        in_specs=(
            P(("dp", "pair"), "ctx", None),
            P(("dp", "pair"), "ctx", None),
            P(("dp", "pair"), "ctx", None),
            P(("dp", "pair"), "ctx", None),
            P(("dp", "pair"), None),
            P(("dp", "pair"), "ctx", None),
            P(("dp", "pair"), "ctx", None),
            P("ctx", "dp"),
            P(),
            P(("ctx", "pair"), None, None),
            P(("ctx", "pair"), None, None),
            P(("ctx", "pair"), None, None),
        ),
        out_specs=P(("dp", "pair"), "ctx", None),
        check_vma=False,
    )
```

```python
import functools
import math

import jax
import jax.numpy as jnp
from jax import lax
from jax.experimental import pallas as pl
from jax.experimental.pallas import tpu as pltpu
from jax.sharding import PartitionSpec as P

RING = 4
TOKENS = 128
WIDTH = 2048
HDIM = 128
HEADS_HERE = 16
FFE = 768
SLOTS = 48
EPSILON = 1e-06
NEGATIVE = -1e30
OFFSETS = (0, -1, 1, 2)
AXES = ("dp", "ctx", "pair")


def shift(value, axes, distance):
    pairs = []
    for x in range(RING):
        for y in range(RING):
            for z in range(RING):
                for core in range(2):
                    to = {"x": x, "y": y, "z": z}
                    to[axes[core]] = (to[axes[core]] + distance) % RING
                    pairs.append(
                        (
                            (x * 16 + y * 4 + z) * 2 + core,
                            (to["x"] * 16 + to["y"] * 4 + to["z"]) * 2 + core,
                        )
                    )
    return lax.ppermute(value, AXES, pairs)


def swap(value):
    return lax.ppermute(value, "pair", [(0, 1), (1, 0)])


def ring_slot(distance):
    distance = lax.rem(distance + 4, 4)
    return jnp.where(distance == 3, 1, jnp.where(distance == 0, 0, distance + 1))


def attend_kernel(offset, lengths, q_ref, kv_ref, out_ref, top_ref, sum_ref, acc_ref):
    place = lax.axis_index("ctx")
    y, z = place // 4, lax.rem(place, 4)
    block = lax.rem(y + offset + 4, 4) * 4 + z
    scale = math.log2(math.e) / math.sqrt(HDIM)
    places = block * TOKENS + lax.broadcasted_iota(jnp.int32, (1, TOKENS), 1)
    starts = jnp.zeros((1, TOKENS), jnp.int32)
    first = jnp.int32(0)
    end = jnp.int32(0)
    for d in range(8):
        end = end + lengths[0, d]
        starts = jnp.maximum(starts, jnp.where(places >= end, end, 0))
        first = jnp.maximum(first, jnp.where(block * TOKENS >= end, end, 0))
    top_ref[...] = jnp.full_like(top_ref, NEGATIVE)
    sum_ref[...] = jnp.zeros_like(sum_ref)
    acc_ref[...] = jnp.zeros_like(acc_ref)
    rows = lax.broadcasted_iota(jnp.int32, (TOKENS, TOKENS), 0)

    def step(chunk, carry):
        slot = ring_slot(lax.rem(chunk, 4) - z) * 4 + ring_slot(chunk // 4 - y)
        keys = kv_ref[slot, :TOKENS, :HDIM]
        values = kv_ref[slot, :TOKENS, HDIM:].T
        key_places = chunk * TOKENS + rows
        allowed = (key_places <= places) & (key_places >= starts)
        bias = jnp.where(allowed, 0.0, NEGATIVE).astype(jnp.float32)
        bias = jnp.concatenate([bias, bias], axis=1)
        for pair in range(HEADS_HERE // 2):
            h = 2 * pair * HDIM
            q = jnp.concatenate([q_ref[:, h : h + HDIM], q_ref[:, h + HDIM : h + 2 * HDIM]], axis=0)
            s = lax.dot_general(
                keys, q, (((1,), (1,)), ((), ())), preferred_element_type=jnp.float32
            )
            s = s * scale + bias
            old = top_ref[pair]
            top = jnp.maximum(old, jnp.max(s, axis=0, keepdims=True))
            weights = jnp.exp2(s - top)
            fade = jnp.exp2(old - top)
            top_ref[pair] = top
            sum_ref[pair] = sum_ref[pair] * fade + jnp.sum(weights, axis=0, keepdims=True)
            acc_ref[pair] = acc_ref[pair] * fade + jnp.dot(
                values, weights.astype(jnp.bfloat16), preferred_element_type=jnp.float32
            )
        return carry

    lax.fori_loop(first // TOKENS, block + 1, step, 0)
    for pair in range(HEADS_HERE // 2):
        h = 2 * pair * HDIM
        mixed = (acc_ref[pair] / sum_ref[pair]).T.astype(jnp.bfloat16)
        out_ref[:, h : h + HDIM] = mixed[:TOKENS]
        out_ref[:, h + HDIM : h + 2 * HDIM] = mixed[TOKENS:]


def attend(offset, lengths, queries, kv):
    vmem = pl.BlockSpec(memory_space=pltpu.VMEM)
    return pl.pallas_call(
        functools.partial(attend_kernel, offset),
        out_shape=jax.ShapeDtypeStruct((TOKENS, WIDTH), jnp.bfloat16),
        in_specs=[pl.BlockSpec(memory_space=pltpu.SMEM), vmem, vmem],
        out_specs=vmem,
        scratch_shapes=[
            pltpu.VMEM((8, 1, 256), jnp.float32),
            pltpu.VMEM((8, 1, 256), jnp.float32),
            pltpu.VMEM((8, HDIM, 256), jnp.float32),
        ],
        compiler_params=pltpu.CompilerParams(vmem_limit_bytes=8 * 2**20),
        cost_estimate=pl.CostEstimate(
            flops=4 * 2**30, bytes_accessed=3 * 2**20, transcendentals=2048 * 640
        ),
        name="attend",
    )(lengths, queries, kv)


def project_kernel(count, *refs):
    att, own, other = refs[0:count], refs[count : count + 4], refs[count + 4 : count + 8]
    outs = refs[count + 8 :]
    x, core = lax.axis_index("dp"), lax.axis_index("pair")
    z = lax.rem(lax.axis_index("ctx"), 4)

    def run(stacks):
        for i in range(4):
            column = lax.rem(x + OFFSETS[i] + 4, 4) * 512
            total = None
            for half in range(2):
                for j in range(4):
                    place = lax.rem(z + OFFSETS[j] + 4, 4) * 512 + half * 256
                    place = pl.ds(pl.multiple_of(place, 256), 256)
                    left = jnp.concatenate([a[:, place] for a in att], axis=0)
                    right = stacks[0][j][i] if half == 0 else stacks[1][i][j]
                    term = jnp.dot(left, right, preferred_element_type=jnp.float32)
                    total = term if total is None else total + term
            total = total.astype(jnp.bfloat16)
            for n in range(count):
                part = total[n * TOKENS : (n + 1) * TOKENS]
                outs[n][:, pl.ds(pl.multiple_of(column, 512), 512)] = part

    @pl.when(core == 0)
    def _():
        run((own, other))

    @pl.when(core == 1)
    def _():
        run((other, own))


def project(attended, own, other):
    vmem = pl.BlockSpec(memory_space=pltpu.VMEM)
    count = len(attended)
    return pl.pallas_call(
        functools.partial(project_kernel, count),
        out_shape=[jax.ShapeDtypeStruct((TOKENS, WIDTH), jnp.bfloat16)] * count,
        in_specs=[vmem] * (count + 8),
        out_specs=[vmem] * count,
        compiler_params=pltpu.CompilerParams(vmem_limit_bytes=14 * 2**20),
        cost_estimate=pl.CostEstimate(
            flops=2 * count * TOKENS * 2048 * 2048,
            bytes_accessed=(8 + count) * 2**20,
            transcendentals=0,
        ),
        name="project",
    )(*attended, *own, *other)


def pieces_of(blocks, cols):
    return [
        jnp.concatenate([blocks[2 * p][:, cols], blocks[2 * p + 1][:, cols]], axis=0)
        for p in range(2)
    ]


def dispatch_kernel(*refs):
    blocks, pick_ref, outs = refs[:4], refs[4], refs[5:]
    for n in range(4):
        cols = pl.ds(n * 512, 512)
        pieces = pieces_of(blocks, cols)
        for chip, out in enumerate(outs):
            for p in range(2):
                rows = jnp.dot(pick_ref[chip, p], pieces[p], preferred_element_type=jnp.float32)
                rows = rows.astype(jnp.bfloat16).reshape(4, SLOTS, 512)
                out[:, p * SLOTS : (p + 1) * SLOTS, cols] = rows


def dispatch(blocks, pick):
    vmem = pl.BlockSpec(memory_space=pltpu.VMEM)
    chips = pick.shape[0]
    return pl.pallas_call(
        dispatch_kernel,
        out_shape=[jax.ShapeDtypeStruct((4, 2 * SLOTS, WIDTH), jnp.bfloat16)] * chips,
        in_specs=[vmem] * 5,
        out_specs=[vmem] * chips,
        compiler_params=pltpu.CompilerParams(vmem_limit_bytes=12 * 2**20),
        cost_estimate=pl.CostEstimate(
            flops=2 * chips * 384 * 256 * 2048, bytes_accessed=6 * 2**20, transcendentals=0
        ),
        name="dispatch",
    )(*blocks, pick)


def combine_kernel(chips, last, *refs):
    sources, put_ref, refs = refs[:chips], refs[chips], refs[chips + 1 :]
    for n in range(4):
        cols = pl.ds(n * 512, 512)
        for p in range(2):
            rows = [
                source[e, p * SLOTS : (p + 1) * SLOTS, cols] for source in sources for e in range(4)
            ]
            mixed = jnp.dot(
                put_ref[p], jnp.concatenate(rows, axis=0), preferred_element_type=jnp.float32
            )
            for half in range(2):
                part = mixed[half * TOKENS : (half + 1) * TOKENS]
                if not last:
                    refs[0][2 * p + half, :, cols] = part
                    continue
                part = part + refs[0][2 * p + half, :, cols]
                out = refs[1 + 2 * p + half]
                out[:, cols] = part.astype(out.dtype)


def combine(sources, put, earlier=None):
    vmem = pl.BlockSpec(memory_space=pltpu.VMEM)
    last = earlier is not None
    if last:
        shapes = [jax.ShapeDtypeStruct((TOKENS, WIDTH), jnp.float32)]
        shapes += [jax.ShapeDtypeStruct((TOKENS, WIDTH), jnp.bfloat16)] * 3
    else:
        shapes = [jax.ShapeDtypeStruct((4, TOKENS, WIDTH), jnp.float32)]
    operands = [*sources, put] + ([earlier] if last else [])
    return pl.pallas_call(
        functools.partial(combine_kernel, len(sources), last),
        out_shape=shapes,
        in_specs=[vmem] * len(operands),
        out_specs=[vmem] * len(shapes),
        compiler_params=pltpu.CompilerParams(vmem_limit_bytes=16 * 2**20),
        cost_estimate=pl.CostEstimate(
            flops=2 * len(sources) * 384 * 256 * 2048, bytes_accessed=8 * 2**20, transcendentals=0
        ),
        name="combine",
    )(*operands)


def experts_kernel(count, *refs):
    sources, refs = refs[:count], refs[count:]
    hbm, refs = refs[:6], refs[6:]
    outs, refs = refs[:count], refs[count:]
    act_ref, gate_buf, up_buf, down_buf, sems = refs
    buffers = (gate_buf, up_buf, down_buf)

    def copies(e):
        side, index, slot = e // 2, e % 2, e % 2
        return [
            pltpu.make_async_copy(
                hbm[3 * side + w].at[index], buffers[w].at[slot], sems.at[w, slot]
            )
            for w in range(3)
        ]

    for e in range(2):
        for c in copies(e):
            c.start()
    for e in range(4):
        slot = e % 2
        waits = copies(e)
        waits[0].wait()
        waits[1].wait()
        rows = jnp.concatenate([source[e] for source in sources], axis=0)
        for n in range(3):
            cols = pl.ds(n * 256, 256)
            gate = jnp.dot(rows, gate_buf[slot, :, cols], preferred_element_type=jnp.float32)
            upward = jnp.dot(rows, up_buf[slot, :, cols], preferred_element_type=jnp.float32)
            act_ref[:, cols] = (gate / (1.0 + jnp.exp(-gate)) * upward).astype(jnp.bfloat16)
        waits[2].wait()
        active = act_ref[...]
        for n in range(4):
            cols = pl.ds(n * 512, 512)
            result = jnp.dot(active, down_buf[slot, :, cols], preferred_element_type=jnp.float32)
            result = result.astype(jnp.bfloat16)
            for i, out in enumerate(outs):
                out[e, :, cols] = result[i * 2 * SLOTS : (i + 1) * 2 * SLOTS]
        if e + 2 < 4:
            for c in copies(e + 2):
                c.start()


def experts(sources, mine, others):
    count = len(sources)
    vmem = pl.BlockSpec(memory_space=pltpu.VMEM)
    hbm = pl.BlockSpec(memory_space=pltpu.HBM)
    rows = count * 4 * 2 * SLOTS
    return pl.pallas_call(
        functools.partial(experts_kernel, count),
        out_shape=[jax.ShapeDtypeStruct((4, 2 * SLOTS, WIDTH), jnp.bfloat16)] * count,
        in_specs=[vmem] * count + [hbm] * 6,
        out_specs=[vmem] * count,
        scratch_shapes=[
            pltpu.VMEM((count * 2 * SLOTS, FFE), jnp.bfloat16),
            pltpu.VMEM((2, WIDTH, FFE), jnp.bfloat16),
            pltpu.VMEM((2, WIDTH, FFE), jnp.bfloat16),
            pltpu.VMEM((2, FFE, WIDTH), jnp.bfloat16),
            pltpu.SemaphoreType.DMA((3, 2)),
        ],
        compiler_params=pltpu.CompilerParams(vmem_limit_bytes=40 * 2**20),
        cost_estimate=pl.CostEstimate(
            flops=6 * rows * 2048 * 768,
            bytes_accessed=(36 + 3 * count) * 2**20,
            transcendentals=rows * 768,
        ),
        name="experts",
    )(*sources, *mine, *others)


def routing(meta, y, z, core):
    meta = jnp.where(core == 0, meta[0], meta[:, 0]).astype(jnp.float32)
    meta = meta.reshape(2, 2, 32, TOKENS).transpose(0, 2, 1, 3).reshape(2, 32, 2 * TOKENS)
    ids = meta[:, :8]
    route = meta[:, 8:16] + meta[:, 16:24] + meta[:, 24:32]
    index = jnp.arange(16, dtype=jnp.int32)
    chip, expert = index // 4, index % 4
    across = jnp.where(chip == 3, 2, jnp.where(chip == 2, 1, -chip))
    on_y, on_z = jnp.where(core == 0, 0, across), jnp.where(core == 0, across, 0)
    chip = (y + on_y + 4) % 4 * 4 + (z + on_z + 4) % 4
    wanted = chip * 4 + (expert + 2 * core) % 4
    same = ids[:, None] == wanted.astype(jnp.float32)[None, :, None, None]
    chosen = jnp.any(same, axis=2)
    share = jnp.sum(jnp.where(same, route[:, None], 0.0), axis=2)
    places = jnp.arange(2 * TOKENS, dtype=jnp.int32)
    before = (places[:, None] < places[None, :]).astype(jnp.bfloat16)
    rank = jnp.einsum(
        "pet,tu->peu", chosen.astype(jnp.bfloat16), before, preferred_element_type=jnp.float32
    )
    rank = jnp.where(chosen, rank, -1.0).astype(jnp.bfloat16)
    share = share.astype(jnp.bfloat16)
    slots = jnp.arange(SLOTS, dtype=jnp.bfloat16)
    pick = (rank[:, :, None] == slots[None, None, :, None]).astype(jnp.bfloat16)
    pick = pick.reshape(2, 4, 4 * SLOTS, 2 * TOKENS).transpose(1, 0, 2, 3)
    by_slot = lambda v: jnp.repeat(v.transpose(0, 2, 1), SLOTS, axis=2)
    slots = jnp.tile(slots, 16)
    put = jnp.where(by_slot(rank) == slots, by_slot(share), jnp.bfloat16(0))
    return pick, put


def after(value, *others):
    return lax.optimization_barrier((value, *others))[0]


def body(
    queries,
    keys,
    values,
    residual,
    doc_lengths,
    expert_ids,
    route_weights,
    out_weight,
    norm_gain,
    expert_gate,
    expert_up,
    expert_down,
):
    f32 = jnp.float32
    x, core = lax.axis_index("dp"), lax.axis_index("pair")
    y, z = lax.axis_index("ctx") // 4, lax.axis_index("ctx") % 4
    yy, zz = ("y", "y"), ("z", "z")
    queries, keys, values = queries[0], keys[0], values[0]

    route = route_weights[0].T
    high = lax.reduce_precision(route, 8, 7)
    middle = lax.reduce_precision(route - high, 8, 7)
    low = route - high - middle
    meta = jnp.concatenate([expert_ids[0].T.astype(f32), high, middle, low])
    meta = meta.astype(jnp.bfloat16)
    meta = jnp.concatenate([meta[:16], meta[16:]], axis=1)

    def kv_of(head):
        pair = jnp.concatenate(
            [
                lax.dynamic_slice_in_dim(keys, head * HDIM, HDIM, 1),
                lax.dynamic_slice_in_dim(values, head * HDIM, HDIM, 1),
            ],
            axis=1,
        )
        return jnp.concatenate([pair, meta])

    kv_to = [kv_of((y - o + 4) % 4) for o in OFFSETS]
    kv_y = kv_to[:1] + [shift(kv_to[k], yy, -OFFSETS[k]) for k in (1, 2, 3)]
    column = jnp.stack(kv_y)
    kv_z = [column] + [shift(column, zz, -o) for o in OFFSETS[1:]]
    kv = jnp.concatenate(kv_z)

    part = lax.dynamic_slice_in_dim(out_weight, core * 256, 256, 0)
    part = after(part, *kv_to)
    inner = jnp.stack([part] + [shift(part, ("x", "z"), -o) for o in OFFSETS[1:]])
    own = [inner] + [shift(inner, ("z", "x"), -o) for o in OFFSETS[1:3]]
    own.append(shift(after(inner, kv_z[1], kv_z[2]), ("z", "x"), -OFFSETS[3]))

    def queries_of(group):
        return lax.dynamic_slice_in_dim(queries, group * WIDTH, WIDTH, 1)

    blocks = [queries_of(y), None, None, shift(queries_of((y + 2) % 4), yy, -2)]
    for k in (1, 2):
        o = OFFSETS[k]
        near = after(queries_of((y - o + 4) % 4), blocks[3], kv)
        blocks[k] = shift(near, yy, -o)

    def attended(k):
        return attend(OFFSETS[k], doc_lengths, blocks[k], kv)

    last = blocks[2]
    blocks[2] = after(last, own[1], own[2])
    mixed = [attended(k) for k in range(4)]
    other = [swap(after(w, mixed[0], mixed[3], mixed[1], last)) for w in own[:3]]
    other.append(swap(after(own[3], mixed[2])))

    far, below, above, here = project([mixed[3], mixed[1], mixed[2], mixed[0]], own, other)

    weights = [expert_gate, expert_up, expert_down]
    swapped = [swap(after(expert_gate, far)), swap(after(expert_up, far))]

    terms = [here, shift(below, yy, -1), shift(above, yy, 1), shift(far, yy, 2)]
    meta = after(kv[:, TOKENS:], terms[3])
    meta = jnp.concatenate([meta[:, :, :TOKENS], meta[:, :, TOKENS:]], axis=1)
    pick, put = routing(meta.reshape(4, 4, 32, TOKENS), y, z, core)

    terms[1] = after(terms[1], pick, put)
    hidden = residual[0].astype(f32) + sum(t.astype(f32) for t in terms)
    mean_square = jnp.mean(hidden * hidden, axis=-1, keepdims=True)
    normed = (hidden * lax.rsqrt(mean_square + EPSILON) * norm_gain).astype(jnp.bfloat16)
    normed = after(normed, *swapped)
    swapped.append(swap(after(expert_down, normed)))

    prim, sec = ("y", "z"), ("z", "y")
    line = [normed] + [shift(normed, prim, -o) for o in OFFSETS[1:]]
    below, above = dispatch(line, pick[1:3])
    here, far = dispatch(line, jnp.stack([pick[0], pick[3]]))
    below, above = shift(below, sec, -1), shift(above, sec, 1)
    rest = (weights, swapped)
    (here,) = experts([here], *rest)
    far = shift(after(far, here, below, above), sec, 2)
    below, above = experts([below, above], *rest)
    (far,) = experts([after(far, below)], *rest)

    below, above = shift(below, sec, 1), shift(above, sec, -1)
    (near,) = combine([here, below, above], put[:, :, : 12 * SLOTS])
    parts = combine([shift(far, sec, 2)], put[:, :, 12 * SLOTS :], near)
    total = hidden + parts[0]
    for k in range(1, 4):
        total = total + shift(parts[k], prim, OFFSETS[k]).astype(f32)
    return total.astype(jnp.bfloat16)[None]


def solution(mesh):
    return jax.shard_map(
        body,
        mesh=mesh,
        in_specs=(
            P(("dp", "pair"), "ctx", None),
            P(("dp", "pair"), "ctx", None),
            P(("dp", "pair"), "ctx", None),
            P(("dp", "pair"), "ctx", None),
            P(("dp", "pair"), None),
            P(("dp", "pair"), "ctx", None),
            P(("dp", "pair"), "ctx", None),
            P("ctx", "dp"),
            P(),
            P(("ctx", "pair"), None, None),
            P(("ctx", "pair"), None, None),
            P(("ctx", "pair"), None, None),
        ),
        out_specs=P(("dp", "pair"), "ctx", None),
        check_vma=False,
    )
```

```python
import functools
import math

import jax
import jax.numpy as jnp
from jax import lax
from jax.experimental import pallas as pl
from jax.experimental.pallas import tpu as pltpu
from jax.sharding import PartitionSpec as P

RING = 4
TOKENS = 128
WIDTH = 2048
HDIM = 128
HEADS_HERE = 16
FFE = 768
SLOTS = 48
EPSILON = 1e-06
NEGATIVE = -1e30
OFFSETS = (0, -1, 1, 2)
AXES = ("dp", "ctx", "pair")


def shift(value, axes, distance):
    pairs = []
    for x in range(RING):
        for y in range(RING):
            for z in range(RING):
                for core in range(2):
                    to = {"x": x, "y": y, "z": z}
                    to[axes[core]] = (to[axes[core]] + distance) % RING
                    pairs.append(
                        (
                            (x * 16 + y * 4 + z) * 2 + core,
                            (to["x"] * 16 + to["y"] * 4 + to["z"]) * 2 + core,
                        )
                    )
    return lax.ppermute(value, AXES, pairs)


def swap(value):
    return lax.ppermute(value, "pair", [(0, 1), (1, 0)])


def ring_slot(distance):
    distance = lax.rem(distance + 4, 4)
    return jnp.where(distance == 3, 1, jnp.where(distance == 0, 0, distance + 1))


def attend_kernel(offset, lengths, q_ref, kv_ref, out_ref, turned_ref, top_ref, sum_ref, acc_ref):
    place = lax.axis_index("ctx")
    y, z = place // 4, lax.rem(place, 4)
    block = lax.rem(y + offset + 4, 4) * 4 + z
    scale = math.log2(math.e) / math.sqrt(HDIM)
    places = block * TOKENS + lax.broadcasted_iota(jnp.int32, (1, TOKENS), 1)
    starts = jnp.zeros((1, TOKENS), jnp.int32)
    first = jnp.int32(0)
    end = jnp.int32(0)
    for d in range(8):
        end = end + lengths[0, d]
        starts = jnp.maximum(starts, jnp.where(places >= end, end, 0))
        first = jnp.maximum(first, jnp.where(block * TOKENS >= end, end, 0))
    top_ref[...] = jnp.full_like(top_ref, NEGATIVE)
    sum_ref[...] = jnp.zeros_like(sum_ref)
    acc_ref[...] = jnp.zeros_like(acc_ref)
    rows = lax.broadcasted_iota(jnp.int32, (TOKENS, TOKENS), 0)
    for head in range(HEADS_HERE):
        h = head * HDIM
        turned_ref[:, h : h + HDIM] = q_ref[:, h : h + HDIM].T

    def step(chunk, carry):
        slot = ring_slot(lax.rem(chunk, 4) - z) * 4 + ring_slot(chunk // 4 - y)
        keys = kv_ref[slot, :TOKENS, :HDIM]
        values = kv_ref[slot, :TOKENS, HDIM:].T
        key_places = chunk * TOKENS + rows
        allowed = (key_places <= places) & (key_places >= starts)
        bias = jnp.where(allowed, 0.0, NEGATIVE).astype(jnp.float32)
        bias = jnp.concatenate([bias, bias], axis=1)
        for pair in range(HEADS_HERE // 2):
            h = 2 * pair * HDIM
            q = turned_ref[:, h : h + 2 * HDIM]
            s = jnp.dot(keys, q, preferred_element_type=jnp.float32)
            s = s * scale + bias
            old = top_ref[pair]
            top = jnp.maximum(old, jnp.max(s, axis=0, keepdims=True))
            weights = jnp.exp2(s - top)
            fade = jnp.exp2(old - top)
            top_ref[pair] = top
            sum_ref[pair] = sum_ref[pair] * fade + jnp.sum(weights, axis=0, keepdims=True)
            acc_ref[pair] = acc_ref[pair] * fade + jnp.dot(
                values, weights.astype(jnp.bfloat16), preferred_element_type=jnp.float32
            )
        return carry

    lax.fori_loop(first // TOKENS, block + 1, step, 0)
    for pair in range(HEADS_HERE // 2):
        h = 2 * pair * HDIM
        mixed = (acc_ref[pair] / sum_ref[pair]).T.astype(jnp.bfloat16)
        out_ref[:, h : h + HDIM] = mixed[:TOKENS]
        out_ref[:, h + HDIM : h + 2 * HDIM] = mixed[TOKENS:]


def attend(offset, lengths, queries, kv):
    vmem = pl.BlockSpec(memory_space=pltpu.VMEM)
    return pl.pallas_call(
        functools.partial(attend_kernel, offset),
        out_shape=jax.ShapeDtypeStruct((TOKENS, WIDTH), jnp.bfloat16),
        in_specs=[pl.BlockSpec(memory_space=pltpu.SMEM), vmem, vmem],
        out_specs=vmem,
        scratch_shapes=[
            pltpu.VMEM((HDIM, WIDTH), jnp.bfloat16),
            pltpu.VMEM((8, 1, 256), jnp.float32),
            pltpu.VMEM((8, 1, 256), jnp.float32),
            pltpu.VMEM((8, HDIM, 256), jnp.float32),
        ],
        compiler_params=pltpu.CompilerParams(vmem_limit_bytes=8 * 2**20),
        cost_estimate=pl.CostEstimate(
            flops=4 * 2**30, bytes_accessed=3 * 2**20, transcendentals=2048 * 640
        ),
        name="attend",
    )(lengths, queries, kv)


def project_kernel(count, *refs):
    att, own, other = refs[0:count], refs[count : count + 4], refs[count + 4 : count + 8]
    outs = refs[count + 8 :]
    x, core = lax.axis_index("dp"), lax.axis_index("pair")
    z = lax.rem(lax.axis_index("ctx"), 4)

    def run(stacks):
        for i in range(4):
            column = lax.rem(x + OFFSETS[i] + 4, 4) * 512
            total = None
            for half in range(2):
                for j in range(4):
                    place = lax.rem(z + OFFSETS[j] + 4, 4) * 512 + half * 256
                    place = pl.ds(pl.multiple_of(place, 256), 256)
                    left = jnp.concatenate([a[:, place] for a in att], axis=0)
                    right = stacks[0][j][i] if half == 0 else stacks[1][i][j]
                    term = jnp.dot(left, right, preferred_element_type=jnp.float32)
                    total = term if total is None else total + term
            total = total.astype(jnp.bfloat16)
            for n in range(count):
                part = total[n * TOKENS : (n + 1) * TOKENS]
                outs[n][:, pl.ds(pl.multiple_of(column, 512), 512)] = part

    @pl.when(core == 0)
    def _():
        run((own, other))

    @pl.when(core == 1)
    def _():
        run((other, own))


def project(attended, own, other):
    vmem = pl.BlockSpec(memory_space=pltpu.VMEM)
    count = len(attended)
    return pl.pallas_call(
        functools.partial(project_kernel, count),
        out_shape=[jax.ShapeDtypeStruct((TOKENS, WIDTH), jnp.bfloat16)] * count,
        in_specs=[vmem] * (count + 8),
        out_specs=[vmem] * count,
        compiler_params=pltpu.CompilerParams(vmem_limit_bytes=14 * 2**20),
        cost_estimate=pl.CostEstimate(
            flops=2 * count * TOKENS * 2048 * 2048,
            bytes_accessed=(8 + count) * 2**20,
            transcendentals=0,
        ),
        name="project",
    )(*attended, *own, *other)


def pieces_of(blocks, cols):
    return [
        jnp.concatenate([blocks[2 * p][:, cols], blocks[2 * p + 1][:, cols]], axis=0)
        for p in range(2)
    ]


def dispatch_kernel(splits, *refs):
    blocks, pick_ref, outs = refs[:4], refs[4], refs[5:]
    for n in range(4):
        cols = pl.ds(n * 512, 512)
        pieces = pieces_of(blocks, cols)
        for (chip, first, count), out in zip(splits, outs):
            some = pl.ds(first * SLOTS, count * SLOTS)
            for p in range(2):
                rows = jnp.dot(
                    pick_ref[chip, p, some], pieces[p], preferred_element_type=jnp.float32
                )
                rows = rows.astype(jnp.bfloat16).reshape(count, SLOTS, 512)
                out[:, p * SLOTS : (p + 1) * SLOTS, cols] = rows


def dispatch(blocks, pick, splits):
    vmem = pl.BlockSpec(memory_space=pltpu.VMEM)
    chips = pick.shape[0]
    return pl.pallas_call(
        functools.partial(dispatch_kernel, splits),
        out_shape=[
            jax.ShapeDtypeStruct((count, 2 * SLOTS, WIDTH), jnp.bfloat16) for _, _, count in splits
        ],
        in_specs=[vmem] * 5,
        out_specs=[vmem] * len(splits),
        compiler_params=pltpu.CompilerParams(vmem_limit_bytes=12 * 2**20),
        cost_estimate=pl.CostEstimate(
            flops=2 * chips * 384 * 256 * 2048, bytes_accessed=6 * 2**20, transcendentals=0
        ),
        name="dispatch",
    )(*blocks, pick)


def combine_kernel(chips, more, last, *refs):
    sources, put_ref, refs = refs[:chips], refs[chips], refs[chips + 1 :]
    earlier, outs = refs[:more], refs[more:]
    for n in range(4):
        cols = pl.ds(n * 512, 512)
        for p in range(2):
            rows = [
                source[e, p * SLOTS : (p + 1) * SLOTS, cols]
                for source in sources
                for e in range(source.shape[0])
            ]
            mixed = jnp.dot(
                put_ref[p], jnp.concatenate(rows, axis=0), preferred_element_type=jnp.float32
            )
            for half in range(2):
                part = mixed[half * TOKENS : (half + 1) * TOKENS]
                for ref in earlier:
                    part = part + ref[2 * p + half, :, cols]
                if last:
                    out = outs[2 * p + half]
                    out[:, cols] = part.astype(out.dtype)
                else:
                    outs[0][2 * p + half, :, cols] = part


def combine(sources, put, earlier=(), last=False):
    vmem = pl.BlockSpec(memory_space=pltpu.VMEM)
    if last:
        shapes = [jax.ShapeDtypeStruct((TOKENS, WIDTH), jnp.float32)]
        shapes += [jax.ShapeDtypeStruct((TOKENS, WIDTH), jnp.bfloat16)] * 3
    else:
        shapes = [jax.ShapeDtypeStruct((4, TOKENS, WIDTH), jnp.float32)]
    operands = [*sources, put, *earlier]
    return pl.pallas_call(
        functools.partial(combine_kernel, len(sources), len(earlier), last),
        out_shape=shapes,
        in_specs=[vmem] * len(operands),
        out_specs=[vmem] * len(shapes),
        compiler_params=pltpu.CompilerParams(vmem_limit_bytes=20 * 2**20),
        cost_estimate=pl.CostEstimate(
            flops=2 * len(sources) * 384 * 256 * 2048, bytes_accessed=8 * 2**20, transcendentals=0
        ),
        name="combine",
    )(*operands)


def experts_kernel(count, sets, *refs):
    sources, refs = refs[:count], refs[count:]
    hbm, refs = refs[: 3 * sets], refs[3 * sets :]
    outs, refs = refs[:count], refs[count:]
    act_ref, gate_buf, up_buf, down_buf, sems = refs
    buffers = (gate_buf, up_buf, down_buf)

    def copies(e):
        side, index, slot = e // 2, e % 2, e % 2
        return [
            pltpu.make_async_copy(
                hbm[3 * side + w].at[index], buffers[w].at[slot], sems.at[w, slot]
            )
            for w in range(3)
        ]

    for e in range(2):
        for c in copies(e):
            c.start()
    for e in range(2 * sets):
        slot = e % 2
        waits = copies(e)
        waits[0].wait()
        waits[1].wait()
        rows = jnp.concatenate([source[e] for source in sources], axis=0)
        for n in range(3):
            cols = pl.ds(n * 256, 256)
            gate = jnp.dot(rows, gate_buf[slot, :, cols], preferred_element_type=jnp.float32)
            upward = jnp.dot(rows, up_buf[slot, :, cols], preferred_element_type=jnp.float32)
            act_ref[:, cols] = (gate / (1.0 + jnp.exp(-gate)) * upward).astype(jnp.bfloat16)
        waits[2].wait()
        active = act_ref[...]
        for n in range(4):
            cols = pl.ds(n * 512, 512)
            result = jnp.dot(active, down_buf[slot, :, cols], preferred_element_type=jnp.float32)
            result = result.astype(jnp.bfloat16)
            for i, out in enumerate(outs):
                out[e, :, cols] = result[i * 2 * SLOTS : (i + 1) * 2 * SLOTS]
        if e + 2 < 2 * sets:
            for c in copies(e + 2):
                c.start()


def experts(sources, *weights):
    count, sets = len(sources), len(weights)
    vmem = pl.BlockSpec(memory_space=pltpu.VMEM)
    hbm = pl.BlockSpec(memory_space=pltpu.HBM)
    rows = count * sets * 4 * SLOTS
    return pl.pallas_call(
        functools.partial(experts_kernel, count, sets),
        out_shape=[jax.ShapeDtypeStruct((2 * sets, 2 * SLOTS, WIDTH), jnp.bfloat16)] * count,
        in_specs=[vmem] * count + [hbm] * (3 * sets),
        out_specs=[vmem] * count,
        scratch_shapes=[
            pltpu.VMEM((count * 2 * SLOTS, FFE), jnp.bfloat16),
            pltpu.VMEM((2, WIDTH, FFE), jnp.bfloat16),
            pltpu.VMEM((2, WIDTH, FFE), jnp.bfloat16),
            pltpu.VMEM((2, FFE, WIDTH), jnp.bfloat16),
            pltpu.SemaphoreType.DMA((3, 2)),
        ],
        compiler_params=pltpu.CompilerParams(vmem_limit_bytes=50 * 2**20),
        cost_estimate=pl.CostEstimate(
            flops=6 * rows * 2048 * 768,
            bytes_accessed=(18 + 2 * count) * sets * 2**20,
            transcendentals=rows * 768,
        ),
        name="experts",
    )(*sources, *[w for some in weights for w in some])


def routing(meta, y, z, core):
    meta = jnp.where(core == 0, meta[0], meta[:, 0]).astype(jnp.float32)
    meta = meta.reshape(2, 2, 32, TOKENS).transpose(0, 2, 1, 3).reshape(2, 32, 2 * TOKENS)
    ids = meta[:, :8]
    route = meta[:, 8:16] + meta[:, 16:24] + meta[:, 24:32]
    index = jnp.arange(16, dtype=jnp.int32)
    chip, expert = index // 4, index % 4
    across = jnp.where(chip == 3, 2, jnp.where(chip == 2, 1, -chip))
    on_y, on_z = jnp.where(core == 0, 0, across), jnp.where(core == 0, across, 0)
    chip = (y + on_y + 4) % 4 * 4 + (z + on_z + 4) % 4
    wanted = chip * 4 + (expert + 2 * core) % 4
    same = ids[:, None] == wanted.astype(jnp.float32)[None, :, None, None]
    chosen = jnp.any(same, axis=2)
    share = jnp.sum(jnp.where(same, route[:, None], 0.0), axis=2)
    places = jnp.arange(2 * TOKENS, dtype=jnp.int32)
    before = (places[:, None] < places[None, :]).astype(jnp.bfloat16)
    rank = jnp.einsum(
        "pet,tu->peu", chosen.astype(jnp.bfloat16), before, preferred_element_type=jnp.float32
    )
    rank = jnp.where(chosen, rank, -1.0).astype(jnp.bfloat16)
    share = share.astype(jnp.bfloat16)
    slots = jnp.arange(SLOTS, dtype=jnp.bfloat16)
    pick = (rank[:, :, None] == slots[None, None, :, None]).astype(jnp.bfloat16)
    pick = pick.reshape(2, 4, 4 * SLOTS, 2 * TOKENS).transpose(1, 0, 2, 3)
    by_slot = lambda v: jnp.repeat(v.transpose(0, 2, 1), SLOTS, axis=2)
    slots = jnp.tile(slots, 16)
    put = jnp.where(by_slot(rank) == slots, by_slot(share), jnp.bfloat16(0))
    return pick, put


def after(value, *others):
    return lax.optimization_barrier((value, *others))[0]


def body(
    queries,
    keys,
    values,
    residual,
    doc_lengths,
    expert_ids,
    route_weights,
    out_weight,
    norm_gain,
    expert_gate,
    expert_up,
    expert_down,
):
    f32 = jnp.float32
    x, core = lax.axis_index("dp"), lax.axis_index("pair")
    y, z = lax.axis_index("ctx") // 4, lax.axis_index("ctx") % 4
    yy, zz = ("y", "y"), ("z", "z")
    queries, keys, values = queries[0], keys[0], values[0]

    route = route_weights[0].T
    high = lax.reduce_precision(route, 8, 7)
    middle = lax.reduce_precision(route - high, 8, 7)
    low = route - high - middle
    meta = jnp.concatenate([expert_ids[0].T.astype(f32), high, middle, low])
    meta = meta.astype(jnp.bfloat16)
    meta = jnp.concatenate([meta[:16], meta[16:]], axis=1)

    def kv_of(head):
        pair = jnp.concatenate(
            [
                lax.dynamic_slice_in_dim(keys, head * HDIM, HDIM, 1),
                lax.dynamic_slice_in_dim(values, head * HDIM, HDIM, 1),
            ],
            axis=1,
        )
        return jnp.concatenate([pair, meta])

    kv_to = [kv_of((y - o + 4) % 4) for o in OFFSETS]
    kv_y = kv_to[:1] + [shift(kv_to[k], yy, -OFFSETS[k]) for k in (1, 2, 3)]
    column = jnp.stack(kv_y)
    kv_z = [column] + [shift(column, zz, -o) for o in OFFSETS[1:]]
    kv = jnp.concatenate(kv_z)

    part = lax.dynamic_slice_in_dim(out_weight, core * 256, 256, 0)
    part = after(part, *kv_to)
    inner = jnp.stack([part] + [shift(part, ("x", "z"), -o) for o in OFFSETS[1:]])
    own = [inner] + [shift(inner, ("z", "x"), -o) for o in OFFSETS[1:3]]
    own.append(shift(after(inner, kv_z[1], kv_z[2]), ("z", "x"), -OFFSETS[3]))

    def queries_of(group):
        return lax.dynamic_slice_in_dim(queries, group * WIDTH, WIDTH, 1)

    blocks = [queries_of(y), None, None, shift(queries_of((y + 2) % 4), yy, -2)]
    for k in (1, 2):
        o = OFFSETS[k]
        near = after(queries_of((y - o + 4) % 4), blocks[3], kv)
        blocks[k] = shift(near, yy, -o)

    def attended(k):
        return attend(OFFSETS[k], doc_lengths, blocks[k], kv)

    last = blocks[2]
    blocks[2] = after(last, own[1], own[2])
    mixed = [attended(k) for k in range(4)]
    other = [swap(after(w, mixed[0], mixed[3], mixed[1], last)) for w in own[:3]]
    other.append(swap(after(own[3], mixed[2])))

    far, below, above, here = project([mixed[3], mixed[1], mixed[2], mixed[0]], own, other)

    weights = [expert_gate, expert_up, expert_down]
    swapped = [swap(after(expert_gate, far)), swap(after(expert_up, far))]

    terms = [here, shift(below, yy, -1), shift(above, yy, 1), shift(far, yy, 2)]
    meta = after(kv[:, TOKENS:], terms[3])
    meta = jnp.concatenate([meta[:, :, :TOKENS], meta[:, :, TOKENS:]], axis=1)
    pick, put = routing(meta.reshape(4, 4, 32, TOKENS), y, z, core)

    terms[1] = after(terms[1], pick, put)
    hidden = residual[0].astype(f32) + sum(t.astype(f32) for t in terms)
    mean_square = jnp.mean(hidden * hidden, axis=-1, keepdims=True)
    normed = (hidden * lax.rsqrt(mean_square + EPSILON) * norm_gain).astype(jnp.bfloat16)
    normed = after(normed, *swapped)
    swapped.append(swap(after(expert_down, normed)))

    prim, sec = ("y", "z"), ("z", "y")
    line = [normed] + [shift(normed, prim, -o) for o in OFFSETS[1:]]
    below, above = dispatch(line, pick[1:3], ((0, 0, 4), (1, 0, 4)))
    here, *far = dispatch(
        line, jnp.stack([pick[0], pick[3]]), ((0, 0, 4), (1, 0, 2), (1, 2, 2))
    )
    below, above = shift(below, sec, -1), shift(above, sec, 1)
    rest = (weights, swapped)
    (here,) = experts([here], *rest)
    far = [shift(after(rows, here, below, above), sec, 2) for rows in far]
    below, above = experts([below, above], *rest)
    (far[0],) = experts([after(far[0], below)], weights)
    (far[1],) = experts([after(far[1], far[0])], swapped)

    below, above = shift(below, sec, 1), shift(above, sec, -1)
    near = combine([here, below, above], put[:, :, : 12 * SLOTS])
    far = [shift(rows, sec, 2) for rows in far]
    near = combine(far[:1], put[:, :, 12 * SLOTS : 14 * SLOTS], near)
    parts = combine(far[1:], put[:, :, 14 * SLOTS :], near, last=True)
    total = hidden + parts[0]
    for k in range(1, 4):
        total = total + shift(parts[k], prim, OFFSETS[k]).astype(f32)
    return total.astype(jnp.bfloat16)[None]


def solution(mesh):
    return jax.shard_map(
        body,
        mesh=mesh,
        in_specs=(
            P(("dp", "pair"), "ctx", None),
            P(("dp", "pair"), "ctx", None),
            P(("dp", "pair"), "ctx", None),
            P(("dp", "pair"), "ctx", None),
            P(("dp", "pair"), None),
            P(("dp", "pair"), "ctx", None),
            P(("dp", "pair"), "ctx", None),
            P("ctx", "dp"),
            P(),
            P(("ctx", "pair"), None, None),
            P(("ctx", "pair"), None, None),
            P(("ctx", "pair"), None, None),
        ),
        out_specs=P(("dp", "pair"), "ctx", None),
        check_vma=False,
    )
```

```python
import functools
import math

import jax
import jax.numpy as jnp
from jax import lax
from jax.experimental import pallas as pl
from jax.experimental.pallas import tpu as pltpu
from jax.sharding import PartitionSpec as P

RING = 4
TOKENS = 128
WIDTH = 2048
HDIM = 128
HEADS_HERE = 16
FFE = 768
SLOTS = 48
EPSILON = 1e-06
NEGATIVE = -1e30
OFFSETS = (0, -1, 1, 2)
AXES = ("dp", "ctx", "pair")


def shift(value, axes, distance):
    pairs = []
    for x in range(RING):
        for y in range(RING):
            for z in range(RING):
                for core in range(2):
                    to = {"x": x, "y": y, "z": z}
                    to[axes[core]] = (to[axes[core]] + distance) % RING
                    pairs.append(
                        (
                            (x * 16 + y * 4 + z) * 2 + core,
                            (to["x"] * 16 + to["y"] * 4 + to["z"]) * 2 + core,
                        )
                    )
    return lax.ppermute(value, AXES, pairs)


def swap(value):
    return lax.ppermute(value, "pair", [(0, 1), (1, 0)])


def ring_slot(distance):
    distance = lax.rem(distance + 4, 4)
    return jnp.where(distance == 3, 1, jnp.where(distance == 0, 0, distance + 1))


def attend_kernel(offset, lengths, q_ref, kv_ref, out_ref, turned_ref, top_ref, sum_ref, acc_ref):
    place = lax.axis_index("ctx")
    y, z = place // 4, lax.rem(place, 4)
    block = lax.rem(y + offset + 4, 4) * 4 + z
    scale = math.log2(math.e) / math.sqrt(HDIM)
    places = block * TOKENS + lax.broadcasted_iota(jnp.int32, (1, TOKENS), 1)
    starts = jnp.zeros((1, TOKENS), jnp.int32)
    first = jnp.int32(0)
    end = jnp.int32(0)
    for d in range(8):
        end = end + lengths[0, d]
        starts = jnp.maximum(starts, jnp.where(places >= end, end, 0))
        first = jnp.maximum(first, jnp.where(block * TOKENS >= end, end, 0))
    top_ref[...] = jnp.full_like(top_ref, NEGATIVE)
    sum_ref[...] = jnp.zeros_like(sum_ref)
    acc_ref[...] = jnp.zeros_like(acc_ref)
    rows = lax.broadcasted_iota(jnp.int32, (TOKENS, TOKENS), 0)
    for head in range(HEADS_HERE):
        h = head * HDIM
        turned_ref[:, h : h + HDIM] = q_ref[:, h : h + HDIM].T

    def step(chunk, carry):
        slot = ring_slot(lax.rem(chunk, 4) - z) * 4 + ring_slot(chunk // 4 - y)
        keys = kv_ref[slot, :TOKENS, :HDIM]
        values = kv_ref[slot, :TOKENS, HDIM:].T
        key_places = chunk * TOKENS + rows
        allowed = (key_places <= places) & (key_places >= starts)
        bias = jnp.where(allowed, 0.0, NEGATIVE).astype(jnp.float32)
        bias = jnp.concatenate([bias, bias], axis=1)
        for pair in range(HEADS_HERE // 2):
            h = 2 * pair * HDIM
            q = turned_ref[:, h : h + 2 * HDIM]
            s = jnp.dot(keys, q, preferred_element_type=jnp.float32)
            s = s * scale + bias
            old = top_ref[pair]
            top = jnp.maximum(old, jnp.max(s, axis=0, keepdims=True))
            weights = jnp.exp2(s - top)
            fade = jnp.exp2(old - top)
            top_ref[pair] = top
            sum_ref[pair] = sum_ref[pair] * fade + jnp.sum(weights, axis=0, keepdims=True)
            acc_ref[pair] = acc_ref[pair] * fade + jnp.dot(
                values, weights.astype(jnp.bfloat16), preferred_element_type=jnp.float32
            )
        return carry

    lax.fori_loop(first // TOKENS, block + 1, step, 0)
    for pair in range(HEADS_HERE // 2):
        h = 2 * pair * HDIM
        mixed = (acc_ref[pair] / sum_ref[pair]).T.astype(jnp.bfloat16)
        out_ref[:, h : h + HDIM] = mixed[:TOKENS]
        out_ref[:, h + HDIM : h + 2 * HDIM] = mixed[TOKENS:]


def attend(offset, lengths, queries, kv):
    vmem = pl.BlockSpec(memory_space=pltpu.VMEM)
    return pl.pallas_call(
        functools.partial(attend_kernel, offset),
        out_shape=jax.ShapeDtypeStruct((TOKENS, WIDTH), jnp.bfloat16),
        in_specs=[pl.BlockSpec(memory_space=pltpu.SMEM), vmem, vmem],
        out_specs=vmem,
        scratch_shapes=[
            pltpu.VMEM((HDIM, WIDTH), jnp.bfloat16),
            pltpu.VMEM((8, 1, 256), jnp.float32),
            pltpu.VMEM((8, 1, 256), jnp.float32),
            pltpu.VMEM((8, HDIM, 256), jnp.float32),
        ],
        compiler_params=pltpu.CompilerParams(vmem_limit_bytes=8 * 2**20),
        cost_estimate=pl.CostEstimate(
            flops=4 * 2**30, bytes_accessed=3 * 2**20, transcendentals=2048 * 640
        ),
        name="attend",
    )(lengths, queries, kv)


def project_kernel(count, *refs):
    att, own, other = refs[0:count], refs[count : count + 4], refs[count + 4 : count + 8]
    outs = refs[count + 8 :]
    x, core = lax.axis_index("dp"), lax.axis_index("pair")
    z = lax.rem(lax.axis_index("ctx"), 4)

    def run(stacks):
        for i in range(4):
            column = lax.rem(x + OFFSETS[i] + 4, 4) * 512
            total = None
            for half in range(2):
                for j in range(4):
                    place = lax.rem(z + OFFSETS[j] + 4, 4) * 512 + half * 256
                    place = pl.ds(pl.multiple_of(place, 256), 256)
                    left = jnp.concatenate([a[:, place] for a in att], axis=0)
                    right = stacks[0][j][i] if half == 0 else stacks[1][i][j]
                    term = jnp.dot(left, right, preferred_element_type=jnp.float32)
                    total = term if total is None else total + term
            total = total.astype(jnp.bfloat16)
            for n in range(count):
                part = total[n * TOKENS : (n + 1) * TOKENS]
                outs[n][:, pl.ds(pl.multiple_of(column, 512), 512)] = part

    @pl.when(core == 0)
    def _():
        run((own, other))

    @pl.when(core == 1)
    def _():
        run((other, own))


def project(attended, own, other):
    vmem = pl.BlockSpec(memory_space=pltpu.VMEM)
    count = len(attended)
    return pl.pallas_call(
        functools.partial(project_kernel, count),
        out_shape=[jax.ShapeDtypeStruct((TOKENS, WIDTH), jnp.bfloat16)] * count,
        in_specs=[vmem] * (count + 8),
        out_specs=[vmem] * count,
        compiler_params=pltpu.CompilerParams(vmem_limit_bytes=14 * 2**20),
        cost_estimate=pl.CostEstimate(
            flops=2 * count * TOKENS * 2048 * 2048,
            bytes_accessed=(8 + count) * 2**20,
            transcendentals=0,
        ),
        name="project",
    )(*attended, *own, *other)


def pieces_of(blocks, cols):
    return [
        jnp.concatenate([blocks[2 * p][:, cols], blocks[2 * p + 1][:, cols]], axis=0)
        for p in range(2)
    ]


def dispatch_kernel(*refs):
    blocks, pick_ref, outs = refs[:4], refs[4], refs[5:]
    for n in range(4):
        cols = pl.ds(n * 512, 512)
        pieces = pieces_of(blocks, cols)
        for chip, out in enumerate(outs):
            for p in range(2):
                rows = jnp.dot(pick_ref[chip, p], pieces[p], preferred_element_type=jnp.float32)
                rows = rows.astype(jnp.bfloat16).reshape(4, SLOTS, 512)
                out[:, p * SLOTS : (p + 1) * SLOTS, cols] = rows


def dispatch(blocks, pick):
    vmem = pl.BlockSpec(memory_space=pltpu.VMEM)
    chips = pick.shape[0]
    return pl.pallas_call(
        dispatch_kernel,
        out_shape=[jax.ShapeDtypeStruct((4, 2 * SLOTS, WIDTH), jnp.bfloat16)] * chips,
        in_specs=[vmem] * 5,
        out_specs=[vmem] * chips,
        compiler_params=pltpu.CompilerParams(vmem_limit_bytes=12 * 2**20),
        cost_estimate=pl.CostEstimate(
            flops=2 * chips * 384 * 256 * 2048, bytes_accessed=6 * 2**20, transcendentals=0
        ),
        name="dispatch",
    )(*blocks, pick)


def combine_kernel(chips, last, *refs):
    sources, put_ref, refs = refs[:chips], refs[chips], refs[chips + 1 :]
    for n in range(4):
        cols = pl.ds(n * 512, 512)
        for p in range(2):
            rows = [
                source[e, p * SLOTS : (p + 1) * SLOTS, cols] for source in sources for e in range(4)
            ]
            mixed = jnp.dot(
                put_ref[p], jnp.concatenate(rows, axis=0), preferred_element_type=jnp.float32
            )
            for half in range(2):
                part = mixed[half * TOKENS : (half + 1) * TOKENS]
                if not last:
                    refs[0][2 * p + half, :, cols] = part
                    continue
                part = part + refs[0][2 * p + half, :, cols]
                out = refs[1 + 2 * p + half]
                out[:, cols] = part.astype(out.dtype)


def combine(sources, put, earlier=None):
    vmem = pl.BlockSpec(memory_space=pltpu.VMEM)
    last = earlier is not None
    if last:
        shapes = [jax.ShapeDtypeStruct((TOKENS, WIDTH), jnp.float32)]
        shapes += [jax.ShapeDtypeStruct((TOKENS, WIDTH), jnp.bfloat16)] * 3
    else:
        shapes = [jax.ShapeDtypeStruct((4, TOKENS, WIDTH), jnp.float32)]
    operands = [*sources, put] + ([earlier] if last else [])
    return pl.pallas_call(
        functools.partial(combine_kernel, len(sources), last),
        out_shape=shapes,
        in_specs=[vmem] * len(operands),
        out_specs=[vmem] * len(shapes),
        compiler_params=pltpu.CompilerParams(vmem_limit_bytes=16 * 2**20),
        cost_estimate=pl.CostEstimate(
            flops=2 * len(sources) * 384 * 256 * 2048, bytes_accessed=8 * 2**20, transcendentals=0
        ),
        name="combine",
    )(*operands)


def experts_kernel(count, *refs):
    sources, refs = refs[:count], refs[count:]
    hbm, refs = refs[:6], refs[6:]
    outs, refs = refs[:count], refs[count:]
    act_ref, gate_buf, up_buf, down_buf, sems = refs
    buffers = (gate_buf, up_buf, down_buf)

    def copies(e):
        side, index, slot = e // 2, e % 2, e % 2
        return [
            pltpu.make_async_copy(
                hbm[3 * side + w].at[index], buffers[w].at[slot], sems.at[w, slot]
            )
            for w in range(3)
        ]

    for e in range(2):
        for c in copies(e):
            c.start()
    for e in range(4):
        slot = e % 2
        waits = copies(e)
        waits[0].wait()
        waits[1].wait()
        rows = jnp.concatenate([source[e] for source in sources], axis=0)
        for n in range(3):
            cols = pl.ds(n * 256, 256)
            gate = jnp.dot(rows, gate_buf[slot, :, cols], preferred_element_type=jnp.float32)
            upward = jnp.dot(rows, up_buf[slot, :, cols], preferred_element_type=jnp.float32)
            act_ref[:, cols] = (gate / (1.0 + jnp.exp(-gate)) * upward).astype(jnp.bfloat16)
        waits[2].wait()
        active = act_ref[...]
        for n in range(4):
            cols = pl.ds(n * 512, 512)
            result = jnp.dot(active, down_buf[slot, :, cols], preferred_element_type=jnp.float32)
            result = result.astype(jnp.bfloat16)
            for i, out in enumerate(outs):
                out[e, :, cols] = result[i * 2 * SLOTS : (i + 1) * 2 * SLOTS]
        if e + 2 < 4:
            for c in copies(e + 2):
                c.start()


def experts(sources, mine, others):
    count = len(sources)
    vmem = pl.BlockSpec(memory_space=pltpu.VMEM)
    hbm = pl.BlockSpec(memory_space=pltpu.HBM)
    rows = count * 4 * 2 * SLOTS
    return pl.pallas_call(
        functools.partial(experts_kernel, count),
        out_shape=[jax.ShapeDtypeStruct((4, 2 * SLOTS, WIDTH), jnp.bfloat16)] * count,
        in_specs=[vmem] * count + [hbm] * 6,
        out_specs=[vmem] * count,
        scratch_shapes=[
            pltpu.VMEM((count * 2 * SLOTS, FFE), jnp.bfloat16),
            pltpu.VMEM((2, WIDTH, FFE), jnp.bfloat16),
            pltpu.VMEM((2, WIDTH, FFE), jnp.bfloat16),
            pltpu.VMEM((2, FFE, WIDTH), jnp.bfloat16),
            pltpu.SemaphoreType.DMA((3, 2)),
        ],
        compiler_params=pltpu.CompilerParams(vmem_limit_bytes=40 * 2**20),
        cost_estimate=pl.CostEstimate(
            flops=6 * rows * 2048 * 768,
            bytes_accessed=(36 + 3 * count) * 2**20,
            transcendentals=rows * 768,
        ),
        name="experts",
    )(*sources, *mine, *others)


def routing(meta, y, z, core):
    meta = jnp.where(core == 0, meta[0], meta[:, 0]).astype(jnp.float32)
    meta = meta.reshape(2, 2, 32, TOKENS).transpose(0, 2, 1, 3).reshape(2, 32, 2 * TOKENS)
    ids = meta[:, :8]
    route = meta[:, 8:16] + meta[:, 16:24] + meta[:, 24:32]
    index = jnp.arange(16, dtype=jnp.int32)
    chip, expert = index // 4, index % 4
    across = jnp.where(chip == 3, 2, jnp.where(chip == 2, 1, -chip))
    on_y, on_z = jnp.where(core == 0, 0, across), jnp.where(core == 0, across, 0)
    chip = (y + on_y + 4) % 4 * 4 + (z + on_z + 4) % 4
    wanted = chip * 4 + (expert + 2 * core) % 4
    same = ids[:, None] == wanted.astype(jnp.float32)[None, :, None, None]
    chosen = jnp.any(same, axis=2)
    share = jnp.sum(jnp.where(same, route[:, None], 0.0), axis=2)
    places = jnp.arange(2 * TOKENS, dtype=jnp.int32)
    before = (places[:, None] < places[None, :]).astype(jnp.bfloat16)
    rank = jnp.einsum(
        "pet,tu->peu", chosen.astype(jnp.bfloat16), before, preferred_element_type=jnp.float32
    )
    rank = jnp.where(chosen, rank, -1.0).astype(jnp.bfloat16)
    share = share.astype(jnp.bfloat16)
    slots = jnp.arange(SLOTS, dtype=jnp.bfloat16)
    pick = (rank[:, :, None] == slots[None, None, :, None]).astype(jnp.bfloat16)
    pick = pick.reshape(2, 4, 4 * SLOTS, 2 * TOKENS).transpose(1, 0, 2, 3)
    by_slot = lambda v: jnp.repeat(v.transpose(0, 2, 1), SLOTS, axis=2)
    slots = jnp.tile(slots, 16)
    put = jnp.where(by_slot(rank) == slots, by_slot(share), jnp.bfloat16(0))
    return pick, put


def after(value, *others):
    return lax.optimization_barrier((value, *others))[0]


def body(
    queries,
    keys,
    values,
    residual,
    doc_lengths,
    expert_ids,
    route_weights,
    out_weight,
    norm_gain,
    expert_gate,
    expert_up,
    expert_down,
):
    f32 = jnp.float32
    x, core = lax.axis_index("dp"), lax.axis_index("pair")
    y, z = lax.axis_index("ctx") // 4, lax.axis_index("ctx") % 4
    yy, zz = ("y", "y"), ("z", "z")
    queries, keys, values = queries[0], keys[0], values[0]

    route = route_weights[0].T
    high = lax.reduce_precision(route, 8, 7)
    middle = lax.reduce_precision(route - high, 8, 7)
    low = route - high - middle
    meta = jnp.concatenate([expert_ids[0].T.astype(f32), high, middle, low])
    meta = meta.astype(jnp.bfloat16)
    meta = jnp.concatenate([meta[:16], meta[16:]], axis=1)

    def kv_of(head):
        pair = jnp.concatenate(
            [
                lax.dynamic_slice_in_dim(keys, head * HDIM, HDIM, 1),
                lax.dynamic_slice_in_dim(values, head * HDIM, HDIM, 1),
            ],
            axis=1,
        )
        return jnp.concatenate([pair, meta])

    kv_to = [kv_of((y - o + 4) % 4) for o in OFFSETS]
    kv_y = kv_to[:1] + [shift(kv_to[k], yy, -OFFSETS[k]) for k in (1, 2, 3)]
    column = jnp.stack(kv_y)
    kv_z = [column] + [shift(column, zz, -o) for o in OFFSETS[1:]]
    kv = jnp.concatenate(kv_z)

    part = lax.dynamic_slice_in_dim(out_weight, core * 256, 256, 0)
    part = after(part, *kv_to)
    inner = jnp.stack([part] + [shift(part, ("x", "z"), -o) for o in OFFSETS[1:]])
    own = [inner] + [shift(inner, ("z", "x"), -o) for o in OFFSETS[1:3]]
    own.append(shift(after(inner, kv_z[1], kv_z[2]), ("z", "x"), -OFFSETS[3]))

    def queries_of(group):
        return lax.dynamic_slice_in_dim(queries, group * WIDTH, WIDTH, 1)

    blocks = [queries_of(y), None, None, shift(queries_of((y + 2) % 4), yy, -2)]
    for k in (1, 2):
        o = OFFSETS[k]
        near = after(queries_of((y - o + 4) % 4), blocks[3], kv)
        blocks[k] = shift(near, yy, -o)

    def attended(k):
        return attend(OFFSETS[k], doc_lengths, blocks[k], kv)

    last = blocks[2]
    blocks[2] = after(last, own[1], own[2])
    mixed = [attended(k) for k in range(4)]
    other = [swap(after(w, mixed[0], mixed[3], mixed[1], last)) for w in own]

    far, below, above, here = project([mixed[3], mixed[1], mixed[2], mixed[0]], own, other)

    weights = [expert_gate, expert_up, expert_down]
    swapped = [swap(after(expert_gate, far)), swap(after(expert_up, far))]

    terms = [here, shift(below, yy, -1), shift(above, yy, 1), shift(far, yy, 2)]
    meta = after(kv[:, TOKENS:], terms[3])
    meta = jnp.concatenate([meta[:, :, :TOKENS], meta[:, :, TOKENS:]], axis=1)
    pick, put = routing(meta.reshape(4, 4, 32, TOKENS), y, z, core)

    terms[1] = after(terms[1], pick, put)
    hidden = residual[0].astype(f32) + sum(t.astype(f32) for t in terms)
    mean_square = jnp.mean(hidden * hidden, axis=-1, keepdims=True)
    normed = (hidden * lax.rsqrt(mean_square + EPSILON) * norm_gain).astype(jnp.bfloat16)
    normed = after(normed, *swapped)
    swapped.append(swap(after(expert_down, normed)))

    prim, sec = ("y", "z"), ("z", "y")
    line = [normed] + [shift(normed, prim, -o) for o in OFFSETS[1:]]
    below, above = dispatch(line, pick[1:3])
    here, far = dispatch(line, jnp.stack([pick[0], pick[3]]))
    below, above = shift(below, sec, -1), shift(above, sec, 1)
    rest = (weights, swapped)
    (here,) = experts([here], *rest)
    far = shift(after(far, here, below, above), sec, 2)
    below, above = experts([below, above], *rest)
    (far,) = experts([after(far, below)], *rest)

    below, above = shift(below, sec, 1), shift(above, sec, -1)
    (near,) = combine([here, below, above], put[:, :, : 12 * SLOTS])
    parts = combine([shift(far, sec, 2)], put[:, :, 12 * SLOTS :], near)
    total = hidden + parts[0]
    for k in range(1, 4):
        total = total + shift(parts[k], prim, OFFSETS[k]).astype(f32)
    return total.astype(jnp.bfloat16)[None]


def solution(mesh):
    return jax.shard_map(
        body,
        mesh=mesh,
        in_specs=(
            P(("dp", "pair"), "ctx", None),
            P(("dp", "pair"), "ctx", None),
            P(("dp", "pair"), "ctx", None),
            P(("dp", "pair"), "ctx", None),
            P(("dp", "pair"), None),
            P(("dp", "pair"), "ctx", None),
            P(("dp", "pair"), "ctx", None),
            P("ctx", "dp"),
            P(),
            P(("ctx", "pair"), None, None),
            P(("ctx", "pair"), None, None),
            P(("ctx", "pair"), None, None),
        ),
        out_specs=P(("dp", "pair"), "ctx", None),
        check_vma=False,
    )
```

```python
import functools
import math

import jax
import jax.numpy as jnp
from jax import lax
from jax.experimental import pallas as pl
from jax.experimental.pallas import tpu as pltpu
from jax.sharding import PartitionSpec as P

RING = 4
TOKENS = 128
WIDTH = 2048
HDIM = 128
HEADS_HERE = 16
FFE = 768
SLOTS = 48
EPSILON = 1e-06
NEGATIVE = -1e30
OFFSETS = (0, -1, 1, 2)
AXES = ("dp", "ctx", "pair")


def shift(value, axes, distance):
    pairs = []
    for x in range(RING):
        for y in range(RING):
            for z in range(RING):
                for core in range(2):
                    to = {"x": x, "y": y, "z": z}
                    to[axes[core]] = (to[axes[core]] + distance) % RING
                    pairs.append(
                        (
                            (x * 16 + y * 4 + z) * 2 + core,
                            (to["x"] * 16 + to["y"] * 4 + to["z"]) * 2 + core,
                        )
                    )
    return lax.ppermute(value, AXES, pairs)


def swap(value):
    return lax.ppermute(value, "pair", [(0, 1), (1, 0)])


def ring_slot(distance):
    distance = lax.rem(distance + 4, 4)
    return jnp.where(distance == 3, 1, jnp.where(distance == 0, 0, distance + 1))


def attend_kernel(offset, lengths, q_ref, kv_ref, out_ref, turned_ref, top_ref, sum_ref, acc_ref):
    place = lax.axis_index("ctx")
    y, z = place // 4, lax.rem(place, 4)
    block = lax.rem(y + offset + 4, 4) * 4 + z
    scale = math.log2(math.e) / math.sqrt(HDIM)
    places = block * TOKENS + lax.broadcasted_iota(jnp.int32, (1, TOKENS), 1)
    starts = jnp.zeros((1, TOKENS), jnp.int32)
    first = jnp.int32(0)
    end = jnp.int32(0)
    for d in range(8):
        end = end + lengths[0, d]
        starts = jnp.maximum(starts, jnp.where(places >= end, end, 0))
        first = jnp.maximum(first, jnp.where(block * TOKENS >= end, end, 0))
    top_ref[...] = jnp.full_like(top_ref, NEGATIVE)
    sum_ref[...] = jnp.zeros_like(sum_ref)
    acc_ref[...] = jnp.zeros_like(acc_ref)
    rows = lax.broadcasted_iota(jnp.int32, (TOKENS, TOKENS), 0)
    for head in range(HEADS_HERE):
        h = head * HDIM
        turned_ref[:, h : h + HDIM] = q_ref[:, h : h + HDIM].T

    def step(chunk, carry):
        slot = ring_slot(lax.rem(chunk, 4) - z) * 4 + ring_slot(chunk // 4 - y)
        keys = kv_ref[slot, :TOKENS, :HDIM]
        values = kv_ref[slot, :TOKENS, HDIM:].T
        key_places = chunk * TOKENS + rows
        allowed = (key_places <= places) & (key_places >= starts)
        bias = jnp.where(allowed, 0.0, NEGATIVE).astype(jnp.float32)
        bias = jnp.concatenate([bias, bias], axis=1)
        for pair in range(HEADS_HERE // 2):
            h = 2 * pair * HDIM
            q = turned_ref[:, h : h + 2 * HDIM]
            s = jnp.dot(keys, q, preferred_element_type=jnp.float32)
            s = s * scale + bias
            old = top_ref[pair]
            top = jnp.maximum(old, jnp.max(s, axis=0, keepdims=True))
            weights = jnp.exp2(s - top)
            fade = jnp.exp2(old - top)
            top_ref[pair] = top
            sum_ref[pair] = sum_ref[pair] * fade + jnp.sum(weights, axis=0, keepdims=True)
            acc_ref[pair] = acc_ref[pair] * fade + jnp.dot(
                values, weights.astype(jnp.bfloat16), preferred_element_type=jnp.float32
            )
        return carry

    lax.fori_loop(first // TOKENS, block + 1, step, 0)
    for pair in range(HEADS_HERE // 2):
        h = 2 * pair * HDIM
        mixed = (acc_ref[pair] / sum_ref[pair]).T.astype(jnp.bfloat16)
        out_ref[:, h : h + HDIM] = mixed[:TOKENS]
        out_ref[:, h + HDIM : h + 2 * HDIM] = mixed[TOKENS:]


def attend(offset, lengths, queries, kv):
    vmem = pl.BlockSpec(memory_space=pltpu.VMEM)
    return pl.pallas_call(
        functools.partial(attend_kernel, offset),
        out_shape=jax.ShapeDtypeStruct((TOKENS, WIDTH), jnp.bfloat16),
        in_specs=[pl.BlockSpec(memory_space=pltpu.SMEM), vmem, vmem],
        out_specs=vmem,
        scratch_shapes=[
            pltpu.VMEM((HDIM, WIDTH), jnp.bfloat16),
            pltpu.VMEM((8, 1, 256), jnp.float32),
            pltpu.VMEM((8, 1, 256), jnp.float32),
            pltpu.VMEM((8, HDIM, 256), jnp.float32),
        ],
        compiler_params=pltpu.CompilerParams(vmem_limit_bytes=8 * 2**20),
        cost_estimate=pl.CostEstimate(
            flops=4 * 2**30, bytes_accessed=3 * 2**20, transcendentals=2048 * 640
        ),
        name="attend",
    )(lengths, queries, kv)


def project_kernel(count, *refs):
    att, own, other = refs[0:count], refs[count : count + 4], refs[count + 4 : count + 8]
    outs = refs[count + 8 :]
    x, core = lax.axis_index("dp"), lax.axis_index("pair")
    z = lax.rem(lax.axis_index("ctx"), 4)

    def run(stacks):
        for i in range(4):
            column = lax.rem(x + OFFSETS[i] + 4, 4) * 512
            total = None
            for half in range(2):
                for j in range(4):
                    place = lax.rem(z + OFFSETS[j] + 4, 4) * 512 + half * 256
                    place = pl.ds(pl.multiple_of(place, 256), 256)
                    left = jnp.concatenate([a[:, place] for a in att], axis=0)
                    right = stacks[0][j][i] if half == 0 else stacks[1][i][j]
                    term = jnp.dot(left, right, preferred_element_type=jnp.float32)
                    total = term if total is None else total + term
            total = total.astype(jnp.bfloat16)
            for n in range(count):
                part = total[n * TOKENS : (n + 1) * TOKENS]
                outs[n][:, pl.ds(pl.multiple_of(column, 512), 512)] = part

    @pl.when(core == 0)
    def _():
        run((own, other))

    @pl.when(core == 1)
    def _():
        run((other, own))


def project(attended, own, other):
    vmem = pl.BlockSpec(memory_space=pltpu.VMEM)
    count = len(attended)
    return pl.pallas_call(
        functools.partial(project_kernel, count),
        out_shape=[jax.ShapeDtypeStruct((TOKENS, WIDTH), jnp.bfloat16)] * count,
        in_specs=[vmem] * (count + 8),
        out_specs=[vmem] * count,
        compiler_params=pltpu.CompilerParams(vmem_limit_bytes=14 * 2**20),
        cost_estimate=pl.CostEstimate(
            flops=2 * count * TOKENS * 2048 * 2048,
            bytes_accessed=(8 + count) * 2**20,
            transcendentals=0,
        ),
        name="project",
    )(*attended, *own, *other)


def pieces_of(blocks, cols):
    return [
        jnp.concatenate([blocks[2 * p][:, cols], blocks[2 * p + 1][:, cols]], axis=0)
        for p in range(2)
    ]


def dispatch_kernel(*refs):
    blocks, pick_ref, outs = refs[:4], refs[4], refs[5:]
    for n in range(4):
        cols = pl.ds(n * 512, 512)
        pieces = pieces_of(blocks, cols)
        for chip, out in enumerate(outs):
            for p in range(2):
                rows = jnp.dot(pick_ref[chip, p], pieces[p], preferred_element_type=jnp.float32)
                rows = rows.astype(jnp.bfloat16).reshape(4, SLOTS, 512)
                out[:, p * SLOTS : (p + 1) * SLOTS, cols] = rows


def dispatch(blocks, pick):
    vmem = pl.BlockSpec(memory_space=pltpu.VMEM)
    chips = pick.shape[0]
    return pl.pallas_call(
        dispatch_kernel,
        out_shape=[jax.ShapeDtypeStruct((4, 2 * SLOTS, WIDTH), jnp.bfloat16)] * chips,
        in_specs=[vmem] * 5,
        out_specs=[vmem] * chips,
        compiler_params=pltpu.CompilerParams(vmem_limit_bytes=12 * 2**20),
        cost_estimate=pl.CostEstimate(
            flops=2 * chips * 384 * 256 * 2048, bytes_accessed=6 * 2**20, transcendentals=0
        ),
        name="dispatch",
    )(*blocks, pick)


def combine_kernel(chips, last, *refs):
    sources, put_ref, refs = refs[:chips], refs[chips], refs[chips + 1 :]
    for n in range(4):
        cols = pl.ds(n * 512, 512)
        for p in range(2):
            rows = [
                source[e, p * SLOTS : (p + 1) * SLOTS, cols] for source in sources for e in range(4)
            ]
            mixed = jnp.dot(
                put_ref[p], jnp.concatenate(rows, axis=0), preferred_element_type=jnp.float32
            )
            for half in range(2):
                part = mixed[half * TOKENS : (half + 1) * TOKENS]
                if not last:
                    refs[0][2 * p + half, :, cols] = part
                    continue
                part = part + refs[0][2 * p + half, :, cols]
                out = refs[1 + 2 * p + half]
                out[:, cols] = part.astype(out.dtype)


def combine(sources, put, earlier=None):
    vmem = pl.BlockSpec(memory_space=pltpu.VMEM)
    last = earlier is not None
    if last:
        shapes = [jax.ShapeDtypeStruct((TOKENS, WIDTH), jnp.float32)]
        shapes += [jax.ShapeDtypeStruct((TOKENS, WIDTH), jnp.bfloat16)] * 3
    else:
        shapes = [jax.ShapeDtypeStruct((4, TOKENS, WIDTH), jnp.float32)]
    operands = [*sources, put] + ([earlier] if last else [])
    return pl.pallas_call(
        functools.partial(combine_kernel, len(sources), last),
        out_shape=shapes,
        in_specs=[vmem] * len(operands),
        out_specs=[vmem] * len(shapes),
        compiler_params=pltpu.CompilerParams(vmem_limit_bytes=16 * 2**20),
        cost_estimate=pl.CostEstimate(
            flops=2 * len(sources) * 384 * 256 * 2048, bytes_accessed=8 * 2**20, transcendentals=0
        ),
        name="combine",
    )(*operands)


def experts_kernel(count, *refs):
    sources, refs = refs[:count], refs[count:]
    hbm, refs = refs[:6], refs[6:]
    outs, refs = refs[:count], refs[count:]
    act_ref, gate_buf, up_buf, down_buf, sems = refs
    buffers = (gate_buf, up_buf, down_buf)

    def copies(e):
        side, index, slot = e // 2, e % 2, e % 2
        return [
            pltpu.make_async_copy(
                hbm[3 * side + w].at[index], buffers[w].at[slot], sems.at[w, slot]
            )
            for w in range(3)
        ]

    for e in range(2):
        for c in copies(e):
            c.start()
    for e in range(4):
        slot = e % 2
        waits = copies(e)
        waits[0].wait()
        waits[1].wait()
        rows = jnp.concatenate([source[e] for source in sources], axis=0)
        for n in range(3):
            cols = pl.ds(n * 256, 256)
            gate = jnp.dot(rows, gate_buf[slot, :, cols], preferred_element_type=jnp.float32)
            upward = jnp.dot(rows, up_buf[slot, :, cols], preferred_element_type=jnp.float32)
            act_ref[:, cols] = (gate / (1.0 + jnp.exp(-gate)) * upward).astype(jnp.bfloat16)
        waits[2].wait()
        active = act_ref[...]
        for n in range(4):
            cols = pl.ds(n * 512, 512)
            result = jnp.dot(active, down_buf[slot, :, cols], preferred_element_type=jnp.float32)
            result = result.astype(jnp.bfloat16)
            for i, out in enumerate(outs):
                out[e, :, cols] = result[i * 2 * SLOTS : (i + 1) * 2 * SLOTS]
        if e + 2 < 4:
            for c in copies(e + 2):
                c.start()


def experts(sources, mine, others):
    count = len(sources)
    vmem = pl.BlockSpec(memory_space=pltpu.VMEM)
    hbm = pl.BlockSpec(memory_space=pltpu.HBM)
    rows = count * 4 * 2 * SLOTS
    return pl.pallas_call(
        functools.partial(experts_kernel, count),
        out_shape=[jax.ShapeDtypeStruct((4, 2 * SLOTS, WIDTH), jnp.bfloat16)] * count,
        in_specs=[vmem] * count + [hbm] * 6,
        out_specs=[vmem] * count,
        scratch_shapes=[
            pltpu.VMEM((count * 2 * SLOTS, FFE), jnp.bfloat16),
            pltpu.VMEM((2, WIDTH, FFE), jnp.bfloat16),
            pltpu.VMEM((2, WIDTH, FFE), jnp.bfloat16),
            pltpu.VMEM((2, FFE, WIDTH), jnp.bfloat16),
            pltpu.SemaphoreType.DMA((3, 2)),
        ],
        compiler_params=pltpu.CompilerParams(vmem_limit_bytes=40 * 2**20),
        cost_estimate=pl.CostEstimate(
            flops=6 * rows * 2048 * 768,
            bytes_accessed=(36 + 3 * count) * 2**20,
            transcendentals=rows * 768,
        ),
        name="experts",
    )(*sources, *mine, *others)


def routing(meta, y, z, core):
    meta = jnp.where(core == 0, meta[0], meta[:, 0]).astype(jnp.float32)
    meta = meta.reshape(2, 2, 32, TOKENS).transpose(0, 2, 1, 3).reshape(2, 32, 2 * TOKENS)
    ids = meta[:, :8]
    route = meta[:, 8:16] + meta[:, 16:24] + meta[:, 24:32]
    index = jnp.arange(16, dtype=jnp.int32)
    chip, expert = index // 4, index % 4
    across = jnp.where(chip == 3, 2, jnp.where(chip == 2, 1, -chip))
    on_y, on_z = jnp.where(core == 0, 0, across), jnp.where(core == 0, across, 0)
    chip = (y + on_y + 4) % 4 * 4 + (z + on_z + 4) % 4
    wanted = chip * 4 + (expert + 2 * core) % 4
    same = ids[:, None] == wanted.astype(jnp.float32)[None, :, None, None]
    chosen = jnp.any(same, axis=2)
    share = jnp.sum(jnp.where(same, route[:, None], 0.0), axis=2)
    places = jnp.arange(2 * TOKENS, dtype=jnp.int32)
    before = (places[:, None] < places[None, :]).astype(jnp.bfloat16)
    rank = jnp.einsum(
        "pet,tu->peu", chosen.astype(jnp.bfloat16), before, preferred_element_type=jnp.float32
    )
    rank = jnp.where(chosen, rank, -1.0).astype(jnp.bfloat16)
    share = share.astype(jnp.bfloat16)
    slots = jnp.arange(SLOTS, dtype=jnp.bfloat16)
    pick = (rank[:, :, None] == slots[None, None, :, None]).astype(jnp.bfloat16)
    pick = pick.reshape(2, 4, 4 * SLOTS, 2 * TOKENS).transpose(1, 0, 2, 3)
    by_slot = lambda v: jnp.repeat(v.transpose(0, 2, 1), SLOTS, axis=2)
    slots = jnp.tile(slots, 16)
    put = jnp.where(by_slot(rank) == slots, by_slot(share), jnp.bfloat16(0))
    return pick, put


def after(value, *others):
    return lax.optimization_barrier((value, *others))[0]


def body(
    queries,
    keys,
    values,
    residual,
    doc_lengths,
    expert_ids,
    route_weights,
    out_weight,
    norm_gain,
    expert_gate,
    expert_up,
    expert_down,
):
    f32 = jnp.float32
    x, core = lax.axis_index("dp"), lax.axis_index("pair")
    y, z = lax.axis_index("ctx") // 4, lax.axis_index("ctx") % 4
    yy, zz = ("y", "y"), ("z", "z")
    queries, keys, values = queries[0], keys[0], values[0]

    route = route_weights[0].T
    high = lax.reduce_precision(route, 8, 7)
    middle = lax.reduce_precision(route - high, 8, 7)
    low = route - high - middle
    meta = jnp.concatenate([expert_ids[0].T.astype(f32), high, middle, low])
    meta = meta.astype(jnp.bfloat16)
    meta = jnp.concatenate([meta[:16], meta[16:]], axis=1)

    def kv_of(head):
        pair = jnp.concatenate(
            [
                lax.dynamic_slice_in_dim(keys, head * HDIM, HDIM, 1),
                lax.dynamic_slice_in_dim(values, head * HDIM, HDIM, 1),
            ],
            axis=1,
        )
        return jnp.concatenate([pair, meta])

    kv_y = [kv_of(y)] + [shift(kv_of((y - o + 4) % 4), yy, -o) for o in OFFSETS[1:]]
    column = jnp.stack(kv_y)
    kv_z = [column] + [shift(column, zz, -o) for o in OFFSETS[1:]]
    kv = jnp.concatenate(kv_z)

    part = lax.dynamic_slice_in_dim(out_weight, core * 256, 256, 0)
    inner = jnp.stack([part] + [shift(part, ("x", "z"), -o) for o in OFFSETS[1:]])
    own = [inner] + [shift(inner, ("z", "x"), -o) for o in OFFSETS[1:3]]
    own.append(shift(after(inner, kv_z[1], kv_z[2]), ("z", "x"), -OFFSETS[3]))

    def queries_of(group):
        return lax.dynamic_slice_in_dim(queries, group * WIDTH, WIDTH, 1)

    blocks = [queries_of(y), None, None, shift(queries_of((y + 2) % 4), yy, -2)]
    for k in (1, 2):
        o = OFFSETS[k]
        near = after(queries_of((y - o + 4) % 4), blocks[3], kv)
        blocks[k] = shift(near, yy, -o)

    meta = kv[:, TOKENS:]
    meta = jnp.concatenate([meta[:, :, :TOKENS], meta[:, :, TOKENS:]], axis=1)
    pick, put = routing(meta.reshape(4, 4, 32, TOKENS), y, z, core)

    def attended(k):
        return attend(OFFSETS[k], doc_lengths, blocks[k], kv)

    last = blocks[2]
    blocks[2] = after(last, *own)
    mixed = [attended(k) for k in range(4)]
    other = [swap(after(w, mixed[0], mixed[3], mixed[1], last)) for w in own]

    far, below, above, here = project([mixed[3], mixed[1], mixed[2], mixed[0]], own, other)

    weights = [expert_gate, expert_up, expert_down]
    swapped = [swap(after(expert_gate, far)), swap(after(expert_up, far))]

    terms = [here, shift(below, yy, -1), shift(above, yy, 1), shift(far, yy, 2)]
    hidden = residual[0].astype(f32) + sum(t.astype(f32) for t in terms)
    mean_square = jnp.mean(hidden * hidden, axis=-1, keepdims=True)
    normed = (hidden * lax.rsqrt(mean_square + EPSILON) * norm_gain).astype(jnp.bfloat16)
    normed = after(normed, pick, put, *swapped)
    swapped.append(swap(after(expert_down, normed)))

    prim, sec = ("y", "z"), ("z", "y")
    line = [normed] + [shift(normed, prim, -o) for o in OFFSETS[1:]]
    below, above = dispatch(line, pick[1:3])
    here, far = dispatch(line, jnp.stack([pick[0], pick[3]]))
    below, above = shift(below, sec, -1), shift(above, sec, 1)
    rest = (weights, swapped)
    (here,) = experts([here], *rest)
    far = shift(after(far, here), sec, 2)
    below, above = experts([below, above], *rest)
    (far,) = experts([after(far, below)], *rest)

    below, above = shift(below, sec, 1), shift(above, sec, -1)
    (near,) = combine([here, below, above], put[:, :, : 12 * SLOTS])
    parts = combine([shift(far, sec, 2)], put[:, :, 12 * SLOTS :], near)
    total = hidden + parts[0]
    for k in range(1, 4):
        total = total + shift(parts[k], prim, OFFSETS[k]).astype(f32)
    return total.astype(jnp.bfloat16)[None]


def solution(mesh):
    return jax.shard_map(
        body,
        mesh=mesh,
        in_specs=(
            P(("dp", "pair"), "ctx", None),
            P(("dp", "pair"), "ctx", None),
            P(("dp", "pair"), "ctx", None),
            P(("dp", "pair"), "ctx", None),
            P(("dp", "pair"), None),
            P(("dp", "pair"), "ctx", None),
            P(("dp", "pair"), "ctx", None),
            P("ctx", "dp"),
            P(),
            P(("ctx", "pair"), None, None),
            P(("ctx", "pair"), None, None),
            P(("ctx", "pair"), None, None),
        ),
        out_specs=P(("dp", "pair"), "ctx", None),
        check_vma=False,
    )
```
